32 devices in a mesh: win: 8 (over y, x, core), head: 4 (over z).
Axes of the slice: x: 2, y: 2, z: 4, core: 2. Of those that a mesh axis runs over, the one named last changes fastest.
Arguments:
- tokens: bfloat16 [65536, 384], P(('win', 'head')), may hold values from -6 to 6
- out_grad: bfloat16 [65536, 384], P(('win', 'head')), may hold values from -6 to 6
- clip_frames: int32 [256], P('win'), may hold values from 4 to 16, as said below
- qkv_weight: float32 [384, 3, 384], P(None, None, 'head'), may hold values from -0.3125 to 0.3125
- qv_bias: float32 [2, 384], P(None, 'head'), may hold values from -3 to 3
- rel_table: float32 [225, 16], P(None, 'head'), may hold values from -6 to 6
- proj_weight: float32 [384, 384], P('head'), may hold values from -1.25 to 1.25
- fc1_weight: float32 [384, 1536], P(None, 'head'), may hold values from -0.3125 to 0.3125
- fc1_bias: float32 [1536], P('head'), may hold values from -1.75 to 1.75
- fc2_weight: float32 [1536, 384], P('head'), may hold values from -0.15625 to 0.15625
- row_params: float32 [6, 384], replicated, as said below
- qkv_first: float32 [384, 3, 384], P(None, None, 'head'), may hold values from -0.00048828125 to 0.00048828125
- qkv_second: float32 [384, 3, 384], P(None, None, 'head'), may hold values from 5.6253097e-10 to 3.3751857e-09
- qvb_first: float32 [2, 384], P(None, 'head'), may hold values from -0.0014648438 to 0.0014648438
- qvb_second: float32 [2, 384], P(None, 'head'), may hold values from 5.0627786e-09 to 3.0376672e-08
- table_first: float32 [225, 16], P(None, 'head'), may hold values from -0.00036621094 to 0.00036621094
- table_second: float32 [225, 16], P(None, 'head'), may hold values from 1.4063274e-10 to 5.6253097e-10
- proj_first: float32 [384, 384], P('head'), may hold values from -0.00048828125 to 0.00048828125
- proj_second: float32 [384, 384], P('head'), may hold values from 5.6253097e-10 to 3.3751857e-09
- fc1_first: float32 [384, 1536], P(None, 'head'), may hold values from -0.00048828125 to 0.00048828125
- fc1_second: float32 [384, 1536], P(None, 'head'), may hold values from 5.6253097e-10 to 3.3751857e-09
- fc1b_first: float32 [1536], P('head'), may hold values from -0.00018310547 to 0.00018310547
- fc1b_second: float32 [1536], P('head'), may hold values from 2.8126546e-11 to 1.12506185e-10
- fc2_first: float32 [1536, 384], P('head'), may hold values from -0.00048828125 to 0.00048828125
- fc2_second: float32 [1536, 384], P('head'), may hold values from 5.6253097e-10 to 3.3751857e-09
- rows_first: float32 [6, 384], replicated, may hold values from -0.0014648438 to 0.0014648438
- rows_second: float32 [6, 384], replicated, may hold values from 5.0627786e-09 to 3.0376672e-08
Outputs:
- output: float32 [65536, 384], P(('win', 'head'))
- input_grad: float32 [65536, 384], P(('win', 'head'))
- grad_norm: float32 [], replicated
- qkv_grad: float32 [384, 3, 384], P(None, None, 'head')
- qkv_moment: float32 [384, 3, 384], P(None, None, 'head')
- qkv_square: float32 [384, 3, 384], P(None, None, 'head')
- qkv_master: float32 [384, 3, 384], P(None, None, 'head')
- qvb_grad: float32 [2, 384], P(None, 'head')
- qvb_moment: float32 [2, 384], P(None, 'head')
- qvb_square: float32 [2, 384], P(None, 'head')
- qvb_master: float32 [2, 384], P(None, 'head')
- table_grad: float32 [225, 16], P(None, 'head')
- table_moment: float32 [225, 16], P(None, 'head')
- table_square: float32 [225, 16], P(None, 'head')
- table_master: float32 [225, 16], P(None, 'head')
- proj_grad: float32 [384, 384], P('head')
- proj_moment: float32 [384, 384], P('head')
- proj_square: float32 [384, 384], P('head')
- proj_master: float32 [384, 384], P('head')
- fc1_grad: float32 [384, 1536], P(None, 'head')
- fc1_moment: float32 [384, 1536], P(None, 'head')
- fc1_square: float32 [384, 1536], P(None, 'head')
- fc1_master: float32 [384, 1536], P(None, 'head')
- fc1b_grad: float32 [1536], P('head')
- fc1b_moment: float32 [1536], P('head')
- fc1b_square: float32 [1536], P('head')
- fc1b_master: float32 [1536], P('head')
- fc2_grad: float32 [1536, 384], P('head')
- fc2_moment: float32 [1536, 384], P('head')
- fc2_square: float32 [1536, 384], P('head')
- fc2_master: float32 [1536, 384], P('head')
- rows_grad: float32 [6, 384], replicated
- rows_moment: float32 [6, 384], replicated
- rows_square: float32 [6, 384], replicated
- rows_master: float32 [6, 384], replicated
The draws below stay inside these ranges and needn't reach their ends.
Inputs may be any that keep to these rules, and one draw needn't show every extreme that they name: Patches of a clip are valid in its first clip_frames time rows; some clip of every draw has all 16. `row_params`: rows in order: first norm's gain, its shift, second norm's gain, its shift, attention output bias, feed-forward output bias.
All inputs are finite; a program needn't handle non-finite values.
Results may differ from the reference program's by a relative error of at most 0.015.
Values may be sent and summed in bfloat16 or wider, within the bound.
A program may use at most 256 MiB of HBM per device.

```python
import math
import jax
import jax.numpy as jnp
from jax import lax

D = 384
HEADS = 16
HDIM = 24
FF = 1536
GRID = 16
WIN = 8
SHIFT = 4
STEP = 10
CLIPS = 256
TOKENS = 65536
TABLE = 225
PARAMS = 1777680


def draw_clip_frames(key, part):
    key = jax.random.fold_in(key, 11)
    key_frames, key_chosen = jax.random.split(key)
    frames = jax.random.randint(key_frames, (CLIPS,), 4, GRID + 1, dtype=jnp.int32)
    chosen = jax.random.randint(key_chosen, (), 0, CLIPS, dtype=jnp.int32)
    return jnp.where(jnp.arange(CLIPS, dtype=jnp.int32) == chosen, GRID, frames).astype(jnp.int32)


def draw_row_params(key, part):
    key = jax.random.fold_in(key, 23)
    key_gain, key_shift = jax.random.split(key)
    ramp = 0.6 + 1.2 * jnp.arange(D, dtype=jnp.float32) / D
    gains = ramp[None, :] * jax.random.uniform(key_gain, (2, D), jnp.float32, 0.8, 1.25)
    shifts = 0.3 * jax.random.normal(key_shift, (4, D), jnp.float32)
    return jnp.stack([gains[0], shifts[0], gains[1], shifts[1], shifts[2], shifts[3]]).astype(jnp.float32)


def shard_levels(own_key, extent, cuts, least, top_value):
    def one(position, blocks):
        steps = jax.random.uniform(jax.random.fold_in(jax.random.fold_in(own_key, 6), position), (blocks,), jnp.float32, least / len(cuts), top_value / len(cuts))
        return jnp.repeat(jnp.exp(steps), extent[position] // blocks).reshape((-1,) + (1,) * (len(extent) - position - 1))

    level = one(*cuts[0])
    for cut in cuts[1:]:
        level = level * one(*cut)
    return level


def centred(stream_key, extent, width, bound, cuts=(), kind=jnp.bfloat16):
    entries = width * jax.random.normal(stream_key, extent, jnp.float32)
    if cuts:
        entries = entries * shard_levels(stream_key, extent, cuts, -0.22, 0.18)
    return jnp.clip(entries, -bound, bound).astype(kind)


def setup_inputs(seed: int = 0) -> dict:
    streams_of = jax.random.split(jax.random.key(seed), 28)
    return {
        "tokens": centred(streams_of[0], (TOKENS, D), 1.0, 6.0, ((0, 32),)),
        "out_grad": centred(streams_of[1], (TOKENS, D), 1.0, 6.0, ((0, 32),)),
        "clip_frames": draw_clip_frames(jax.random.fold_in(streams_of[27], 71), 0),
        "qkv_weight": centred(streams_of[3], (D, 3, D), D ** -0.5, 0.3125, ((2, 4),), jnp.float32),
        "qv_bias": centred(streams_of[4], (2, D), 0.5, 3.0, ((1, 4),), jnp.float32),
        "rel_table": centred(streams_of[5], (TABLE, HEADS), 1.0, 6.0, ((1, 4),), jnp.float32),
        "proj_weight": centred(streams_of[6], (D, D), (D // 16) ** -0.5, 1.25, ((0, 4),), jnp.float32),
        "fc1_weight": centred(streams_of[7], (D, FF), D ** -0.5, 0.3125, ((1, 4),), jnp.float32),
        "fc1_bias": centred(streams_of[8], (FF,), 0.3, 1.75, ((0, 4),), jnp.float32),
        "fc2_weight": centred(streams_of[9], (FF, D), FF ** -0.5, 0.15625, ((0, 4),), jnp.float32),
        "row_params": draw_row_params(jax.random.fold_in(streams_of[27], 71), 0),
        "qkv_first": centred(streams_of[11], (D, 3, D), (0.111 * PARAMS ** -0.5), 0.00048828125, ((2, 4),), jnp.float32),
        "qkv_second": jnp.clip(jnp.exp(math.log(3.3751856864938645e-09) - 1.79175944 * jax.random.uniform(streams_of[12], (D, 3, D), jnp.float32) ** shard_levels(streams_of[12], (D, 3, D), ((2, 4),), -0.2, 0.2)), 5.625309662526945e-10, 3.3751856864938645e-09),
        "qvb_first": centred(streams_of[13], (2, D), (0.333 * PARAMS ** -0.5), 0.0014648438, ((1, 4),), jnp.float32),
        "qvb_second": jnp.clip(jnp.exp(math.log(3.0376671844578595e-08) - 1.7917595 * jax.random.uniform(streams_of[14], (2, D), jnp.float32) ** shard_levels(streams_of[14], (2, D), ((1, 4),), -0.2, 0.2)), 5.062778640763099e-09, 3.0376671844578595e-08),
        "table_first": centred(streams_of[15], (TABLE, HEADS), (0.08 * PARAMS ** -0.5), 0.00036621094, ((1, 4),), jnp.float32),
        "table_second": jnp.clip(jnp.exp(math.log(5.625309662526945e-10) - 1.3862944 * jax.random.uniform(streams_of[16], (TABLE, HEADS), jnp.float32) ** shard_levels(streams_of[16], (TABLE, HEADS), ((1, 4),), -0.2, 0.2)), 1.4063274156317362e-10, 5.625309662526945e-10),
        "proj_first": centred(streams_of[17], (D, D), (0.111 * PARAMS ** -0.5), 0.00048828125, ((0, 4),), jnp.float32),
        "proj_second": jnp.clip(jnp.exp(math.log(3.3751856864938645e-09) - 1.79175944 * jax.random.uniform(streams_of[18], (D, D), jnp.float32) ** shard_levels(streams_of[18], (D, D), ((0, 4),), -0.2, 0.2)), 5.625309662526945e-10, 3.3751856864938645e-09),
        "fc1_first": centred(streams_of[19], (D, FF), (0.111 * PARAMS ** -0.5), 0.00048828125, ((1, 4),), jnp.float32),
        "fc1_second": jnp.clip(jnp.exp(math.log(3.3751856864938645e-09) - 1.79175944 * jax.random.uniform(streams_of[20], (D, FF), jnp.float32) ** shard_levels(streams_of[20], (D, FF), ((1, 4),), -0.2, 0.2)), 5.625309662526945e-10, 3.3751856864938645e-09),
        "fc1b_first": centred(streams_of[21], (FF,), (0.04 * PARAMS ** -0.5), 0.00018310547, ((0, 4),), jnp.float32),
        "fc1b_second": jnp.clip(jnp.exp(math.log(1.1250618492386621e-10) - 1.3862944 * jax.random.uniform(streams_of[22], (FF,), jnp.float32) ** shard_levels(streams_of[22], (FF,), ((0, 4),), -0.2, 0.2)), 2.8126546230966554e-11, 1.1250618492386621e-10),
        "fc2_first": centred(streams_of[23], (FF, D), (0.111 * PARAMS ** -0.5), 0.00048828125, ((0, 4),), jnp.float32),
        "fc2_second": jnp.clip(jnp.exp(math.log(3.3751856864938645e-09) - 1.79175944 * jax.random.uniform(streams_of[24], (FF, D), jnp.float32) ** shard_levels(streams_of[24], (FF, D), ((0, 4),), -0.2, 0.2)), 5.625309662526945e-10, 3.3751856864938645e-09),
        "rows_first": centred(streams_of[25], (6, D), (0.333 * PARAMS ** -0.5), 0.0014648438, (), jnp.float32),
        "rows_second": jnp.clip(jnp.exp(jax.random.uniform(streams_of[26], (6, D), jnp.float32, math.log(5.062778640763099e-09), math.log(3.0376671844578595e-08))), 5.062778640763099e-09, 3.0376671844578595e-08),
    }


NORM_EPS = 1e-05
MASKED = -1000000000.0
CLIP_LIMIT = 1.0
LEARN_RATE = 0.1
ROW_RATE = 0.5
BETA_ONE = 0.9
BETA_TWO = 0.999
ADAM_EPS = 1e-08
WEIGHT_DECAY = 0.01
HIGHEST_MODE = lax.Precision.HIGHEST

@jax.custom_vjp
def low(v):
    return lax.optimization_barrier(v.astype(jnp.bfloat16)).astype(jnp.float32)

@jax.custom_vjp
def low_back(v):
    return v

def low_keep(v):
    return (low(v), None)

def low_pass(kept, grad):
    return (grad,)

def back_keep(v):
    return (v, None)

def back_low(kept, grad):
    return (low(grad),)
low.defvjp(low_keep, low_pass)
low_back.defvjp(back_keep, back_low)

def layer_norm(values, gain, shift):
    center = values - lax.optimization_barrier(jnp.mean(values, axis=-1, keepdims=True))
    spread = lax.optimization_barrier(jnp.mean(center * center, axis=-1, keepdims=True))
    return center * lax.rsqrt(spread + NORM_EPS) * gain + shift

def split_grid(grid_values):
    leading = grid_values.shape[:-2]
    rank_lead = len(leading)
    shaped = grid_values.reshape(leading + (GRID // WIN, WIN, GRID // WIN, WIN))
    axes_order = tuple(range(rank_lead)) + (rank_lead, rank_lead + 2, rank_lead + 1, rank_lead + 3)
    return shaped.transpose(axes_order).reshape(leading + ((GRID // WIN) ** 2, WIN * WIN))

def window_masks(frames):
    places = jnp.arange(GRID, dtype=jnp.int32)
    region = jnp.where(places < GRID - WIN, 0, jnp.where(places < GRID - SHIFT, 1, 2)).astype(jnp.int32)
    region_grid = split_grid(region[:, None] * 3 + region[None, :])
    anchor = (places + SHIFT) % GRID
    valid_rows = anchor[None, :] < frames[:, None]
    valid_grid = split_grid(jnp.broadcast_to(valid_rows[:, :, None], (frames.shape[0], GRID, GRID)))
    same_region = region_grid[:, :, None] == region_grid[:, None, :]
    allowed = same_region[None] & valid_grid[:, :, None, :]
    return allowed.reshape(-1, WIN * WIN, WIN * WIN)

def position_index():
    places = jnp.arange(WIN * WIN, dtype=jnp.int32)
    row_at = places // WIN
    col_at = places % WIN
    return (row_at[:, None] - row_at[None, :] + WIN - 1) * (2 * WIN - 1) + col_at[:, None] - col_at[None, :] + WIN - 1

def to_windows(values):
    columns = values.shape[-1]
    number = values.shape[0] // (GRID * GRID)
    shaped = jnp.roll(values.reshape(number, GRID, GRID, columns), (-SHIFT, -SHIFT), axis=(1, 2))
    shaped = shaped.reshape(number, GRID // WIN, WIN, GRID // WIN, WIN, columns).transpose(0, 1, 3, 2, 4, 5)
    return shaped.reshape(number * GRID * GRID, columns)

def from_windows(values):
    columns = values.shape[-1]
    number = values.shape[0] // (GRID * GRID)
    shaped = values.reshape(number, GRID // WIN, GRID // WIN, WIN, WIN, columns).transpose(0, 1, 3, 2, 4, 5)
    shaped = jnp.roll(shaped.reshape(number, GRID, GRID, columns), (SHIFT, SHIFT), axis=(1, 2))
    return shaped.reshape(number * GRID * GRID, columns)

def block_forward(inputs, frames, params):
    qkv_weight, qv_bias, rel_table, proj_weight, fc1_weight, fc1_bias, fc2_weight, row_params = params
    normed_one = low(layer_norm(inputs, row_params[0], row_params[1]))
    joined_rows = jnp.dot(normed_one, low(qkv_weight.reshape(D, 3 * D)), precision=HIGHEST_MODE)
    query_low = low(low_back(joined_rows[:, :D] + qv_bias[0]))
    keys_low = low(low_back(joined_rows[:, D:2 * D]))
    values_low = low(low_back(joined_rows[:, 2 * D:] + qv_bias[1]))
    shape_four = (-1, WIN * WIN, HEADS, HDIM)
    query_heads = to_windows(query_low).reshape(shape_four)
    keys_heads = to_windows(keys_low).reshape(shape_four)
    values_heads = to_windows(values_low).reshape(shape_four)
    raw_scores = jnp.einsum('wqhd,wkhd->whqk', query_heads, keys_heads, precision=HIGHEST_MODE)
    position_bias = rel_table[position_index()].transpose(2, 0, 1)
    allowed = window_masks(frames)[:, None]
    scores = low_back(jnp.where(allowed, raw_scores * HDIM ** (-0.5) + position_bias, MASKED))
    probs = jax.nn.softmax(scores, axis=-1)
    mixed_heads = jnp.einsum('whqk,wkhd->wqhd', low(probs), values_heads, precision=HIGHEST_MODE)
    attended = low(low_back(from_windows(mixed_heads.reshape(-1, D))))
    branch = low_back(jnp.dot(attended, low(proj_weight), precision=HIGHEST_MODE) + row_params[4])
    middle = inputs + branch
    normed_two = low(layer_norm(middle, row_params[2], row_params[3]))
    upper_rows = low_back(jnp.dot(normed_two, low(fc1_weight), precision=HIGHEST_MODE) + fc1_bias)
    hidden = low(jax.nn.gelu(upper_rows, approximate=False))
    return middle + jnp.dot(hidden, low(fc2_weight), precision=HIGHEST_MODE) + row_params[5]

def adam_step(weight, gradient, moment, second, factor, rate):
    clipped = gradient * factor
    moment_new = BETA_ONE * moment + (1.0 - BETA_ONE) * clipped
    second_new = BETA_TWO * second + (1.0 - BETA_TWO) * clipped * clipped
    moment_hat = moment_new / (1.0 - BETA_ONE ** STEP)
    second_hat = second_new / (1.0 - BETA_TWO ** STEP)
    master = weight - rate * (moment_hat / (jnp.sqrt(second_hat) + ADAM_EPS) + WEIGHT_DECAY * weight)
    return (gradient, moment_new, second_new, master)

def reference(tokens, out_grad, clip_frames, qkv_weight, qv_bias, rel_table, proj_weight, fc1_weight, fc1_bias, fc2_weight, row_params, qkv_first, qkv_second, qvb_first, qvb_second, table_first, table_second, proj_first, proj_second, fc1_first, fc1_second, fc1b_first, fc1b_second, fc2_first, fc2_second, rows_first, rows_second):
    weights = (qkv_weight, qv_bias, rel_table, proj_weight, fc1_weight, fc1_bias, fc2_weight, row_params)
    group_clips = math.gcd(CLIPS, 16)
    group_count = CLIPS // group_clips
    group_rows = group_clips * GRID * GRID
    inputs = tokens.astype(jnp.float32).reshape(group_count, group_rows, D)
    cotangent = out_grad.astype(jnp.float32).reshape(group_count, group_rows, D)
    frames = clip_frames.reshape(group_count, group_clips)

    def one_group(totals, pieces):
        piece_in, piece_cot, piece_frames = pieces

        def forward(values, params):
            return block_forward(values, piece_frames, params)
        result, pullback = jax.vjp(forward, piece_in, weights)
        d_values, d_params = pullback(piece_cot)
        return (jax.tree.map(jnp.add, totals, d_params), (result, d_values))
    starting = jax.tree.map(jnp.zeros_like, weights)
    gradients, (results, d_results) = lax.scan(one_group, starting, (inputs, cotangent, frames))
    squares = jnp.zeros((), jnp.float32)
    for member in gradients:
        squares = squares + jnp.sum(member * member)
    grad_norm = jnp.sqrt(squares)
    factor = jnp.minimum(1.0, CLIP_LIMIT / (grad_norm + 1e-06))
    firsts = (qkv_first, qvb_first, table_first, proj_first, fc1_first, fc1b_first, fc2_first, rows_first)
    seconds = (qkv_second, qvb_second, table_second, proj_second, fc1_second, fc1b_second, fc2_second, rows_second)
    rates = (LEARN_RATE, LEARN_RATE, ROW_RATE, LEARN_RATE, LEARN_RATE, LEARN_RATE, LEARN_RATE, ROW_RATE)
    updated = []
    for weight, gradient, moment, second, rate in zip(weights, gradients, firsts, seconds, rates):
        updated.extend(adam_step(weight, gradient, moment, second, factor, rate))
    return (results.reshape(TOKENS, D), d_results.reshape(TOKENS, D), grad_norm, updated[0], updated[1], updated[2], updated[3], updated[4], updated[5], updated[6], updated[7], updated[8], updated[9], updated[10], updated[11], updated[12], updated[13], updated[14], updated[15], updated[16], updated[17], updated[18], updated[19], updated[20], updated[21], updated[22], updated[23], updated[24], updated[25], updated[26], updated[27], updated[28], updated[29], updated[30], updated[31])
```

```python
from functools import partial

import jax
import jax.numpy as jnp
from jax import lax
from jax.experimental import pallas as pl
from jax.experimental.pallas import tpu as pltpu
from jax.sharding import PartitionSpec as P

D = 384
HDIM = 24
HEADS = 16
GROUPS = 4
PER = 4
LANES = 128
FF = 1536
GRID = 16
WIN = 8
CLIP = GRID * GRID
SPOT = WIN * WIN
SHIFT = 4
STEP = 10
CHUNK = 384

NORM_EPS = 1e-05
MASKED = -1000000000.0
CLIP_LIMIT = 1.0
LEARN_RATE = 0.1
ROW_RATE = 0.5
BETA_ONE = 0.9
BETA_TWO = 0.999
ADAM_EPS = 1e-08
WEIGHT_DECAY = 0.01
SCALE = HDIM ** (-0.5)
F32 = jnp.float32
BF16 = jnp.bfloat16
VMEM_LIMIT = 58 * 1024 * 1024


def nn(a, b):
    return lax.dot_general(a, b, (((1,), (0,)), ((), ())), preferred_element_type=F32)


def nt(a, b):
    return lax.dot_general(a, b, (((1,), (1,)), ((), ())), preferred_element_type=F32)


def tn(a, b):
    return lax.dot_general(a, b, (((0,), (0,)), ((), ())), preferred_element_type=F32)


def iota(shape, axis):
    return lax.broadcasted_iota(jnp.int32, shape, axis)


def fold(x):
    return jnp.sum(x.reshape(x.shape[0] // 8, 8, x.shape[1]), axis=0)


def normalize(x):
    center = x - jnp.mean(x, axis=-1, keepdims=True)
    spread = jnp.mean(center * center, axis=-1, keepdims=True)
    inverse = lax.rsqrt(spread + NORM_EPS)
    return center * inverse, inverse


def norm_back(e, n, inverse, gain):
    q = e * gain
    return inverse * (
        q - jnp.mean(q, axis=-1, keepdims=True) - n * jnp.mean(q * n, axis=-1, keepdims=True)
    )


def to_windows(x):
    low = iota((8, x.shape[1]), 0) < 4
    first, second = [], []
    for t in range(GRID):
        a = x[16 * t : 16 * t + 8]
        b = x[16 * t + 8 : 16 * t + 16]
        first.append(pltpu.roll(jnp.where(low, b, a), 4, axis=0))
        second.append(pltpu.roll(jnp.where(low, a, b), 4, axis=0))
    pieces = []
    for wt in range(2):
        for side in (first, second):
            for a in range(WIN):
                pieces.append(side[(wt * WIN + a + SHIFT) % GRID])
    return jnp.concatenate(pieces, axis=0)


def from_windows(y):
    low = iota((8, y.shape[1]), 0) < 4
    pieces = []
    for t in range(GRID):
        rolled = (t - SHIFT) % GRID
        base = (rolled // WIN) * 128 + (rolled % WIN) * 8
        u = pltpu.roll(y[base : base + 8], 4, axis=0)
        v = pltpu.roll(y[base + 64 : base + 72], 4, axis=0)
        pieces.append(jnp.where(low, v, u))
        pieces.append(jnp.where(low, u, v))
    return jnp.concatenate(pieces, axis=0)


def head_masks(dtype):
    lane = iota((16, LANES), 1) // HDIM
    return [jnp.where(lane == h, 1.0, 0.0).astype(F32).astype(dtype) for h in range(PER)]


def stack_heads(x, masks):
    tiles = x.reshape(SPOT // 16, 16, LANES)
    return jnp.concatenate([(tiles * m[None]).reshape(SPOT, LANES) for m in masks], axis=0)


def pick_heads(r):
    lane = iota((SPOT, LANES), 1)
    out = r[3 * SPOT :]
    for h in (2, 1, 0):
        out = jnp.where(lane < (h + 1) * HDIM, r[h * SPOT : (h + 1) * SPOT], out)
    return out


def key_times(wt, wf):
    j = iota((SPOT, PER * SPOT), 0)
    i = iota((SPOT, PER * SPOT), 1) % SPOT
    time = (wt * WIN + j // WIN + SHIFT) % GRID
    same = j >= 0
    if wt:
        same = same & ((j // WIN < 4) == (i // WIN < 4))
    if wf:
        same = same & ((j % WIN < 4) == (i % WIN < 4))
    return jnp.where(same, time, 99)


def split_three(x):
    one = x.astype(BF16)
    rest = x - one.astype(F32)
    two = rest.astype(BF16)
    three = (rest - two.astype(F32)).astype(BF16)
    return one, two, three


def build_bias(table_ref, bias_ref):
    row = iota((256, 256), 0)
    lane = iota((256, 256), 1)
    spot = lane % SPOT
    base = spot // WIN * (2 * WIN - 1) + spot % WIN
    for g in range(GROUPS):
        total = None
        for h in range(PER):
            head = g * PER + h
            own = jnp.where((row == base) & (lane // SPOT == h), 1.0, 0.0).astype(F32).astype(BF16)
            line = jnp.broadcast_to(table_ref[head : head + 1, :], (8, 256))
            spread = jnp.concatenate(
                [
                    pltpu.roll(line, (15 * a + 144) % 256, axis=1, stride=1, stride_axis=0)
                    for a in range(WIN)
                ],
                axis=0,
            )
            for part in split_three(spread):
                term = nn(part, own)
                total = term if total is None else total + term
        bias_ref[g] = total


def gelu_parts(u):
    mag = jnp.abs(u) * (0.5**0.5)
    t = 1.0 / (1.0 + 0.3275911 * mag)
    bell = jnp.exp(-0.5 * (u * u))
    poly = t * (
        0.127414796
        + t * (-0.142248368 + t * (0.7107068705 + t * (-0.7265760135 + t * 0.5307027145)))
    )
    tail = poly * bell
    return jnp.where(u >= 0.0, 1.0 - tail, tail), bell * 0.3989422804014327


def front_kernel(
    frames_ref,
    tok_ref,
    og_ref,
    wqkv_ref,
    bqv_ref,
    table_ref,
    wproj_ref,
    w1_ref,
    b1_ref,
    w2_ref,
    rowp_ref,
    out_ref,
    qkv_ref,
    probs_ref,
    datt_ref,
    dmid_ref,
    g1_ref,
    g2_ref,
    gp_ref,
    rows_ref,
    gb_ref,
    bias_ref,
    time_ref,
    att_ref,
):
    step = pl.program_id(0)

    @pl.when(step == 0)
    def _():
        build_bias(table_ref, bias_ref)
        for wt in range(2):
            for wf in range(2):
                time_ref[wt * 2 + wf] = key_times(wt, wf)
        for ref in (g1_ref, g2_ref, gp_ref, rows_ref, gb_ref):
            ref[...] = jnp.zeros_like(ref)

    frames = frames_ref[step]
    x = to_windows(tok_ref[...].astype(F32))
    og = to_windows(og_ref[...].astype(F32))
    n1, _ = normalize(x)
    n1 = (n1 * rowp_ref[0:1] + rowp_ref[1:2]).astype(BF16)
    for part in range(3):
        cols = slice(part * 512, part * 512 + 512)
        y = nn(n1, wqkv_ref[:, cols])
        if part == 0:
            y = y + bqv_ref[0:1]
        if part == 2:
            y = y + bqv_ref[1:2]
        qkv_ref[:, cols] = y.astype(BF16)
    masks = head_masks(BF16)
    for w in range(4):
        rows = slice(w * SPOT, w * SPOT + SPOT)
        for g in range(GROUPS):
            q = qkv_ref[rows, g * LANES : g * LANES + LANES]
            k = qkv_ref[rows, 512 + g * LANES : 512 + g * LANES + LANES]
            v = qkv_ref[rows, 1024 + g * LANES : 1024 + g * LANES + LANES]
            s = nt(k, stack_heads(q, masks)) * SCALE + bias_ref[g]
            s = jnp.where(time_ref[w] < frames, s, MASKED)
            e = jnp.exp(s - jnp.max(s, axis=0, keepdims=True))
            p = (e * (1.0 / jnp.sum(e, axis=0, keepdims=True))).astype(BF16)
            probs_ref[0, w, g] = p
            o = pick_heads(tn(p, v))
            att_ref[rows, g * LANES : g * LANES + LANES] = o.astype(BF16)
    att = att_ref[...]
    middle = x + nn(att, wproj_ref[...]) + rowp_ref[4:5]
    nrm, inv = normalize(middle)
    n2f = nrm * rowp_ref[2:3] + rowp_ref[3:4]
    n2 = n2f.astype(BF16)
    n2t = n2.T
    ogb = og.astype(BF16)
    ogt = ogb.T
    ffn = None
    dn2 = None
    for c in range(FF // CHUNK):
        cols = slice(c * CHUNK, c * CHUNK + CHUNK)
        u = nn(n2, w1_ref[:, cols]) + b1_ref[0:1, cols]
        phi, dens = gelu_parts(u)
        hid = (u * phi).astype(BF16)
        du = ((phi + u * dens) * nt(ogb, w2_ref[cols, :])).astype(BF16)
        gb_ref[:, cols] += fold(du.astype(F32))
        g1_ref[:, cols] += nn(n2t, du)
        g2_ref[:, cols] += nn(ogt, hid)
        a = nn(hid, w2_ref[cols, :])
        b = nt(du, w1_ref[:, cols])
        ffn = a if ffn is None else ffn + a
        dn2 = b if dn2 is None else dn2 + b
    out_ref[...] = from_windows(middle + ffn + rowp_ref[5:6])
    dmid = og + norm_back(dn2, nrm, inv, rowp_ref[2:3])
    dmid_ref[...] = dmid
    dbr = dmid.astype(BF16)
    rows_ref[0] += fold(dn2 * nrm)
    rows_ref[1] += fold(dn2)
    rows_ref[2] += fold(dbr.astype(F32))
    rows_ref[3] += fold(og)
    gp_ref[...] += tn(att, dbr)
    datt_ref[...] = nt(dbr, wproj_ref[...]).astype(BF16)


def back_kernel(
    frames_ref,
    tok_ref,
    qkv_ref,
    probs_ref,
    datt_ref,
    dmid_ref,
    wqkv_ref,
    rowp_ref,
    din_ref,
    gq_ref,
    rows_ref,
    gqv_ref,
    gt_ref,
    time_ref,
    tacc_ref,
    dj_ref,
):
    step = pl.program_id(0)

    @pl.when(step == 0)
    def _():
        for wt in range(2):
            for wf in range(2):
                time_ref[wt * 2 + wf] = key_times(wt, wf)
        for ref in (gq_ref, rows_ref, gqv_ref, tacc_ref):
            ref[...] = jnp.zeros_like(ref)

    frames = frames_ref[step]
    masks = head_masks(BF16)
    for g in range(GROUPS):
        tacc = None
        for w in range(4):
            rows = slice(w * SPOT, w * SPOT + SPOT)
            cq = slice(g * LANES, g * LANES + LANES)
            ck = slice(512 + g * LANES, 512 + g * LANES + LANES)
            cv = slice(1024 + g * LANES, 1024 + g * LANES + LANES)
            q = qkv_ref[rows, cq]
            k = qkv_ref[rows, ck]
            v = qkv_ref[rows, cv]
            do = stack_heads(datt_ref[rows, cq], masks)
            p = probs_ref[0, w, g]
            pf = p.astype(F32)
            dp = nt(v, do)
            inner = jnp.sum(pf * dp, axis=0, keepdims=True)
            ds = jnp.where(time_ref[w] < frames, pf * (dp - inner), 0.0)
            tacc = ds if tacc is None else tacc + ds
            ds = ds.astype(BF16)
            dj_ref[rows, cq] = (pick_heads(tn(ds, k)) * SCALE).astype(BF16)
            dj_ref[rows, ck] = (nn(ds, stack_heads(q, masks)) * SCALE).astype(BF16)
            dj_ref[rows, cv] = nn(p, do).astype(BF16)
        tacc_ref[g] += tacc
    n, inv = normalize(to_windows(tok_ref[...].astype(F32)))
    n1t = (n * rowp_ref[0:1] + rowp_ref[1:2]).astype(BF16).T
    dj = dj_ref[...]
    gqv_ref[:, :512] += fold(dj[:, :512].astype(F32))
    gqv_ref[:, 512:] += fold(dj[:, 1024:].astype(F32))
    dn1 = nt(dj, wqkv_ref[...])
    gq_ref[...] += nn(n1t, dj)
    rows_ref[0] += fold(dn1 * n)
    rows_ref[1] += fold(dn1)
    din = dmid_ref[...] + norm_back(dn1, n, inv, rowp_ref[0:1])
    din_ref[...] = from_windows(din)

    @pl.when(step == pl.num_programs(0) - 1)
    def _():
        row = iota((256, 256), 0)
        lane = iota((256, 256), 1)
        spot = row % SPOT
        base = 112 - (spot // WIN * (2 * WIN - 1) + spot % WIN)
        for h in range(PER):
            own = jnp.where((lane == base) & (row // SPOT == h), 1.0, 0.0).astype(F32).astype(BF16)
            for g in range(GROUPS):
                spread = None
                for part in split_three(tacc_ref[g]):
                    term = nn(part, own)
                    spread = term if spread is None else spread + term
                total = None
                for a in range(WIN):
                    piece = pltpu.roll(
                        spread[a * 8 : a * 8 + 8], 15 * a, axis=1, stride=1, stride_axis=0
                    )
                    total = piece if total is None else total + piece
                head = g * PER + h
                gt_ref[head : head + 1, :] = jnp.sum(total, axis=0, keepdims=True)


def whole(shape):
    return pl.BlockSpec(shape, lambda i: (0,) * len(shape))


def front(frames, tok, og, wqkv, bqv, table, wproj, w1, b1, w2, rowp):
    rows = tok.shape[0]
    clips = rows // CLIP
    line = lambda width: pl.BlockSpec((CLIP, width), lambda i: (i, 0))
    probs = (1, 4, GROUPS, SPOT, PER * SPOT)
    shape = jax.ShapeDtypeStruct
    return pl.pallas_call(
        front_kernel,
        grid=(clips,),
        in_specs=[pl.BlockSpec(memory_space=pltpu.SMEM), line(D), line(D)]
        + [whole(a.shape) for a in (wqkv, bqv, table, wproj, w1, b1, w2, rowp)],
        out_specs=[
            line(D),
            line(1536),
            pl.BlockSpec(probs, lambda i: (i, 0, 0, 0, 0)),
            line(512),
            line(D),
            whole((D, FF)),
            whole((D, FF)),
            whole((512, D)),
            whole((4, 8, D)),
            whole((8, FF)),
        ],
        out_shape=[
            shape((rows, D), F32),
            shape((rows, 1536), BF16),
            shape((clips,) + probs[1:], BF16),
            shape((rows, 512), BF16),
            shape((rows, D), F32),
            shape((D, FF), F32),
            shape((D, FF), F32),
            shape((512, D), F32),
            shape((4, 8, D), F32),
            shape((8, FF), F32),
        ],
        scratch_shapes=[
            pltpu.VMEM((GROUPS, SPOT, PER * SPOT), F32),
            pltpu.VMEM((4, SPOT, PER * SPOT), jnp.int32),
            pltpu.VMEM((CLIP, 512), BF16),
        ],
        compiler_params=pltpu.CompilerParams(vmem_limit_bytes=VMEM_LIMIT),
    )(frames, tok, og, wqkv, bqv, table, wproj, w1, b1, w2, rowp)


def back(frames, tok, qkv, probs, datt, dmid, wqkv, rowp):
    rows = tok.shape[0]
    clips = rows // CLIP
    line = lambda width: pl.BlockSpec((CLIP, width), lambda i: (i, 0))
    shape = jax.ShapeDtypeStruct
    return pl.pallas_call(
        back_kernel,
        grid=(clips,),
        in_specs=[
            pl.BlockSpec(memory_space=pltpu.SMEM),
            line(D),
            line(1536),
            pl.BlockSpec((1,) + probs.shape[1:], lambda i: (i, 0, 0, 0, 0)),
            line(512),
            line(D),
            whole(wqkv.shape),
            whole(rowp.shape),
        ],
        out_specs=[
            line(D),
            whole((D, 1536)),
            whole((2, 8, D)),
            whole((8, 1024)),
            whole((HEADS, 256)),
        ],
        out_shape=[
            shape((rows, D), F32),
            shape((D, 1536), F32),
            shape((2, 8, D), F32),
            shape((8, 1024), F32),
            shape((HEADS, 256), F32),
        ],
        scratch_shapes=[
            pltpu.VMEM((4, SPOT, PER * SPOT), jnp.int32),
            pltpu.VMEM((GROUPS, SPOT, PER * SPOT), F32),
            pltpu.VMEM((CLIP, 1536), BF16),
        ],
        compiler_params=pltpu.CompilerParams(vmem_limit_bytes=VMEM_LIMIT),
    )(frames, tok, qkv, probs, datt, dmid, wqkv, rowp)


def adam_step(weight, gradient, moment, second, factor, rate):
    clipped = gradient * factor
    moment_new = BETA_ONE * moment + (1.0 - BETA_ONE) * clipped
    second_new = BETA_TWO * second + (1.0 - BETA_TWO) * clipped * clipped
    moment_hat = moment_new / (1.0 - BETA_ONE**STEP)
    second_hat = second_new / (1.0 - BETA_TWO**STEP)
    master = weight - rate * (
        moment_hat / (jnp.sqrt(second_hat) + ADAM_EPS) + WEIGHT_DECAY * weight
    )
    return (gradient, moment_new, second_new, master)


def shards(
    tokens,
    out_grad,
    clip_frames,
    qkv_weight,
    qv_bias,
    rel_table,
    proj_weight,
    fc1_weight,
    fc1_bias,
    fc2_weight,
    row_params,
    qkv_first,
    qkv_second,
    qvb_first,
    qvb_second,
    table_first,
    table_second,
    proj_first,
    proj_second,
    fc1_first,
    fc1_second,
    fc1b_first,
    fc1b_second,
    fc2_first,
    fc2_second,
    rows_first,
    rows_second,
):
    gather = partial(lax.all_gather, axis_name="head", tiled=True)
    clips = tokens.shape[0] // CLIP
    parts = lax.axis_size("head")
    local = rel_table.shape[1] * HDIM
    groups = rel_table.shape[1] // PER
    frames = lax.dynamic_slice(clip_frames, (lax.axis_index("head") * clips,), (clips,))
    pad = LANES - PER * HDIM
    wqkv = qkv_weight.astype(BF16).reshape(D, 3, groups, PER * HDIM)
    wqkv = gather(jnp.pad(wqkv, ((0, 0), (0, 0), (0, 0), (0, pad))), axis=2).reshape(D, 1536)
    bqv = jnp.pad(qv_bias.reshape(2, groups, PER * HDIM), ((0, 0), (0, 0), (0, pad)))
    bqv = gather(bqv, axis=1).reshape(2, 512)
    table = gather(jnp.pad(rel_table.T, ((0, 0), (0, 256 - rel_table.shape[0]))), axis=0)
    wproj = proj_weight.astype(BF16).reshape(groups, PER * HDIM, D)
    wproj = gather(jnp.pad(wproj, ((0, 0), (0, pad), (0, 0))), axis=0).reshape(512, D)
    w1 = gather(fc1_weight.astype(BF16), axis=1)
    b1 = gather(fc1_bias, axis=0).reshape(1, FF)
    w2 = gather(fc2_weight.astype(BF16), axis=0)
    output, qkv, probs, datt, dmid, g1, g2, gp, rows_f, gb = front(
        frames, tokens, out_grad, wqkv, bqv, table, wproj, w1, b1, w2, row_params
    )
    input_grad, gq, rows_b, gqv, gt = back(
        frames, tokens, qkv, probs, datt, dmid, wqkv, row_params
    )
    scatter = lambda v, dim: lax.psum(
        lax.psum_scatter(v, "head", scatter_dimension=dim, tiled=True), "win"
    )
    qkv_summed = scatter(gq.reshape(D, 3, GROUPS, LANES), 2)[..., : PER * HDIM].reshape(D, 3, local)
    gqv = jnp.sum(gqv, axis=0).reshape(2, GROUPS, LANES)
    qvb_summed = scatter(gqv, 1)[..., : PER * HDIM].reshape(2, local)
    table_summed = scatter(gt, 0)[:, : rel_table.shape[0]][:, ::-1].T
    proj_summed = scatter(gp.reshape(GROUPS, LANES, D), 0)[:, : PER * HDIM].reshape(local, D)
    fc1_summed = scatter(g1, 1)
    fc1b_summed = scatter(jnp.sum(gb, axis=0), 0)
    fc2_summed = scatter(g2, 1).T
    rows_gradient = lax.psum(jnp.sum(jnp.concatenate([rows_b, rows_f]), axis=1), ("win", "head"))
    gradients = (
        qkv_summed,
        qvb_summed,
        table_summed,
        proj_summed,
        fc1_summed,
        fc1b_summed,
        fc2_summed,
        rows_gradient,
    )
    square = lambda v: jnp.sum(v * v)
    total = lax.psum(sum(square(g) for g in gradients[:7]), "head")
    grad_norm = jnp.sqrt(total + square(rows_gradient))
    factor = jnp.minimum(1.0, CLIP_LIMIT / (grad_norm + 1e-06))
    weights = (
        qkv_weight,
        qv_bias,
        rel_table,
        proj_weight,
        fc1_weight,
        fc1_bias,
        fc2_weight,
        row_params,
    )
    firsts = (
        qkv_first,
        qvb_first,
        table_first,
        proj_first,
        fc1_first,
        fc1b_first,
        fc2_first,
        rows_first,
    )
    seconds = (
        qkv_second,
        qvb_second,
        table_second,
        proj_second,
        fc1_second,
        fc1b_second,
        fc2_second,
        rows_second,
    )
    rates = (
        LEARN_RATE,
        LEARN_RATE,
        ROW_RATE,
        LEARN_RATE,
        LEARN_RATE,
        LEARN_RATE,
        LEARN_RATE,
        ROW_RATE,
    )
    updated = []
    for weight, gradient, moment, second, rate in zip(weights, gradients, firsts, seconds, rates):
        updated.extend(adam_step(weight, gradient, moment, second, factor, rate))
    return (output, input_grad, grad_norm, *updated)


def solution(mesh):
    rows = P(("win", "head"), None)
    last3, last2, first2, first1 = P(None, None, "head"), P(None, "head"), P("head", None), P("head")
    each = (last3, last2, last2, first2, last2, first1, first2, P())
    return jax.shard_map(
        shards,
        mesh=mesh,
        in_specs=(rows, rows, P("win")) + each + tuple(s for s in each for _ in range(2)),
        out_specs=(rows, rows, P()) + tuple(s for s in each for _ in range(4)),
        check_vma=False,
    )
```

```python
from functools import partial

import jax
import jax.numpy as jnp
from jax import lax
from jax.experimental import pallas as pl
from jax.experimental.pallas import tpu as pltpu
from jax.sharding import PartitionSpec as P

D = 384
HDIM = 24
HEADS = 16
GROUPS = 4
PER = 4
LANES = 128
FF = 1536
GRID = 16
WIN = 8
CLIP = GRID * GRID
SPOT = WIN * WIN
SHIFT = 4
STEP = 10
CHUNK = 384

NORM_EPS = 1e-05
MASKED = -1000000000.0
CLIP_LIMIT = 1.0
LEARN_RATE = 0.1
ROW_RATE = 0.5
BETA_ONE = 0.9
BETA_TWO = 0.999
ADAM_EPS = 1e-08
WEIGHT_DECAY = 0.01
SCALE = HDIM ** (-0.5)
F32 = jnp.float32
BF16 = jnp.bfloat16
VMEM_LIMIT = 58 * 1024 * 1024


def nn(a, b):
    return lax.dot_general(a, b, (((1,), (0,)), ((), ())), preferred_element_type=F32)


def nt(a, b):
    return lax.dot_general(a, b, (((1,), (1,)), ((), ())), preferred_element_type=F32)


def tn(a, b):
    return lax.dot_general(a, b, (((0,), (0,)), ((), ())), preferred_element_type=F32)


def iota(shape, axis):
    return lax.broadcasted_iota(jnp.int32, shape, axis)


def fold(x):
    return jnp.sum(x.reshape(x.shape[0] // 8, 8, x.shape[1]), axis=0)


def normalize(x):
    center = x - jnp.mean(x, axis=-1, keepdims=True)
    spread = jnp.mean(center * center, axis=-1, keepdims=True)
    inverse = lax.rsqrt(spread + NORM_EPS)
    return center * inverse, inverse


def norm_back(e, n, inverse, gain):
    q = e * gain
    return inverse * (
        q - jnp.mean(q, axis=-1, keepdims=True) - n * jnp.mean(q * n, axis=-1, keepdims=True)
    )


def to_windows(x):
    low = iota((8, x.shape[1]), 0) < 4
    first, second = [], []
    for t in range(GRID):
        a = x[16 * t : 16 * t + 8]
        b = x[16 * t + 8 : 16 * t + 16]
        first.append(pltpu.roll(jnp.where(low, b, a), 4, axis=0))
        second.append(pltpu.roll(jnp.where(low, a, b), 4, axis=0))
    pieces = []
    for wt in range(2):
        for side in (first, second):
            for a in range(WIN):
                pieces.append(side[(wt * WIN + a + SHIFT) % GRID])
    return jnp.concatenate(pieces, axis=0)


def from_windows(y):
    low = iota((8, y.shape[1]), 0) < 4
    pieces = []
    for t in range(GRID):
        rolled = (t - SHIFT) % GRID
        base = (rolled // WIN) * 128 + (rolled % WIN) * 8
        u = pltpu.roll(y[base : base + 8], 4, axis=0)
        v = pltpu.roll(y[base + 64 : base + 72], 4, axis=0)
        pieces.append(jnp.where(low, v, u))
        pieces.append(jnp.where(low, u, v))
    return jnp.concatenate(pieces, axis=0)


def head_masks(dtype):
    lane = iota((16, LANES), 1) // HDIM
    return [jnp.where(lane == h, 1.0, 0.0).astype(F32).astype(dtype) for h in range(PER)]


def stack_heads(x, masks):
    tiles = x.reshape(SPOT // 16, 16, LANES)
    return jnp.concatenate([(tiles * m[None]).reshape(SPOT, LANES) for m in masks], axis=0)


def pick_heads(r):
    lane = iota((SPOT, LANES), 1)
    out = r[3 * SPOT :]
    for h in (2, 1, 0):
        out = jnp.where(lane < (h + 1) * HDIM, r[h * SPOT : (h + 1) * SPOT], out)
    return out


def key_times(wt, wf):
    j = iota((SPOT, PER * SPOT), 0)
    i = iota((SPOT, PER * SPOT), 1) % SPOT
    time = (wt * WIN + j // WIN + SHIFT) % GRID
    same = j >= 0
    if wt:
        same = same & ((j // WIN < 4) == (i // WIN < 4))
    if wf:
        same = same & ((j % WIN < 4) == (i % WIN < 4))
    return jnp.where(same, time, 99)


def split_three(x):
    one = x.astype(BF16)
    rest = x - one.astype(F32)
    two = rest.astype(BF16)
    three = (rest - two.astype(F32)).astype(BF16)
    return one, two, three


def build_bias(table_ref, bias_ref):
    row = iota((256, 256), 0)
    lane = iota((256, 256), 1)
    spot = lane % SPOT
    base = spot // WIN * (2 * WIN - 1) + spot % WIN
    for g in range(GROUPS):
        total = None
        for h in range(PER):
            own = jnp.where((row == base) & (lane // SPOT == h), 1.0, 0.0).astype(F32).astype(BF16)
            line = jnp.broadcast_to(table_ref[g, 1 + h : 2 + h, :256], (8, 256))
            spread = jnp.concatenate(
                [
                    pltpu.roll(line, (15 * a + 144) % 256, axis=1, stride=1, stride_axis=0)
                    for a in range(WIN)
                ],
                axis=0,
            )
            for part in split_three(spread):
                term = nn(part, own)
                total = term if total is None else total + term
        bias_ref[g] = total


def gelu_parts(u):
    mag = jnp.abs(u) * (0.5**0.5)
    t = 1.0 / (1.0 + 0.3275911 * mag)
    bell = jnp.exp(-0.5 * (u * u))
    poly = t * (
        0.127414796
        + t * (-0.142248368 + t * (0.7107068705 + t * (-0.7265760135 + t * 0.5307027145)))
    )
    tail = poly * bell
    return jnp.where(u >= 0.0, 1.0 - tail, tail), bell * 0.3989422804014327


def place(win, head):
    return {"win": win, "head": head}


def remote(src, dst, send, recv, win, head):
    return pltpu.make_async_remote_copy(
        src_ref=src,
        dst_ref=dst,
        send_sem=send,
        recv_sem=recv,
        device_id=place(win, head),
        device_id_type=pl.DeviceIdType.MESH,
    )


def position():
    win, head = lax.axis_index("win"), lax.axis_index("head")
    core, cell = win % 2, (win // 2) % 4
    return win, head, core, cell, win - core - 2 * cell


def greet():
    win, head, core, cell, base = position()
    barrier = pltpu.get_barrier_semaphore()
    peers = [(win, (head + d) % 4) for d in (1, 2, 3)]
    peers += [(base + 2 * ((cell + d) % 4) + core, head) for d in (1, 2, 3)]
    peers += [(win + 1 - 2 * core, head)]
    for w, h in peers:
        pl.semaphore_signal(barrier, inc=1, device_id=place(w, h), device_id_type=pl.DeviceIdType.MESH)
    pl.semaphore_wait(barrier, len(peers))


def shard_view(ref, wide, head, start, count):
    if wide:
        return ref.at[pl.ds(start, count), pl.ds(pl.multiple_of(head * D, LANES), D)]
    rows = ref.shape[0] // 4
    return ref.at[pl.ds(pl.multiple_of(head * rows + start, 16), count), :]


def gather_stages(own, full, wide, sems):
    win, head, core, cell, base = position()
    rows = own.shape[0]
    half, part = rows // 2, rows // 8
    mine = pl.multiple_of(core * half + cell * part, 16)
    near = pl.multiple_of(core * half, 16)

    def over_head(d):
        view = shard_view(full, wide, head, mine, part)
        return remote(
            own.at[pl.ds(mine, part), :], view, sems.at[0, d], sems.at[1, d], win, (head + d + 1) % 4
        )

    def over_cell(d, c):
        view = shard_view(full, wide, (head + 3 - d) % 4, mine, part)
        peer = base + 2 * ((cell + c + 1) % 4) + core
        return remote(view, view, sems.at[2 + c, d], sems.at[5 + c, d], peer, head)

    def over_core(d):
        view = shard_view(full, wide, (head + 3 - d) % 4, near, half)
        return remote(view, view, sems.at[8, d], sems.at[9, d], win + 1 - 2 * core, head)

    local = pltpu.make_async_copy(own, shard_view(full, wide, head, 0, rows), sems.at[10, 0])

    def first():
        local.start()
        for d in range(3):
            over_head(d).start()

    def second():
        for d in range(3):
            over_head(d).wait_recv()
            for c in range(3):
                over_cell(d, c).start()

    def third():
        for d in range(3):
            for c in range(3):
                over_cell(d, c).wait_recv()
            over_core(d).start()

    def last():
        for d in range(3):
            over_core(d).wait_recv()
        local.wait()
        for d in range(3):
            over_head(d).wait_send()
            for c in range(3):
                over_cell(d, c).wait_send()
            over_core(d).wait_send()

    return first, second, third, last


def front_kernel(
    frames_ref,
    tok_ref,
    og_ref,
    qown_ref,
    pown_ref,
    aown_ref,
    bown_ref,
    sown_ref,
    rowp_ref,
    out_ref,
    qkv_ref,
    probs_ref,
    datt_ref,
    dmid_ref,
    g1_ref,
    g2_ref,
    gp_ref,
    rows_ref,
    gb_ref,
    wout_ref,
    bias_ref,
    time_ref,
    att_ref,
    wqkv_ref,
    wproj_ref,
    w1_ref,
    w2_ref,
    small_ref,
    bqkv_ref,
    b1_ref,
    wsems,
    ssems,
):
    step = pl.program_id(0)

    @pl.when(step == 0)
    def _():
        greet()
        win, head = lax.axis_index("win"), lax.axis_index("head")
        stages = [
            gather_stages(own, full, wide, wsems.at[i])
            for i, (own, full, wide) in enumerate(
                (
                    (qown_ref, wqkv_ref, True),
                    (pown_ref, wproj_ref, False),
                    (aown_ref, w1_ref, True),
                    (bown_ref, w2_ref, False),
                )
            )
        ]
        small = [
            remote(
                sown_ref, small_ref.at[head], ssems.at[0, d], ssems.at[1, d], win, (head + d + 1) % 4
            )
            for d in range(3)
        ]
        own_small = pltpu.make_async_copy(sown_ref, small_ref.at[head], ssems.at[2, 0])
        own_small.start()
        for copy in small:
            copy.start()
        for k in range(4):
            for stage in stages:
                stage[k]()
        own_small.wait()
        for copy in small:
            copy.wait()
        for g in range(4):
            bqkv_ref[0:1, g * D : g * D + LANES] = small_ref[g, 0:1, :LANES]
            bqkv_ref[0:1, g * D + LANES : g * D + 2 * LANES] = jnp.zeros((1, LANES), F32)
            bqkv_ref[0:1, g * D + 2 * LANES : g * D + D] = small_ref[g, 0:1, LANES : 2 * LANES]
            b1_ref[0:1, g * D : g * D + D] = small_ref[g, 5:6, :]
        build_bias(small_ref, bias_ref)
        for wt in range(2):
            for wf in range(2):
                time_ref[wt * 2 + wf] = key_times(wt, wf)
        for ref in (g1_ref, g2_ref, gp_ref, rows_ref, gb_ref):
            ref[...] = jnp.zeros_like(ref)

    frames = frames_ref[step]
    x = to_windows(tok_ref[...].astype(F32))
    og = to_windows(og_ref[...].astype(F32))
    n1, _ = normalize(x)
    n1 = (n1 * rowp_ref[0:1] + rowp_ref[1:2]).astype(BF16)
    for part in range(3):
        cols = slice(part * 512, part * 512 + 512)
        y = nn(n1, wqkv_ref[:, cols]) + bqkv_ref[0:1, cols]
        qkv_ref[:, cols] = y.astype(BF16)
    masks = head_masks(BF16)
    for w in range(4):
        rows = slice(w * SPOT, w * SPOT + SPOT)
        for g in range(GROUPS):
            q = qkv_ref[rows, g * D : g * D + LANES]
            k = qkv_ref[rows, g * D + LANES : g * D + 2 * LANES]
            v = qkv_ref[rows, g * D + 2 * LANES : g * D + D]
            s = nt(k, stack_heads(q, masks)) * SCALE + bias_ref[g]
            s = jnp.where(time_ref[w] < frames, s, MASKED)
            e = jnp.exp(s - jnp.max(s, axis=0, keepdims=True))
            p = (e * (1.0 / jnp.sum(e, axis=0, keepdims=True))).astype(BF16)
            probs_ref[0, w, g] = p
            o = pick_heads(tn(p, v))
            att_ref[rows, g * LANES : g * LANES + LANES] = o.astype(BF16)
    att = att_ref[...]
    middle = x + nn(att, wproj_ref[...]) + rowp_ref[4:5]
    nrm, inv = normalize(middle)
    n2f = nrm * rowp_ref[2:3] + rowp_ref[3:4]
    n2 = n2f.astype(BF16)
    n2t = n2.T
    ogb = og.astype(BF16)
    ogt = ogb.T
    ffn = None
    dn2 = None
    for c in range(FF // CHUNK):
        cols = slice(c * CHUNK, c * CHUNK + CHUNK)
        u = nn(n2, w1_ref[:, cols]) + b1_ref[0:1, cols]
        phi, dens = gelu_parts(u)
        hid = (u * phi).astype(BF16)
        du = ((phi + u * dens) * nt(ogb, w2_ref[cols, :])).astype(BF16)
        gb_ref[:, cols] += fold(du.astype(F32))
        g1_ref[:, cols] += nn(n2t, du)
        g2_ref[:, cols] += nn(ogt, hid)
        a = nn(hid, w2_ref[cols, :])
        b = nt(du, w1_ref[:, cols])
        ffn = a if ffn is None else ffn + a
        dn2 = b if dn2 is None else dn2 + b
    out_ref[...] = from_windows(middle + ffn + rowp_ref[5:6])
    dmid = og + norm_back(dn2, nrm, inv, rowp_ref[2:3])
    dmid_ref[...] = dmid
    dbr = dmid.astype(BF16)
    rows_ref[0] += fold(dn2 * nrm)
    rows_ref[1] += fold(dn2)
    rows_ref[2] += fold(dbr.astype(F32))
    rows_ref[3] += fold(og)
    gp_ref[...] += tn(att, dbr)
    datt_ref[...] = nt(dbr, wproj_ref[...]).astype(BF16)

    @pl.when(step == pl.num_programs(0) - 1)
    def _():
        wout_ref[...] = wqkv_ref[...]


def back_kernel(
    frames_ref,
    tok_ref,
    qkv_ref,
    probs_ref,
    datt_ref,
    dmid_ref,
    wqkv_ref,
    rowp_ref,
    din_ref,
    gq_ref,
    rows_ref,
    gqv_ref,
    gt_ref,
    time_ref,
    tacc_ref,
    dj_ref,
):
    step = pl.program_id(0)

    @pl.when(step == 0)
    def _():
        for wt in range(2):
            for wf in range(2):
                time_ref[wt * 2 + wf] = key_times(wt, wf)
        for ref in (gq_ref, rows_ref, gqv_ref, tacc_ref):
            ref[...] = jnp.zeros_like(ref)

    frames = frames_ref[step]
    masks = head_masks(BF16)
    for g in range(GROUPS):
        tacc = None
        for w in range(4):
            rows = slice(w * SPOT, w * SPOT + SPOT)
            cq = slice(g * D, g * D + LANES)
            ck = slice(g * D + LANES, g * D + 2 * LANES)
            cv = slice(g * D + 2 * LANES, g * D + D)
            q = qkv_ref[rows, cq]
            k = qkv_ref[rows, ck]
            v = qkv_ref[rows, cv]
            do = stack_heads(datt_ref[rows, g * LANES : g * LANES + LANES], masks)
            p = probs_ref[0, w, g]
            pf = p.astype(F32)
            dp = nt(v, do)
            inner = jnp.sum(pf * dp, axis=0, keepdims=True)
            ds = jnp.where(time_ref[w] < frames, pf * (dp - inner), 0.0)
            tacc = ds if tacc is None else tacc + ds
            ds = ds.astype(BF16)
            dj_ref[rows, cq] = (pick_heads(tn(ds, k)) * SCALE).astype(BF16)
            dj_ref[rows, ck] = (nn(ds, stack_heads(q, masks)) * SCALE).astype(BF16)
            dj_ref[rows, cv] = nn(p, do).astype(BF16)
        tacc_ref[g] += tacc
    n, inv = normalize(to_windows(tok_ref[...].astype(F32)))
    n1t = (n * rowp_ref[0:1] + rowp_ref[1:2]).astype(BF16).T
    dj = dj_ref[...]
    gqv_ref[...] += fold(dj.astype(F32))
    dn1 = nt(dj, wqkv_ref[...])
    gq_ref[...] += nn(n1t, dj)
    rows_ref[0] += fold(dn1 * n)
    rows_ref[1] += fold(dn1)
    din = dmid_ref[...] + norm_back(dn1, n, inv, rowp_ref[0:1])
    din_ref[...] = from_windows(din)

    @pl.when(step == pl.num_programs(0) - 1)
    def _():
        row = iota((256, 256), 0)
        lane = iota((256, 256), 1)
        spot = row % SPOT
        base = 112 - (spot // WIN * (2 * WIN - 1) + spot % WIN)
        for h in range(PER):
            own = jnp.where((lane == base) & (row // SPOT == h), 1.0, 0.0).astype(F32).astype(BF16)
            for g in range(GROUPS):
                spread = None
                for part in split_three(tacc_ref[g]):
                    term = nn(part, own)
                    spread = term if spread is None else spread + term
                total = None
                for a in range(WIN):
                    piece = pltpu.roll(
                        spread[a * 8 : a * 8 + 8], 15 * a, axis=1, stride=1, stride_axis=0
                    )
                    total = piece if total is None else total + piece
                head = g * PER + h
                gt_ref[head : head + 1, :] = jnp.sum(total, axis=0, keepdims=True)


def whole(shape):
    return pl.BlockSpec(shape, lambda i: (0,) * len(shape))


def front(frames, tok, og, qown, pown, aown, bown, sown, rowp):
    rows = tok.shape[0]
    clips = rows // CLIP
    line = lambda width: pl.BlockSpec((CLIP, width), lambda i: (i, 0))
    probs = (1, 4, GROUPS, SPOT, PER * SPOT)
    shape = jax.ShapeDtypeStruct
    sems = pltpu.SemaphoreType.DMA
    return pl.pallas_call(
        front_kernel,
        grid=(clips,),
        in_specs=[pl.BlockSpec(memory_space=pltpu.SMEM), line(D), line(D)]
        + [whole(a.shape) for a in (qown, pown, aown, bown, sown, rowp)],
        out_specs=[
            line(D),
            line(1536),
            pl.BlockSpec(probs, lambda i: (i, 0, 0, 0, 0)),
            line(512),
            line(D),
            whole((D, FF)),
            whole((D, FF)),
            whole((512, D)),
            whole((4, 8, D)),
            whole((8, FF)),
            whole((D, 1536)),
        ],
        out_shape=[
            shape((rows, D), F32),
            shape((rows, 1536), BF16),
            shape((clips,) + probs[1:], BF16),
            shape((rows, 512), BF16),
            shape((rows, D), F32),
            shape((D, FF), F32),
            shape((D, FF), F32),
            shape((512, D), F32),
            shape((4, 8, D), F32),
            shape((8, FF), F32),
            shape((D, 1536), BF16),
        ],
        scratch_shapes=[
            pltpu.VMEM((GROUPS, SPOT, PER * SPOT), F32),
            pltpu.VMEM((4, SPOT, PER * SPOT), jnp.int32),
            pltpu.VMEM((CLIP, 512), BF16),
            pltpu.VMEM((D, 1536), BF16),
            pltpu.VMEM((512, D), BF16),
            pltpu.VMEM((D, FF), BF16),
            pltpu.VMEM((FF, D), BF16),
            pltpu.VMEM((GROUPS, 8, D), F32),
            pltpu.VMEM((8, 1536), F32),
            pltpu.VMEM((8, FF), F32),
            sems((4, 11, 3)),
            sems((3, 3)),
        ],
        compiler_params=pltpu.CompilerParams(
            vmem_limit_bytes=VMEM_LIMIT, collective_id=0, has_side_effects=True
        ),
    )(frames, tok, og, qown, pown, aown, bown, sown, rowp)


def back(frames, tok, qkv, probs, datt, dmid, wqkv, rowp):
    rows = tok.shape[0]
    clips = rows // CLIP
    line = lambda width: pl.BlockSpec((CLIP, width), lambda i: (i, 0))
    shape = jax.ShapeDtypeStruct
    return pl.pallas_call(
        back_kernel,
        grid=(clips,),
        in_specs=[
            pl.BlockSpec(memory_space=pltpu.SMEM),
            line(D),
            line(1536),
            pl.BlockSpec((1,) + probs.shape[1:], lambda i: (i, 0, 0, 0, 0)),
            line(512),
            line(D),
            whole(wqkv.shape),
            whole(rowp.shape),
        ],
        out_specs=[
            line(D),
            whole((D, 1536)),
            whole((2, 8, D)),
            whole((8, 1536)),
            whole((HEADS, 256)),
        ],
        out_shape=[
            shape((rows, D), F32),
            shape((D, 1536), F32),
            shape((2, 8, D), F32),
            shape((8, 1536), F32),
            shape((HEADS, 256), F32),
        ],
        scratch_shapes=[
            pltpu.VMEM((4, SPOT, PER * SPOT), jnp.int32),
            pltpu.VMEM((GROUPS, SPOT, PER * SPOT), F32),
            pltpu.VMEM((CLIP, 1536), BF16),
        ],
        compiler_params=pltpu.CompilerParams(vmem_limit_bytes=VMEM_LIMIT),
    )(frames, tok, qkv, probs, datt, dmid, wqkv, rowp)


def adam_step(weight, gradient, moment, second, factor, rate):
    clipped = gradient * factor
    moment_new = BETA_ONE * moment + (1.0 - BETA_ONE) * clipped
    second_new = BETA_TWO * second + (1.0 - BETA_TWO) * clipped * clipped
    moment_hat = moment_new / (1.0 - BETA_ONE**STEP)
    second_hat = second_new / (1.0 - BETA_TWO**STEP)
    master = weight - rate * (
        moment_hat / (jnp.sqrt(second_hat) + ADAM_EPS) + WEIGHT_DECAY * weight
    )
    return (gradient, moment_new, second_new, master)


def shards(
    tokens,
    out_grad,
    clip_frames,
    qkv_weight,
    qv_bias,
    rel_table,
    proj_weight,
    fc1_weight,
    fc1_bias,
    fc2_weight,
    row_params,
    qkv_first,
    qkv_second,
    qvb_first,
    qvb_second,
    table_first,
    table_second,
    proj_first,
    proj_second,
    fc1_first,
    fc1_second,
    fc1b_first,
    fc1b_second,
    fc2_first,
    fc2_second,
    rows_first,
    rows_second,
):
    clips = tokens.shape[0] // CLIP
    local = rel_table.shape[1] * HDIM
    offsets = rel_table.shape[0]
    frames = lax.dynamic_slice(clip_frames, (lax.axis_index("head") * clips,), (clips,))
    pad = LANES - local
    qown = jnp.pad(qkv_weight.astype(BF16), ((0, 0), (0, 0), (0, pad))).reshape(D, D)
    pown = jnp.pad(proj_weight.astype(BF16), ((0, pad), (0, 0)))
    aown, bown = fc1_weight.astype(BF16), fc2_weight.astype(BF16)
    bias_row = jnp.pad(qv_bias, ((0, 1), (0, pad))).reshape(1, D)
    sown = jnp.concatenate(
        [
            bias_row,
            jnp.pad(rel_table.T, ((0, 0), (0, D - offsets))),
            fc1_bias[None],
            jnp.zeros((2, D), F32),
        ]
    )
    output, qkv, probs, datt, dmid, g1, g2, gp, rows_f, gb, wqkv = front(
        frames, tokens, out_grad, qown, pown, aown, bown, sown, row_params
    )
    input_grad, gq, rows_b, gqv, gt = back(
        frames, tokens, qkv, probs, datt, dmid, wqkv, row_params
    )
    scatter = lambda v, dim: lax.psum(
        lax.psum_scatter(v, "head", scatter_dimension=dim, tiled=True), "win"
    )
    qkv_summed = scatter(gq, 1).reshape(D, 3, LANES)[..., :local]
    qvb_summed = scatter(jnp.sum(gqv, axis=0), 0).reshape(3, LANES)[::2, :local]
    table_summed = scatter(gt, 0)[:, : offsets][:, ::-1].T
    proj_summed = scatter(gp.reshape(GROUPS, LANES, D), 0)[:, : PER * HDIM].reshape(local, D)
    fc1_summed = scatter(g1, 1)
    fc1b_summed = scatter(jnp.sum(gb, axis=0), 0)
    fc2_summed = scatter(g2, 1).T
    rows_gradient = lax.psum(jnp.sum(jnp.concatenate([rows_b, rows_f]), axis=1), ("win", "head"))
    gradients = (
        qkv_summed,
        qvb_summed,
        table_summed,
        proj_summed,
        fc1_summed,
        fc1b_summed,
        fc2_summed,
        rows_gradient,
    )
    square = lambda v: jnp.sum(v * v)
    total = lax.psum(sum(square(g) for g in gradients[:7]), "head")
    grad_norm = jnp.sqrt(total + square(rows_gradient))
    factor = jnp.minimum(1.0, CLIP_LIMIT / (grad_norm + 1e-06))
    weights = (
        qkv_weight,
        qv_bias,
        rel_table,
        proj_weight,
        fc1_weight,
        fc1_bias,
        fc2_weight,
        row_params,
    )
    firsts = (
        qkv_first,
        qvb_first,
        table_first,
        proj_first,
        fc1_first,
        fc1b_first,
        fc2_first,
        rows_first,
    )
    seconds = (
        qkv_second,
        qvb_second,
        table_second,
        proj_second,
        fc1_second,
        fc1b_second,
        fc2_second,
        rows_second,
    )
    rates = (
        LEARN_RATE,
        LEARN_RATE,
        ROW_RATE,
        LEARN_RATE,
        LEARN_RATE,
        LEARN_RATE,
        LEARN_RATE,
        ROW_RATE,
    )
    updated = []
    for weight, gradient, moment, second, rate in zip(weights, gradients, firsts, seconds, rates):
        updated.extend(adam_step(weight, gradient, moment, second, factor, rate))
    return (output, input_grad, grad_norm, *updated)


def solution(mesh):
    rows = P(("win", "head"), None)
    last3, last2, first2, first1 = P(None, None, "head"), P(None, "head"), P("head", None), P("head")
    each = (last3, last2, last2, first2, last2, first1, first2, P())
    return jax.shard_map(
        shards,
        mesh=mesh,
        in_specs=(rows, rows, P("win")) + each + tuple(s for s in each for _ in range(2)),
        out_specs=(rows, rows, P()) + tuple(s for s in each for _ in range(4)),
        check_vma=False,
    )
```

```python
from functools import partial

import jax
import jax.numpy as jnp
from jax import lax
from jax.experimental import pallas as pl
from jax.experimental.pallas import tpu as pltpu
from jax.sharding import PartitionSpec as P

D = 384
HDIM = 24
HEADS = 16
GROUPS = 4
PER = 4
LANES = 128
FF = 1536
GRID = 16
WIN = 8
CLIP = GRID * GRID
SPOT = WIN * WIN
SHIFT = 4
STEP = 10
CHUNK = 384

NORM_EPS = 1e-05
MASKED = -1000000000.0
CLIP_LIMIT = 1.0
LEARN_RATE = 0.1
ROW_RATE = 0.5
BETA_ONE = 0.9
BETA_TWO = 0.999
ADAM_EPS = 1e-08
WEIGHT_DECAY = 0.01
SCALE = HDIM ** (-0.5)
F32 = jnp.float32
BF16 = jnp.bfloat16
VMEM_LIMIT = 58 * 1024 * 1024


def nn(a, b):
    return lax.dot_general(a, b, (((1,), (0,)), ((), ())), preferred_element_type=F32)


def nt(a, b):
    return lax.dot_general(a, b, (((1,), (1,)), ((), ())), preferred_element_type=F32)


def tn(a, b):
    return lax.dot_general(a, b, (((0,), (0,)), ((), ())), preferred_element_type=F32)


def iota(shape, axis):
    return lax.broadcasted_iota(jnp.int32, shape, axis)


def fold(x):
    return jnp.sum(x.reshape(x.shape[0] // 8, 8, x.shape[1]), axis=0)


def normalize(x):
    center = x - jnp.mean(x, axis=-1, keepdims=True)
    spread = jnp.mean(center * center, axis=-1, keepdims=True)
    inverse = lax.rsqrt(spread + NORM_EPS)
    return center * inverse, inverse


def norm_back(e, n, inverse, gain):
    q = e * gain
    return inverse * (
        q - jnp.mean(q, axis=-1, keepdims=True) - n * jnp.mean(q * n, axis=-1, keepdims=True)
    )


def to_windows(x):
    low = iota((8, x.shape[1]), 0) < 4
    first, second = [], []
    for t in range(GRID):
        a = x[16 * t : 16 * t + 8]
        b = x[16 * t + 8 : 16 * t + 16]
        first.append(pltpu.roll(jnp.where(low, b, a), 4, axis=0))
        second.append(pltpu.roll(jnp.where(low, a, b), 4, axis=0))
    pieces = []
    for wt in range(2):
        for side in (first, second):
            for a in range(WIN):
                pieces.append(side[(wt * WIN + a + SHIFT) % GRID])
    return jnp.concatenate(pieces, axis=0)


def from_windows(y):
    low = iota((8, y.shape[1]), 0) < 4
    pieces = []
    for t in range(GRID):
        rolled = (t - SHIFT) % GRID
        base = (rolled // WIN) * 128 + (rolled % WIN) * 8
        u = pltpu.roll(y[base : base + 8], 4, axis=0)
        v = pltpu.roll(y[base + 64 : base + 72], 4, axis=0)
        pieces.append(jnp.where(low, v, u))
        pieces.append(jnp.where(low, u, v))
    return jnp.concatenate(pieces, axis=0)


def head_masks(dtype):
    lane = iota((16, LANES), 1) // HDIM
    return [jnp.where(lane == h, 1.0, 0.0).astype(F32).astype(dtype) for h in range(PER)]


def stack_heads(x, masks):
    tiles = x.reshape(SPOT // 16, 16, LANES)
    return jnp.concatenate([(tiles * m[None]).reshape(SPOT, LANES) for m in masks], axis=0)


def pick_heads(r):
    lane = iota((SPOT, LANES), 1)
    out = r[3 * SPOT :]
    for h in (2, 1, 0):
        out = jnp.where(lane < (h + 1) * HDIM, r[h * SPOT : (h + 1) * SPOT], out)
    return out


def key_times(wt, wf):
    j = iota((SPOT, PER * SPOT), 0)
    i = iota((SPOT, PER * SPOT), 1) % SPOT
    time = (wt * WIN + j // WIN + SHIFT) % GRID
    same = j >= 0
    if wt:
        same = same & ((j // WIN < 4) == (i // WIN < 4))
    if wf:
        same = same & ((j % WIN < 4) == (i % WIN < 4))
    return jnp.where(same, time, 99)


def split_three(x):
    one = x.astype(BF16)
    rest = x - one.astype(F32)
    two = rest.astype(BF16)
    three = (rest - two.astype(F32)).astype(BF16)
    return one, two, three


def build_bias(table_ref, bias_ref):
    row = iota((256, 256), 0)
    lane = iota((256, 256), 1)
    spot = lane % SPOT
    base = spot // WIN * (2 * WIN - 1) + spot % WIN
    for g in range(GROUPS):
        total = None
        for h in range(PER):
            own = jnp.where((row == base) & (lane // SPOT == h), 1.0, 0.0).astype(F32).astype(BF16)
            line = jnp.broadcast_to(table_ref[g, 1 + h : 2 + h, :256], (8, 256))
            spread = jnp.concatenate(
                [
                    pltpu.roll(line, (15 * a + 144) % 256, axis=1, stride=1, stride_axis=0)
                    for a in range(WIN)
                ],
                axis=0,
            )
            for part in split_three(spread):
                term = nn(part, own)
                total = term if total is None else total + term
        bias_ref[g] = total


def gelu_parts(u):
    mag = jnp.abs(u) * (0.5**0.5)
    t = 1.0 / (1.0 + 0.3275911 * mag)
    bell = jnp.exp(-0.5 * (u * u))
    poly = t * (
        0.127414796
        + t * (-0.142248368 + t * (0.7107068705 + t * (-0.7265760135 + t * 0.5307027145)))
    )
    tail = poly * bell
    return jnp.where(u >= 0.0, 1.0 - tail, tail), bell * 0.3989422804014327


def place(win, head):
    return {"win": win, "head": head}


def remote(src, dst, send, recv, win, head):
    return pltpu.make_async_remote_copy(
        src_ref=src,
        dst_ref=dst,
        send_sem=send,
        recv_sem=recv,
        device_id=place(win, head),
        device_id_type=pl.DeviceIdType.MESH,
    )


def position():
    win, head = lax.axis_index("win"), lax.axis_index("head")
    core, cell = win % 2, (win // 2) % 4
    return win, head, core, cell, win - core - 2 * cell


def greet():
    win, head, core, cell, base = position()
    barrier = pltpu.get_barrier_semaphore()
    peers = [(win, (head + d) % 4) for d in (1, 2, 3)]
    peers += [(base + 2 * ((cell + d) % 4) + core, head) for d in (1, 2, 3)]
    peers += [(win + 1 - 2 * core, head)]
    for w, h in peers:
        pl.semaphore_signal(barrier, inc=1, device_id=place(w, h), device_id_type=pl.DeviceIdType.MESH)
    pl.semaphore_wait(barrier, len(peers))


def shard_view(ref, wide, head, start, count):
    if wide:
        return ref.at[pl.ds(start, count), pl.ds(pl.multiple_of(head * D, LANES), D)]
    rows = ref.shape[0] // 4
    return ref.at[pl.ds(pl.multiple_of(head * rows + start, 16), count), :]


def gather_stages(own, full, wide, sems):
    win, head, core, cell, base = position()
    rows = own.shape[0]
    half, part = rows // 2, rows // 8
    mine = pl.multiple_of(core * half + cell * part, 16)
    near = pl.multiple_of(core * half, 16)

    def over_head(d):
        view = shard_view(full, wide, head, mine, part)
        return remote(
            own.at[pl.ds(mine, part), :], view, sems.at[0, d], sems.at[1, d], win, (head + d + 1) % 4
        )

    def over_cell(d, c):
        view = shard_view(full, wide, (head + 3 - d) % 4, mine, part)
        peer = base + 2 * ((cell + c + 1) % 4) + core
        return remote(view, view, sems.at[2 + c, d], sems.at[5 + c, d], peer, head)

    def over_core(d):
        view = shard_view(full, wide, (head + 3 - d) % 4, near, half)
        return remote(view, view, sems.at[8, d], sems.at[9, d], win + 1 - 2 * core, head)

    local = pltpu.make_async_copy(own, shard_view(full, wide, head, 0, rows), sems.at[10, 0])

    def first():
        local.start()
        for d in range(3):
            over_head(d).start()

    def second():
        for d in range(3):
            over_head(d).wait_recv()
            for c in range(3):
                over_cell(d, c).start()

    def third():
        for d in range(3):
            for c in range(3):
                over_cell(d, c).wait_recv()
            over_core(d).start()

    def last():
        for d in range(3):
            over_core(d).wait_recv()
        local.wait()
        for d in range(3):
            over_head(d).wait_send()
            for c in range(3):
                over_cell(d, c).wait_send()
            over_core(d).wait_send()

    return first, second, third, last


def reduce_stages(buf, from_core, from_cell, from_upper, from_head, final, sems):
    win, head, core, cell, base = position()
    rows = buf.shape[0]
    half, part = rows // 2, rows // 8
    near = pl.multiple_of(core * half, 16)
    far = pl.multiple_of((1 - core) * half, 16)
    mine = pl.multiple_of(core * half + cell * part, 16)
    other = win + 1 - 2 * core
    own = pl.ds(mine, part)

    def lanes(h):
        return pl.ds(pl.multiple_of(h * D, LANES), D)

    def to_core():
        return remote(
            buf.at[pl.ds(far, half), :], from_core, sems.at[0, 0], sems.at[1, 0], other, head
        )

    def to_cell(c):
        peer = (cell + c + 1) % 4
        start = pl.multiple_of(core * half + peer * part, 16)
        return remote(
            buf.at[pl.ds(start, part), :],
            from_cell.at[c],
            sems.at[0, 1 + c],
            sems.at[1, 1 + c],
            base + 2 * peer + core,
            head,
        )

    def to_upper(b):
        peer = win + (8 << b) - 2 * (8 << b) * (win // (8 << b) % 2)
        return remote(
            buf.at[own, :], from_upper.at[b], sems.at[0, 14 + b], sems.at[1, 14 + b], peer, head
        )

    def to_head(d):
        peer = (head + d + 1) % 4
        return remote(
            buf.at[own, lanes(peer)],
            from_head.at[d],
            sems.at[0, 4 + d],
            sems.at[1, 4 + d],
            win,
            peer,
        )

    def back_cell(c):
        peer = (cell + c + 1) % 4
        return remote(
            final.at[own, :],
            final.at[own, :],
            sems.at[0, 7 + c],
            sems.at[1, 7 + c],
            base + 2 * peer + core,
            head,
        )

    def back_core():
        view = final.at[pl.ds(near, half), :]
        return remote(view, view, sems.at[0, 10], sems.at[1, 10], other, head)

    def first():
        to_core().start()

    def second():
        to_core().wait_recv()
        for k in range(4):
            start = pl.multiple_of(core * half + k * part, 16)
            block = pl.ds(start, part)
            total = buf[block, :].astype(F32) + from_core[k * part : k * part + part].astype(F32)
            buf[block, :] = total.astype(BF16)
        for c in range(3):
            to_cell(c).start()

    def third():
        for c in range(3):
            to_cell(c).wait_recv()
        total = buf[own, :].astype(F32)
        for c in range(3):
            total = total + from_cell[c].astype(F32)
        buf[own, :] = total.astype(BF16)
        for b in range(from_upper.shape[0] - 1):
            to_upper(b).start()
            to_upper(b).wait()
            buf[own, :] = (buf[own, :].astype(F32) + from_upper[b].astype(F32)).astype(BF16)
        for d in range(3):
            to_head(d).start()

    def fourth():
        for d in range(3):
            to_head(d).wait_recv()
        total = buf[own, lanes(head)].astype(F32)
        for d in range(3):
            total = total + from_head[d].astype(F32)
        final[own, :] = total.astype(BF16)
        for c in range(3):
            back_cell(c).start()

    def fifth():
        for c in range(3):
            back_cell(c).wait_recv()
        back_core().start()

    def last():
        back_core().wait_recv()
        to_core().wait_send()
        for c in range(3):
            to_cell(c).wait_send()
            to_head(c).wait_send()
            back_cell(c).wait_send()
        back_core().wait_send()

    return first, second, third, fourth, fifth, last


def small_stages(buf, from_core, cells, from_upper, heads, final, sems):
    win, head, core, cell, base = position()
    other = win + 1 - 2 * core

    def lanes(h):
        return pl.ds(pl.multiple_of(h * D, LANES), D)

    def to_core():
        return remote(buf, from_core, sems.at[0, 0], sems.at[1, 0], other, head)

    def to_cell(c):
        view = cells.at[cell]
        peer = base + 2 * ((cell + c + 1) % 4) + core
        return remote(view, view, sems.at[0, 1 + c], sems.at[1, 1 + c], peer, head)

    def to_upper(b):
        peer = win + (8 << b) - 2 * (8 << b) * (win // (8 << b) % 2)
        return remote(buf, from_upper.at[b], sems.at[0, 14 + b], sems.at[1, 14 + b], peer, head)

    def to_head(d):
        peer = (head + d + 1) % 4
        return remote(
            buf.at[:, lanes(peer)], heads.at[head], sems.at[0, 4 + d], sems.at[1, 4 + d], win, peer
        )

    def first():
        to_core().start()

    def second():
        to_core().wait()
        cells[cell] = buf[...] + from_core[...]
        for c in range(3):
            to_cell(c).start()

    def third():
        for c in range(3):
            to_cell(c).wait()
        buf[...] = (cells[0] + cells[1]) + (cells[2] + cells[3])
        for b in range(from_upper.shape[0] - 1):
            to_upper(b).start()
            to_upper(b).wait()
            buf[...] = buf[...] + from_upper[b]
        heads[head] = buf[:, lanes(head)]
        for d in range(3):
            to_head(d).start()

    def last():
        for d in range(3):
            to_head(d).wait()
        final[...] = (heads[0] + heads[1]) + (heads[2] + heads[3])

    return first, second, third, last


def clip_rows(c, count=CLIP):
    return pl.ds(pl.multiple_of(c * count, count), count)


def block_kernel(
    clips,
    frames_ref,
    tok_hbm,
    og_hbm,
    qown_ref,
    pown_ref,
    aown_ref,
    bown_ref,
    sown_ref,
    rowp_ref,
    out_hbm,
    din_hbm,
    early_ref,
    late_ref,
    esmall_ref,
    lsmall_ref,
    norm_ref,
    tok_ref,
    og_ref,
    out_ref,
    dmid_ref,
    qkv_ref,
    probs_ref,
    att_ref,
    wqkv_ref,
    wproj_ref,
    w1_ref,
    w2_ref,
    small_ref,
    bqkv_ref,
    b1_ref,
    bias_ref,
    time_ref,
    g1_ref,
    g2_ref,
    gp_ref,
    rows_ref,
    gb_ref,
    gqv_ref,
    tacc_ref,
    ebuf,
    lbuf,
    esbuf,
    lsbuf,
    core_e,
    core_l,
    core_es,
    core_ls,
    cell_e,
    cell_l,
    cell_es,
    cell_ls,
    up_e,
    up_l,
    up_es,
    up_ls,
    head_e,
    head_l,
    head_es,
    head_ls,
    efinal,
    lfinal,
    nslots,
    wsems,
    ssems,
    rsems,
    nsems,
    osems,
):
    win, head, core, cell, base = position()
    load_tok = pltpu.make_async_copy(tok_hbm, tok_ref, osems.at[2, 0])
    load_og = pltpu.make_async_copy(og_hbm, og_ref, osems.at[2, 1])
    load_tok.start()
    load_og.start()
    greet()
    small = [
        remote(sown_ref, small_ref.at[head], ssems.at[0, d], ssems.at[1, d], win, (head + d + 1) % 4)
        for d in range(3)
    ]
    own_small = pltpu.make_async_copy(sown_ref, small_ref.at[head], ssems.at[2, 0])
    gq_w = gather_stages(qown_ref, wqkv_ref, True, wsems.at[0])
    others = [
        gather_stages(own, full, wide, wsems.at[1 + i])
        for i, (own, full, wide) in enumerate(
            ((pown_ref, wproj_ref, False), (aown_ref, w1_ref, True), (bown_ref, w2_ref, False))
        )
    ]
    gq_w[0]()
    own_small.start()
    for copy in small:
        copy.start()
    for wt in range(2):
        for wf in range(2):
            time_ref[wt * 2 + wf] = key_times(wt, wf)
    for ref in (g1_ref, g2_ref, gp_ref, rows_ref, gb_ref, gqv_ref, tacc_ref, esbuf, lsbuf):
        ref[...] = jnp.zeros_like(ref)
    gq_w[1]()
    own_small.wait()
    for copy in small:
        copy.wait()
    for g in range(4):
        bqkv_ref[0:1, g * D : g * D + LANES] = small_ref[g, 0:1, :LANES]
        bqkv_ref[0:1, g * D + LANES : g * D + 2 * LANES] = jnp.zeros((1, LANES), F32)
        bqkv_ref[0:1, g * D + 2 * LANES : g * D + D] = small_ref[g, 0:1, LANES : 2 * LANES]
        b1_ref[0:1, g * D : g * D + D] = small_ref[g, 5:6, :]
    build_bias(small_ref, bias_ref)
    gq_w[2]()
    for k in others:
        k[0]()
    gq_w[3]()
    load_tok.wait()

    def attend(c, carry):
        rows = clip_rows(c)
        frames = frames_ref[c]
        x = to_windows(tok_ref[rows, :].astype(F32))
        n1, _ = normalize(x)
        n1 = (n1 * rowp_ref[0:1] + rowp_ref[1:2]).astype(BF16)
        for part in range(3):
            cols = slice(part * 512, part * 512 + 512)
            y = nn(n1, wqkv_ref[:, cols]) + bqkv_ref[0:1, cols]
            qkv_ref[rows, cols] = y.astype(BF16)
        masks = head_masks(BF16)
        for w in range(4):
            spots = pl.ds(pl.multiple_of(c * CLIP + w * SPOT, SPOT), SPOT)
            for g in range(GROUPS):
                q = qkv_ref[spots, g * D : g * D + LANES]
                k = qkv_ref[spots, g * D + LANES : g * D + 2 * LANES]
                v = qkv_ref[spots, g * D + 2 * LANES : g * D + D]
                s = nt(k, stack_heads(q, masks)) * SCALE + bias_ref[g]
                s = jnp.where(time_ref[w] < frames, s, MASKED)
                e = jnp.exp(s - jnp.max(s, axis=0, keepdims=True))
                p = (e * (1.0 / jnp.sum(e, axis=0, keepdims=True))).astype(BF16)
                probs_ref[c, w, g] = p
                o = pick_heads(tn(p, v))
                att_ref[spots, g * LANES : g * LANES + LANES] = o.astype(BF16)
        return carry

    def feed(c, carry):
        rows = clip_rows(c)
        x = to_windows(tok_ref[rows, :].astype(F32))
        og = to_windows(og_ref[rows, :].astype(F32))
        att = att_ref[rows, :]
        middle = x + nn(att, wproj_ref[...]) + rowp_ref[4:5]
        nrm, inv = normalize(middle)
        n2 = (nrm * rowp_ref[2:3] + rowp_ref[3:4]).astype(BF16)
        n2t = n2.T
        ogb = og.astype(BF16)
        ogt = ogb.T
        ffn = None
        dn2 = None
        for j in range(FF // CHUNK):
            cols = slice(j * CHUNK, j * CHUNK + CHUNK)
            u = nn(n2, w1_ref[:, cols]) + b1_ref[0:1, cols]
            phi, dens = gelu_parts(u)
            hid = (u * phi).astype(BF16)
            du = ((phi + u * dens) * nt(ogb, w2_ref[cols, :])).astype(BF16)
            gb_ref[:, cols] += fold(du.astype(F32))
            g1_ref[:, cols] += nn(n2t, du)
            g2_ref[:, cols] += nn(ogt, hid)
            a = nn(hid, w2_ref[cols, :])
            b = nt(du, w1_ref[:, cols])
            ffn = a if ffn is None else ffn + a
            dn2 = b if dn2 is None else dn2 + b
        out_ref[rows, :] = from_windows(middle + ffn + rowp_ref[5:6])
        pltpu.make_async_copy(out_ref.at[rows, :], out_hbm.at[rows, :], osems.at[0, c]).start()
        dmid = og + norm_back(dn2, nrm, inv, rowp_ref[2:3])
        dmid_ref[rows, :] = dmid
        dbr = dmid.astype(BF16)
        rows_ref[2] += fold(dn2 * nrm)
        rows_ref[3] += fold(dn2)
        rows_ref[4] += fold(dbr.astype(F32))
        rows_ref[5] += fold(og)
        attt = att.T
        for g in range(GROUPS):
            gp_ref[:, g * D : g * D + D] += nn(attt[g * LANES : g * LANES + LANES], dbr)
        att_ref[rows, :] = nt(dbr, wproj_ref[...]).astype(BF16)
        return carry

    def attend_back(c, carry):
        rows = clip_rows(c)
        frames = frames_ref[c]
        masks = head_masks(BF16)
        for g in range(GROUPS):
            tacc = None
            for w in range(4):
                spots = pl.ds(pl.multiple_of(c * CLIP + w * SPOT, SPOT), SPOT)
                cq = slice(g * D, g * D + LANES)
                ck = slice(g * D + LANES, g * D + 2 * LANES)
                cv = slice(g * D + 2 * LANES, g * D + D)
                q = qkv_ref[spots, cq]
                k = qkv_ref[spots, ck]
                v = qkv_ref[spots, cv]
                do = stack_heads(att_ref[spots, g * LANES : g * LANES + LANES], masks)
                p = probs_ref[c, w, g]
                pf = p.astype(F32)
                dp = nt(v, do)
                inner = jnp.sum(pf * dp, axis=0, keepdims=True)
                ds = jnp.where(time_ref[w] < frames, pf * (dp - inner), 0.0)
                tacc = ds if tacc is None else tacc + ds
                ds = ds.astype(BF16)
                qkv_ref[spots, cq] = (pick_heads(tn(ds, k)) * SCALE).astype(BF16)
                qkv_ref[spots, ck] = (nn(ds, stack_heads(q, masks)) * SCALE).astype(BF16)
                qkv_ref[spots, cv] = nn(p, do).astype(BF16)
            tacc_ref[g] += tacc
        gqv_ref[...] += fold(qkv_ref[rows, :].astype(F32))
        n, _ = normalize(to_windows(tok_ref[rows, :].astype(F32)))
        n1t = (n * rowp_ref[0:1] + rowp_ref[1:2]).astype(BF16).T
        g1_ref[...] += nn(n1t, qkv_ref[rows, :])
        return carry

    def entry_back(c, carry):
        rows = clip_rows(c)
        n, inv = normalize(to_windows(tok_ref[rows, :].astype(F32)))
        dn1 = nt(qkv_ref[rows, :], wqkv_ref[...])
        rows_ref[0] += fold(dn1 * n)
        rows_ref[1] += fold(dn1)
        din = dmid_ref[rows, :] + norm_back(dn1, n, inv, rowp_ref[0:1])
        dmid_ref[rows, :] = from_windows(din)
        pltpu.make_async_copy(dmid_ref.at[rows, :], din_hbm.at[rows, :], osems.at[1, c]).start()
        return carry

    def span(share):
        return clips * share // 8

    lax.fori_loop(0, span(2), attend, 0)
    for k in others:
        k[1]()
    lax.fori_loop(span(2), span(5), attend, 0)
    for k in others:
        k[2]()
    lax.fori_loop(span(5), span(8), attend, 0)
    for k in others:
        k[3]()
    load_og.wait()
    lax.fori_loop(0, clips, feed, 0)

    early = reduce_stages(ebuf, core_e, cell_e, up_e, head_e, efinal, rsems.at[0])
    early_small = small_stages(esbuf, core_es, cell_es, up_es, head_es, esmall_ref, rsems.at[1])
    late = reduce_stages(lbuf, core_l, cell_l, up_l, head_l, lfinal, rsems.at[2])
    late_small = small_stages(lsbuf, core_ls, cell_ls, up_ls, head_ls, lsmall_ref, rsems.at[3])
    ebuf[0:D, :] = g1_ref[...].astype(BF16)
    ebuf[D : 2 * D, :] = g2_ref[...].astype(BF16)
    ebuf[2 * D : 2 * D + LANES, :] = gp_ref[...].astype(BF16)
    early[0]()
    g1_ref[...] = jnp.zeros_like(g1_ref)
    esbuf[0:1, :] = jnp.sum(gb_ref[...], axis=0, keepdims=True)
    for r in range(4):
        line = jnp.sum(rows_ref[2 + r], axis=0, keepdims=True)
        for g in range(GROUPS):
            esbuf[1 + r : 2 + r, g * D : g * D + D] = line
    early_small[0]()
    lax.fori_loop(0, span(1), attend_back, 0)
    early[1]()
    early_small[1]()
    lax.fori_loop(span(1), span(4), attend_back, 0)
    early[2]()
    early_small[2]()
    lax.fori_loop(span(4), span(6), attend_back, 0)
    early[3]()
    early_small[3]()
    lax.fori_loop(span(6), span(7), attend_back, 0)
    early[4]()
    lax.fori_loop(span(7), span(8), attend_back, 0)
    lbuf[...] = g1_ref[...].astype(BF16)
    late[0]()
    for g in range(GROUPS):
        cols = slice(g * D, g * D + LANES)
        lsbuf[0:1, cols] = jnp.sum(gqv_ref[:, cols], axis=0, keepdims=True)
        cols = slice(g * D + 2 * LANES, g * D + D)
        lsbuf[0:1, cols] = jnp.sum(gqv_ref[:, cols], axis=0, keepdims=True)
    fold_table(tacc_ref, lsbuf)
    late[1]()
    early[5]()
    lax.fori_loop(0, span(6), entry_back, 0)
    late[2]()
    lax.fori_loop(span(6), span(8), entry_back, 0)
    for r in range(2):
        line = jnp.sum(rows_ref[r], axis=0, keepdims=True)
        for g in range(GROUPS):
            lsbuf[4 + r : 5 + r, g * D : g * D + D] = line
    late_small[0]()
    late[3]()
    late_small[1]()
    late[4]()
    late_small[2]()
    late[5]()
    late_small[3]()
    early_ref[...] = efinal[...]
    late_ref[...] = lfinal[...]
    square = jnp.zeros((8, D), F32)
    for ref in (efinal, lfinal):
        value = ref[...].astype(F32)
        square = square + fold(value * value)
    es, ls = esmall_ref[...], lsmall_ref[...]
    row = iota((8, D), 0)
    square = square + jnp.where(row < 1, es * es, 0.0) + jnp.where(row < 4, ls * ls, 0.0)
    common = jnp.where((row >= 1) & (row < 5), es * es, 0.0)
    common = common + jnp.where((row >= 4) & (row < 6), ls * ls, 0.0)
    nslots[head] = jnp.broadcast_to(jnp.sum(square, keepdims=True), (8, LANES))
    sends = [
        remote(
            nslots.at[head], nslots.at[head], nsems.at[0, d], nsems.at[1, d], win, (head + d + 1) % 4
        )
        for d in range(3)
    ]
    for copy in sends:
        copy.start()
    for copy in sends:
        copy.wait()
    total = (nslots[0] + nslots[1]) + (nslots[2] + nslots[3])
    norm_ref[...] = jnp.sqrt(total + jnp.sum(common, keepdims=True))

    def finish(c, carry):
        rows = clip_rows(c)
        pltpu.make_async_copy(out_ref.at[rows, :], out_hbm.at[rows, :], osems.at[0, c]).wait()
        pltpu.make_async_copy(dmid_ref.at[rows, :], din_hbm.at[rows, :], osems.at[1, c]).wait()
        return carry

    lax.fori_loop(0, clips, finish, 0)


def fold_table(tacc_ref, lsbuf):
    row = iota((256, 256), 0)
    lane = iota((256, 256), 1)
    spot = row % SPOT
    base = 112 - (spot // WIN * (2 * WIN - 1) + spot % WIN)
    for h in range(PER):
        own = jnp.where((lane == base) & (row // SPOT == h), 1.0, 0.0).astype(F32).astype(BF16)
        for g in range(GROUPS):
            spread = None
            for part in split_three(tacc_ref[g]):
                term = nn(part, own)
                spread = term if spread is None else spread + term
            total = None
            for a in range(WIN):
                piece = pltpu.roll(
                    spread[a * 8 : a * 8 + 8], 15 * a, axis=1, stride=1, stride_axis=0
                )
                total = piece if total is None else total + piece
            line = jnp.sum(total, axis=0, keepdims=True)
            for half in range(2):
                at = h * 256 + half * LANES
                lsbuf[1 + at // D : 2 + at // D, g * D + at % D : g * D + at % D + LANES] = line[
                    :, half * LANES : half * LANES + LANES
                ]


def block(frames, tok, og, qown, pown, aown, bown, sown, rowp):
    rows = tok.shape[0]
    clips = rows // CLIP
    upper = max(lax.axis_size("win") // 8, 1).bit_length() - 1
    shape = jax.ShapeDtypeStruct
    sems = pltpu.SemaphoreType.DMA
    vmem = pltpu.VMEM
    spec = pl.BlockSpec
    inside = lambda: spec(memory_space=vmem)
    outside = lambda: spec(memory_space=pl.ANY)
    early, late = 2 * D + LANES, D
    return pl.pallas_call(
        partial(block_kernel, clips),
        in_specs=[spec(memory_space=pltpu.SMEM), outside(), outside()] + [inside()] * 6,
        out_specs=[outside(), outside()] + [inside()] * 5,
        out_shape=[
            shape((rows, D), F32),
            shape((rows, D), F32),
            shape((early, D), BF16),
            shape((late, D), BF16),
            shape((8, D), F32),
            shape((8, D), F32),
            shape((8, LANES), F32),
        ],
        scratch_shapes=[
            vmem((rows, D), BF16),
            vmem((rows, D), BF16),
            vmem((rows, D), F32),
            vmem((rows, D), F32),
            vmem((rows, 1536), BF16),
            vmem((clips, 4, GROUPS, SPOT, PER * SPOT), BF16),
            vmem((rows, 512), BF16),
            vmem((D, 1536), BF16),
            vmem((512, D), BF16),
            vmem((D, FF), BF16),
            vmem((FF, D), BF16),
            vmem((GROUPS, 8, D), F32),
            vmem((8, 1536), F32),
            vmem((8, FF), F32),
            vmem((GROUPS, SPOT, PER * SPOT), F32),
            vmem((4, SPOT, PER * SPOT), jnp.int32),
            vmem((D, FF), F32),
            vmem((D, FF), F32),
            vmem((LANES, 1536), F32),
            vmem((6, 8, D), F32),
            vmem((8, FF), F32),
            vmem((8, 1536), F32),
            vmem((GROUPS, SPOT, PER * SPOT), F32),
            vmem((early, 1536), BF16),
            vmem((late, 1536), BF16),
            vmem((8, 1536), F32),
            vmem((8, 1536), F32),
            vmem((early // 2, 1536), BF16),
            vmem((late // 2, 1536), BF16),
            vmem((8, 1536), F32),
            vmem((8, 1536), F32),
            vmem((3, early // 8, 1536), BF16),
            vmem((3, late // 8, 1536), BF16),
            vmem((4, 8, 1536), F32),
            vmem((4, 8, 1536), F32),
            vmem((upper + 1, early // 8, 1536), BF16),
            vmem((upper + 1, late // 8, 1536), BF16),
            vmem((upper + 1, 8, 1536), F32),
            vmem((upper + 1, 8, 1536), F32),
            vmem((3, early // 8, D), BF16),
            vmem((3, late // 8, D), BF16),
            vmem((4, 8, D), F32),
            vmem((4, 8, D), F32),
            vmem((early, D), BF16),
            vmem((late, D), BF16),
            vmem((4, 8, LANES), F32),
            sems((4, 11, 3)),
            sems((3, 3)),
            sems((4, 2, 14 + upper)),
            sems((2, 3)),
            sems((3, max(clips, 2))),
        ],
        compiler_params=pltpu.CompilerParams(
            vmem_limit_bytes=VMEM_LIMIT, collective_id=0, has_side_effects=True
        ),
    )(frames, tok, og, qown, pown, aown, bown, sown, rowp)


def adam_step(weight, gradient, moment, second, factor, rate):
    clipped = gradient * factor
    moment_new = BETA_ONE * moment + (1.0 - BETA_ONE) * clipped
    second_new = BETA_TWO * second + (1.0 - BETA_TWO) * clipped * clipped
    moment_hat = moment_new / (1.0 - BETA_ONE**STEP)
    second_hat = second_new / (1.0 - BETA_TWO**STEP)
    master = weight - rate * (
        moment_hat / (jnp.sqrt(second_hat) + ADAM_EPS) + WEIGHT_DECAY * weight
    )
    return (gradient, moment_new, second_new, master)


def shards(
    tokens,
    out_grad,
    clip_frames,
    qkv_weight,
    qv_bias,
    rel_table,
    proj_weight,
    fc1_weight,
    fc1_bias,
    fc2_weight,
    row_params,
    qkv_first,
    qkv_second,
    qvb_first,
    qvb_second,
    table_first,
    table_second,
    proj_first,
    proj_second,
    fc1_first,
    fc1_second,
    fc1b_first,
    fc1b_second,
    fc2_first,
    fc2_second,
    rows_first,
    rows_second,
):
    clips = tokens.shape[0] // CLIP
    local = rel_table.shape[1] * HDIM
    offsets = rel_table.shape[0]
    frames = lax.dynamic_slice(clip_frames, (lax.axis_index("head") * clips,), (clips,))
    pad = LANES - local
    qown = jnp.pad(qkv_weight.astype(BF16), ((0, 0), (0, 0), (0, pad))).reshape(D, D)
    pown = jnp.pad(proj_weight.astype(BF16), ((0, pad), (0, 0)))
    aown, bown = fc1_weight.astype(BF16), fc2_weight.astype(BF16)
    bias_row = jnp.pad(qv_bias, ((0, 1), (0, pad))).reshape(1, D)
    sown = jnp.concatenate(
        [
            bias_row,
            jnp.pad(rel_table.T, ((0, 0), (0, D - offsets))),
            fc1_bias[None],
            jnp.zeros((2, D), F32),
        ]
    )
    output, input_grad, early, late, esmall, lsmall, norm = block(
        frames, tokens, out_grad, qown, pown, aown, bown, sown, row_params
    )
    early, late = early.astype(F32), late.astype(F32)
    grad_norm = norm[0, 0]
    factor = jnp.minimum(1.0, CLIP_LIMIT / (grad_norm + 1e-06))
    table = lsmall[1:4].reshape(-1)[: PER * 256].reshape(PER, 256)
    gradients = (
        late.reshape(D, 3, LANES)[..., :local],
        lsmall[0].reshape(3, LANES)[::2, :local],
        table[:, :offsets][:, ::-1].T,
        early[2 * D : 2 * D + local],
        early[:D],
        esmall[0],
        early[D : 2 * D].T,
        jnp.concatenate([lsmall[4:6], esmall[1:5]]),
    )
    weights = (
        qkv_weight,
        qv_bias,
        rel_table,
        proj_weight,
        fc1_weight,
        fc1_bias,
        fc2_weight,
        row_params,
    )
    firsts = (
        qkv_first,
        qvb_first,
        table_first,
        proj_first,
        fc1_first,
        fc1b_first,
        fc2_first,
        rows_first,
    )
    seconds = (
        qkv_second,
        qvb_second,
        table_second,
        proj_second,
        fc1_second,
        fc1b_second,
        fc2_second,
        rows_second,
    )
    rates = (
        LEARN_RATE,
        LEARN_RATE,
        ROW_RATE,
        LEARN_RATE,
        LEARN_RATE,
        LEARN_RATE,
        LEARN_RATE,
        ROW_RATE,
    )
    updated = []
    for weight, gradient, moment, second, rate in zip(weights, gradients, firsts, seconds, rates):
        updated.extend(adam_step(weight, gradient, moment, second, factor, rate))
    return (output, input_grad, grad_norm, *updated)


def solution(mesh):
    rows = P(("win", "head"), None)
    last3, last2, first2, first1 = P(None, None, "head"), P(None, "head"), P("head", None), P("head")
    each = (last3, last2, last2, first2, last2, first1, first2, P())
    return jax.shard_map(
        shards,
        mesh=mesh,
        in_specs=(rows, rows, P("win")) + each + tuple(s for s in each for _ in range(2)),
        out_specs=(rows, rows, P()) + tuple(s for s in each for _ in range(4)),
        check_vma=False,
    )
```

```python
from functools import partial

import jax
import jax.numpy as jnp
from jax import lax
from jax.experimental import pallas as pl
from jax.experimental.pallas import tpu as pltpu
from jax.sharding import PartitionSpec as P

D = 384
HDIM = 24
HEADS = 16
GROUPS = 4
PER = 4
LANES = 128
FF = 1536
GRID = 16
WIN = 8
CLIP = GRID * GRID
SPOT = WIN * WIN
SHIFT = 4
STEP = 10
CHUNK = 768
PAIR = 2 * CLIP

NORM_EPS = 1e-05
MASKED = -1000000000.0
CLIP_LIMIT = 1.0
LEARN_RATE = 0.1
ROW_RATE = 0.5
BETA_ONE = 0.9
BETA_TWO = 0.999
ADAM_EPS = 1e-08
WEIGHT_DECAY = 0.01
SCALE = HDIM ** (-0.5)
F32 = jnp.float32
BF16 = jnp.bfloat16
VMEM_LIMIT = 60 * 1024 * 1024


def nn(a, b):
    return lax.dot_general(a, b, (((1,), (0,)), ((), ())), preferred_element_type=F32)


def nt(a, b):
    return lax.dot_general(a, b, (((1,), (1,)), ((), ())), preferred_element_type=F32)


def tn(a, b):
    return lax.dot_general(a, b, (((0,), (0,)), ((), ())), preferred_element_type=F32)


def iota(shape, axis):
    return lax.broadcasted_iota(jnp.int32, shape, axis)


def fold(x):
    return jnp.sum(x.reshape(x.shape[0] // 8, 8, x.shape[1]), axis=0)


def normalize(x):
    center = x - jnp.mean(x, axis=-1, keepdims=True)
    spread = jnp.mean(center * center, axis=-1, keepdims=True)
    inverse = lax.rsqrt(spread + NORM_EPS)
    return center * inverse, inverse


def norm_back(e, n, inverse, gain):
    q = e * gain
    return inverse * (
        q - jnp.mean(q, axis=-1, keepdims=True) - n * jnp.mean(q * n, axis=-1, keepdims=True)
    )


def to_windows(x):
    low = iota((8, x.shape[1]), 0) < 4
    first, second = [], []
    for t in range(GRID):
        a = x[16 * t : 16 * t + 8]
        b = x[16 * t + 8 : 16 * t + 16]
        first.append(pltpu.roll(jnp.where(low, b, a), 4, axis=0))
        second.append(pltpu.roll(jnp.where(low, a, b), 4, axis=0))
    pieces = []
    for wt in range(2):
        for side in (first, second):
            for a in range(WIN):
                pieces.append(side[(wt * WIN + a + SHIFT) % GRID])
    return jnp.concatenate(pieces, axis=0)


def from_windows(y):
    low = iota((8, y.shape[1]), 0) < 4
    pieces = []
    for t in range(GRID):
        rolled = (t - SHIFT) % GRID
        base = (rolled // WIN) * 128 + (rolled % WIN) * 8
        u = pltpu.roll(y[base : base + 8], 4, axis=0)
        v = pltpu.roll(y[base + 64 : base + 72], 4, axis=0)
        pieces.append(jnp.where(low, v, u))
        pieces.append(jnp.where(low, u, v))
    return jnp.concatenate(pieces, axis=0)


def head_masks(dtype):
    lane = iota((16, LANES), 1) // HDIM
    return [jnp.where(lane == h, 1.0, 0.0).astype(F32).astype(dtype) for h in range(PER)]


def stack_heads(x, masks):
    tiles = x.reshape(SPOT // 16, 16, LANES)
    return jnp.concatenate([(tiles * m[None]).reshape(SPOT, LANES) for m in masks], axis=0)


def pick_heads(r):
    lane = iota((SPOT, LANES), 1)
    out = r[3 * SPOT :]
    for h in (2, 1, 0):
        out = jnp.where(lane < (h + 1) * HDIM, r[h * SPOT : (h + 1) * SPOT], out)
    return out


def key_times(wt, wf):
    j = iota((SPOT, PER * SPOT), 0)
    i = iota((SPOT, PER * SPOT), 1) % SPOT
    time = (wt * WIN + j // WIN + SHIFT) % GRID
    same = j >= 0
    if wt:
        same = same & ((j // WIN < 4) == (i // WIN < 4))
    if wf:
        same = same & ((j % WIN < 4) == (i % WIN < 4))
    return jnp.where(same, time, 99)


def split_three(x):
    one = x.astype(BF16)
    rest = x - one.astype(F32)
    two = rest.astype(BF16)
    three = (rest - two.astype(F32)).astype(BF16)
    return one, two, three


def build_bias(table_ref, bias_ref):
    row = iota((256, 256), 0)
    lane = iota((256, 256), 1)
    spot = lane % SPOT
    base = spot // WIN * (2 * WIN - 1) + spot % WIN
    for g in range(GROUPS):
        total = None
        for h in range(PER):
            own = jnp.where((row == base) & (lane // SPOT == h), 1.0, 0.0).astype(F32).astype(BF16)
            line = jnp.broadcast_to(table_ref[g, 1 + h : 2 + h, :256], (8, 256))
            spread = jnp.concatenate(
                [
                    pltpu.roll(line, (15 * a + 144) % 256, axis=1, stride=1, stride_axis=0)
                    for a in range(WIN)
                ],
                axis=0,
            )
            for part in split_three(spread):
                term = nn(part, own)
                total = term if total is None else total + term
        bias_ref[g] = total


def gelu_parts(u):
    mag = jnp.abs(u) * (0.5**0.5)
    t = 1.0 / (1.0 + 0.3275911 * mag)
    bell = jnp.exp(-0.5 * (u * u))
    poly = t * (
        0.127414796
        + t * (-0.142248368 + t * (0.7107068705 + t * (-0.7265760135 + t * 0.5307027145)))
    )
    tail = poly * bell
    return jnp.where(u >= 0.0, 1.0 - tail, tail), bell * 0.3989422804014327


def place(win, head):
    return {"win": win, "head": head}


def remote(src, dst, send, recv, win, head):
    return pltpu.make_async_remote_copy(
        src_ref=src,
        dst_ref=dst,
        send_sem=send,
        recv_sem=recv,
        device_id=place(win, head),
        device_id_type=pl.DeviceIdType.MESH,
    )


def position():
    win, head = lax.axis_index("win"), lax.axis_index("head")
    core, cell = win % 2, (win // 2) % 4
    return win, head, core, cell, win - core - 2 * cell


def greet():
    win, head, core, cell, base = position()
    barrier = pltpu.get_barrier_semaphore()
    peers = [(win, (head + d) % 4) for d in (1, 2, 3)]
    peers += [(base + 2 * ((cell + d) % 4) + core, head) for d in (1, 2, 3)]
    peers += [(win + 1 - 2 * core, head)]
    for w, h in peers:
        pl.semaphore_signal(barrier, inc=1, device_id=place(w, h), device_id_type=pl.DeviceIdType.MESH)
    pl.semaphore_wait(barrier, len(peers))


def shard_view(ref, wide, head, start, count):
    if wide:
        return ref.at[pl.ds(start, count), pl.ds(pl.multiple_of(head * D, LANES), D)]
    rows = ref.shape[0] // 4
    return ref.at[pl.ds(pl.multiple_of(head * rows + start, 16), count), :]


def gather_stages(rows, full, wide, sems):
    win, head, core, cell, base = position()
    half, part = rows // 2, rows // 8
    mine = pl.multiple_of(core * half + cell * part, 16)
    near = pl.multiple_of(core * half, 16)

    def over_head(d):
        view = shard_view(full, wide, head, mine, part)
        return remote(view, view, sems.at[0, d], sems.at[1, d], win, (head + d + 1) % 4)

    def over_cell(d, c):
        view = shard_view(full, wide, (head + 3 - d) % 4, mine, part)
        peer = base + 2 * ((cell + c + 1) % 4) + core
        return remote(view, view, sems.at[2 + c, d], sems.at[5 + c, d], peer, head)

    def over_core(d):
        view = shard_view(full, wide, (head + 3 - d) % 4, near, half)
        return remote(view, view, sems.at[8, d], sems.at[9, d], win + 1 - 2 * core, head)

    def first():
        for d in range(3):
            over_head(d).start()

    def second():
        for d in range(3):
            over_head(d).wait_recv()
            for c in range(3):
                over_cell(d, c).start()

    def third():
        for d in range(3):
            for c in range(3):
                over_cell(d, c).wait_recv()
            over_core(d).start()

    def last():
        for d in range(3):
            over_core(d).wait_recv()
        for d in range(3):
            over_head(d).wait_send()
            for c in range(3):
                over_cell(d, c).wait_send()
            over_core(d).wait_send()

    return first, second, third, last


def reduce_stages(buf, from_core, from_cell, from_upper, from_head, final, sems):
    win, head, core, cell, base = position()
    rows = buf.shape[0]
    half, part = rows // 2, rows // 8
    near = pl.multiple_of(core * half, 16)
    far = pl.multiple_of((1 - core) * half, 16)
    mine = pl.multiple_of(core * half + cell * part, 16)
    other = win + 1 - 2 * core
    own = pl.ds(mine, part)

    def lanes(h):
        return pl.ds(pl.multiple_of(h * D, LANES), D)

    def to_core():
        return remote(
            buf.at[pl.ds(far, half), :], from_core, sems.at[0, 0], sems.at[1, 0], other, head
        )

    def to_cell(c):
        peer = (cell + c + 1) % 4
        start = pl.multiple_of(core * half + peer * part, 16)
        return remote(
            buf.at[pl.ds(start, part), :],
            from_cell.at[c],
            sems.at[0, 1 + c],
            sems.at[1, 1 + c],
            base + 2 * peer + core,
            head,
        )

    def to_upper(b):
        peer = win + (8 << b) - 2 * (8 << b) * (win // (8 << b) % 2)
        return remote(
            buf.at[own, :], from_upper.at[b], sems.at[0, 14 + b], sems.at[1, 14 + b], peer, head
        )

    def to_head(d):
        peer = (head + d + 1) % 4
        return remote(
            buf.at[own, lanes(peer)],
            from_head.at[d],
            sems.at[0, 4 + d],
            sems.at[1, 4 + d],
            win,
            peer,
        )

    def back_cell(c):
        peer = (cell + c + 1) % 4
        return remote(
            final.at[own, :],
            final.at[own, :],
            sems.at[0, 7 + c],
            sems.at[1, 7 + c],
            base + 2 * peer + core,
            head,
        )

    def back_core():
        view = final.at[pl.ds(near, half), :]
        return remote(view, view, sems.at[0, 10], sems.at[1, 10], other, head)

    def first():
        to_core().start()

    def second():
        to_core().wait_recv()
        for k in range(4):
            start = pl.multiple_of(core * half + k * part, 16)
            block = pl.ds(start, part)
            total = buf[block, :].astype(F32) + from_core[k * part : k * part + part].astype(F32)
            buf[block, :] = total.astype(BF16)
        for c in range(3):
            to_cell(c).start()

    def third():
        for c in range(3):
            to_cell(c).wait_recv()
        total = buf[own, :].astype(F32)
        for c in range(3):
            total = total + from_cell[c].astype(F32)
        buf[own, :] = total.astype(BF16)
        for b in range(from_upper.shape[0] - 1):
            to_upper(b).start()
            to_upper(b).wait()
            buf[own, :] = (buf[own, :].astype(F32) + from_upper[b].astype(F32)).astype(BF16)
        for d in range(3):
            to_head(d).start()

    def fourth():
        for d in range(3):
            to_head(d).wait_recv()
        total = buf[own, lanes(head)].astype(F32)
        for d in range(3):
            total = total + from_head[d].astype(F32)
        final[own, :] = total.astype(BF16)
        for c in range(3):
            back_cell(c).start()

    def fifth():
        for c in range(3):
            back_cell(c).wait_recv()
        back_core().start()

    def last():
        back_core().wait_recv()
        to_core().wait_send()
        for c in range(3):
            to_cell(c).wait_send()
            to_head(c).wait_send()
            back_cell(c).wait_send()
        back_core().wait_send()

    return first, second, third, fourth, fifth, last


def small_stages(buf, from_core, cells, from_upper, heads, final, sems):
    win, head, core, cell, base = position()
    other = win + 1 - 2 * core

    def lanes(h):
        return pl.ds(pl.multiple_of(h * D, LANES), D)

    def to_core():
        return remote(buf, from_core, sems.at[0, 0], sems.at[1, 0], other, head)

    def to_cell(c):
        view = cells.at[cell]
        peer = base + 2 * ((cell + c + 1) % 4) + core
        return remote(view, view, sems.at[0, 1 + c], sems.at[1, 1 + c], peer, head)

    def to_upper(b):
        peer = win + (8 << b) - 2 * (8 << b) * (win // (8 << b) % 2)
        return remote(buf, from_upper.at[b], sems.at[0, 14 + b], sems.at[1, 14 + b], peer, head)

    def to_head(d):
        peer = (head + d + 1) % 4
        return remote(
            buf.at[:, lanes(peer)], heads.at[head], sems.at[0, 4 + d], sems.at[1, 4 + d], win, peer
        )

    def first():
        to_core().start()

    def second():
        to_core().wait()
        cells[cell] = buf[...] + from_core[...]
        for c in range(3):
            to_cell(c).start()

    def third():
        for c in range(3):
            to_cell(c).wait()
        buf[...] = (cells[0] + cells[1]) + (cells[2] + cells[3])
        for b in range(from_upper.shape[0] - 1):
            to_upper(b).start()
            to_upper(b).wait()
            buf[...] = buf[...] + from_upper[b]
        heads[head] = buf[:, lanes(head)]
        for d in range(3):
            to_head(d).start()

    def last():
        for d in range(3):
            to_head(d).wait()
        final[...] = (heads[0] + heads[1]) + (heads[2] + heads[3])

    return first, second, third, last


def clip_rows(c, count=CLIP):
    return pl.ds(pl.multiple_of(c * count, count), count)


def block_kernel(
    clips,
    frames_ref,
    tok_hbm,
    og_hbm,
    qraw_ref,
    praw_ref,
    araw_ref,
    braw_ref,
    qvb_ref,
    table_ref,
    fc1b_ref,
    rowp_ref,
    out_hbm,
    din_hbm,
    early_ref,
    late_ref,
    esmall_ref,
    lsmall_ref,
    norm_ref,
    sown_ref,
    turn_ref,
    tok_ref,
    og_ref,
    out_ref,
    dmid_ref,
    n1t_ref,
    n2t_ref,
    ogt_ref,
    qkv_ref,
    dj_ref,
    du_ref,
    probs_ref,
    att_ref,
    wqkv_ref,
    wproj_ref,
    w1_ref,
    w2_ref,
    small_ref,
    bqkv_ref,
    b1_ref,
    bias_ref,
    time_ref,
    rows_ref,
    gb_ref,
    gqv_ref,
    tacc_ref,
    ebuf,
    lbuf,
    esbuf,
    lsbuf,
    core_e,
    core_l,
    core_es,
    core_ls,
    cell_e,
    cell_l,
    cell_es,
    cell_ls,
    up_e,
    up_l,
    up_es,
    up_ls,
    head_e,
    head_l,
    head_es,
    head_ls,
    nslots,
    wsems,
    ssems,
    rsems,
    nsems,
    osems,
):
    win, head, core, cell, base = position()
    first_clip = head * clips

    def enter(c, carry):
        for part in range(2):
            rows = clip_rows(2 * c + part)
            n1, _ = normalize(to_windows(tok_ref[rows, :].astype(F32)))
            n1 = (n1 * rowp_ref[0:1] + rowp_ref[1:2]).astype(BF16)
            att_ref[rows, :D] = n1
            n1t_ref[:, rows] = n1.T
        return carry

    def project(c, carry):
        rows = clip_rows(c, PAIR)
        for part in range(3):
            cols = slice(part * 512, part * 512 + 512)
            y = nn(att_ref[rows, :D], wqkv_ref[:, cols]) + bqkv_ref[0:1, cols]
            qkv_ref[rows, cols] = y.astype(BF16)
        return carry

    def attend(c, carry):
        frames = frames_ref[first_clip + c]
        masks = head_masks(BF16)
        for w in range(4):
            spots = pl.ds(pl.multiple_of(c * CLIP + w * SPOT, SPOT), SPOT)
            for g in range(GROUPS):
                q = qkv_ref[spots, g * D : g * D + LANES]
                k = qkv_ref[spots, g * D + LANES : g * D + 2 * LANES]
                s = nt(k, stack_heads(q, masks)) * SCALE + bias_ref[g]
                s = jnp.where(time_ref[w] < frames, s, MASKED)
                e = jnp.exp(s - jnp.max(s, axis=0, keepdims=True))
                p = (e * (1.0 / jnp.sum(e, axis=0, keepdims=True))).astype(BF16)
                probs_ref[c, w, g] = p
        for w in range(4):
            spots = pl.ds(pl.multiple_of(c * CLIP + w * SPOT, SPOT), SPOT)
            for g in range(GROUPS):
                v = qkv_ref[spots, g * D + 2 * LANES : g * D + D]
                o = pick_heads(tn(probs_ref[c, w, g], v))
                att_ref[spots, g * LANES : g * LANES + LANES] = o.astype(BF16)
        return carry

    def send_out(c):
        return pltpu.make_async_copy(
            out_ref.at[clip_rows(c % 2, PAIR), :], out_hbm.at[clip_rows(c, PAIR), :], osems.at[0, c]
        )

    def feed(c, carry):
        rows = clip_rows(c, PAIR)
        clip = [clip_rows(2 * c + part) for part in range(2)]
        x = jnp.concatenate([to_windows(tok_ref[r, :].astype(F32)) for r in clip], axis=0)
        og = jnp.concatenate([to_windows(og_ref[r, :].astype(F32)) for r in clip], axis=0)
        middle = x + nn(att_ref[rows, :], wproj_ref[...]) + rowp_ref[4:5]
        nrm, inv = normalize(middle)
        n2 = (nrm * rowp_ref[2:3] + rowp_ref[3:4]).astype(BF16)
        n2t_ref[:, rows] = n2.T
        ogb = og.astype(BF16)
        ogt_ref[:, rows] = ogb.T
        for j in range(FF // CHUNK):
            cols = slice(j * CHUNK, j * CHUNK + CHUNK)
            u = nn(n2, w1_ref[:, cols]) + b1_ref[0:1, cols]
            phi, dens = gelu_parts(u)
            dj_ref[rows, cols] = (u * phi).astype(BF16)
            du = ((phi + u * dens) * nt(ogb, w2_ref[cols, :])).astype(BF16)
            du_ref[rows, cols] = du
            gb_ref[:, cols] += fold(du.astype(F32))
        dmid_ref[rows, :] = middle
        og_ref[rows, :] = ogb
        return carry

    def feed_out(c, carry):
        rows = clip_rows(c, PAIR)
        middle = dmid_ref[rows, :]
        og = og_ref[rows, :].astype(F32)
        result = middle + nn(dj_ref[rows, :], w2_ref[...]) + rowp_ref[5:6]

        @pl.when(c >= 2)
        def _():
            send_out(c - 2).wait()

        for part in range(2):
            r = pl.ds(pl.multiple_of(c % 2 * PAIR + part * CLIP, CLIP), CLIP)
            out_ref[r, :] = from_windows(result[part * CLIP : part * CLIP + CLIP])
        send_out(c).start()
        dn2 = nt(du_ref[rows, :], w1_ref[...])
        nrm, inv = normalize(middle)
        dmid = og + norm_back(dn2, nrm, inv, rowp_ref[2:3])
        dmid_ref[rows, :] = dmid
        dbr = dmid.astype(BF16)
        rows_ref[2] += fold(dn2 * nrm)
        rows_ref[3] += fold(dn2)
        rows_ref[4] += fold(dbr.astype(F32))
        rows_ref[5] += fold(og)
        og_ref[rows, :] = dbr
        return carry

    def feed_grads():
        for j in range(FF // 512):
            cols = slice(j * 512, j * 512 + 512)
            ebuf[0:D, cols] = nn(n2t_ref[...], du_ref[:, cols]).astype(BF16)
            ebuf[D : 2 * D, cols] = nn(ogt_ref[...], dj_ref[:, cols]).astype(BF16)

    def branch_grads():
        for g in range(GROUPS):
            part = tn(att_ref[:, g * LANES : g * LANES + LANES], og_ref[...])
            lbuf[D : D + LANES, g * D : g * D + D] = part.astype(BF16)
        for j in range(clips // 2):
            r = slice(j * PAIR, j * PAIR + PAIR)
            att_ref[r, :] = nt(og_ref[r, :], wproj_ref[...]).astype(BF16)

    def attend_back(c, carry):
        rows = clip_rows(c)
        frames = frames_ref[first_clip + c]
        masks = head_masks(BF16)
        for g in range(GROUPS):
            tacc = None
            for w in range(4):
                spots = pl.ds(pl.multiple_of(c * CLIP + w * SPOT, SPOT), SPOT)
                v = qkv_ref[spots, g * D + 2 * LANES : g * D + D]
                do = stack_heads(att_ref[spots, g * LANES : g * LANES + LANES], masks)
                p = probs_ref[c, w, g]
                pf = p.astype(F32)
                dp = nt(v, do)
                inner = jnp.sum(pf * dp, axis=0, keepdims=True)
                ds = jnp.where(time_ref[w] < frames, pf * (dp - inner), 0.0)
                tacc = ds if tacc is None else tacc + ds
                du_ref[w * SPOT : w * SPOT + SPOT, g * 256 : g * 256 + 256] = ds.astype(BF16)
                dj_ref[spots, g * D + 2 * LANES : g * D + D] = nn(p, do).astype(BF16)
            tacc_ref[g] += tacc
        for g in range(GROUPS):
            for w in range(4):
                spots = pl.ds(pl.multiple_of(c * CLIP + w * SPOT, SPOT), SPOT)
                cq = slice(g * D, g * D + LANES)
                ck = slice(g * D + LANES, g * D + 2 * LANES)
                q = qkv_ref[spots, cq]
                k = qkv_ref[spots, ck]
                ds = du_ref[w * SPOT : w * SPOT + SPOT, g * 256 : g * 256 + 256]
                dj_ref[spots, cq] = (pick_heads(tn(ds, k)) * SCALE).astype(BF16)
                dj_ref[spots, ck] = (nn(ds, stack_heads(q, masks)) * SCALE).astype(BF16)
        gqv_ref[...] += fold(dj_ref[rows, :].astype(F32))
        return carry

    def entry_back(c, carry):
        rows = clip_rows(c, PAIR)
        clip = [clip_rows(2 * c + part) for part in range(2)]
        x = jnp.concatenate([to_windows(tok_ref[r, :].astype(F32)) for r in clip], axis=0)
        n, inv = normalize(x)
        dn1 = nt(dj_ref[rows, :], wqkv_ref[...])
        rows_ref[0] += fold(dn1 * n)
        rows_ref[1] += fold(dn1)
        din = dmid_ref[rows, :] + norm_back(dn1, n, inv, rowp_ref[0:1])
        for part in range(2):
            r = clip[part]
            dmid_ref[r, :] = from_windows(din[part * CLIP : part * CLIP + CLIP])
        pltpu.make_async_copy(dmid_ref.at[rows, :], din_hbm.at[rows, :], osems.at[1, c]).start()
        return carry

    load_tok = pltpu.make_async_copy(tok_hbm, tok_ref, osems.at[2, 0])
    load_og = pltpu.make_async_copy(og_hbm, og_ref, osems.at[2, 1])
    load_tok.start()
    load_og.start()
    small = [
        remote(sown_ref, small_ref.at[head], ssems.at[0, d], ssems.at[1, d], win, (head + d + 1) % 4)
        for d in range(3)
    ]
    own_small = pltpu.make_async_copy(sown_ref, small_ref.at[head], ssems.at[2, 0])
    gq_w = gather_stages(D, wqkv_ref, True, wsems.at[0])
    others = [
        gather_stages(rows, full, wide, wsems.at[1 + i])
        for i, (rows, full, wide) in enumerate(
            ((LANES, wproj_ref, False), (D, w1_ref, True), (D, w2_ref, False))
        )
    ]
    for p in range(3):
        part = qraw_ref[:, p, :].astype(BF16).astype(F32)
        part = jnp.concatenate([part, jnp.zeros((D, LANES - part.shape[1]), F32)], axis=1)
        wqkv_ref[:, pl.ds(pl.multiple_of(head * D + p * LANES, LANES), LANES)] = part.astype(BF16)
    greet()
    gq_w[0]()
    width = qvb_ref.shape[1]
    sown_ref[...] = jnp.zeros_like(sown_ref)
    sown_ref[0:1, :width] = qvb_ref[0:1, :]
    sown_ref[0:1, LANES : LANES + width] = qvb_ref[1:2, :]
    turn_ref[...] = jnp.zeros_like(turn_ref)
    turn_ref[: table_ref.shape[0], :PER] = table_ref[...]
    sown_ref[1 : 1 + PER, :256] = turn_ref[...].T[:PER, :]
    sown_ref[5:6, :] = fc1b_ref[...]
    own_small.start()
    for copy in small:
        copy.start()
    width = praw_ref.shape[0]
    tall = jnp.concatenate([praw_ref[...], jnp.zeros((LANES - width, D), F32)])
    wproj_ref[pl.ds(pl.multiple_of(head * LANES, LANES), LANES), :] = tall.astype(BF16)
    shard = pl.ds(pl.multiple_of(head * D, LANES), D)
    w1_ref[:, shard] = araw_ref[...].astype(BF16)
    w2_ref[shard, :] = braw_ref[...].astype(BF16)
    for k in others:
        k[0]()
    for wt in range(2):
        for wf in range(2):
            time_ref[wt * 2 + wf] = key_times(wt, wf)
    for ref in (rows_ref, gb_ref, gqv_ref, tacc_ref, esbuf, lsbuf):
        ref[...] = jnp.zeros_like(ref)
    load_tok.wait()
    lax.fori_loop(0, clips // 2, enter, 0)
    gq_w[1]()
    own_small.wait()
    for copy in small:
        copy.wait()
    for g in range(4):
        bqkv_ref[0:1, g * D : g * D + LANES] = small_ref[g, 0:1, :LANES]
        bqkv_ref[0:1, g * D + LANES : g * D + 2 * LANES] = jnp.zeros((1, LANES), F32)
        bqkv_ref[0:1, g * D + 2 * LANES : g * D + D] = small_ref[g, 0:1, LANES : 2 * LANES]
        b1_ref[0:1, g * D : g * D + D] = small_ref[g, 5:6, :]
    build_bias(small_ref, bias_ref)
    gq_w[2]()
    gq_w[3]()
    for k in others:
        k[1]()

    def span(share):
        return clips * share // 8

    lax.fori_loop(0, clips // 2, project, 0)
    lax.fori_loop(0, clips, attend, 0)
    for k in others:
        k[2]()
    for k in others:
        k[3]()
    load_og.wait()
    lax.fori_loop(0, clips // 2, feed, 0)
    feed_grads()

    early = reduce_stages(ebuf, core_e, cell_e, up_e, head_e, early_ref, rsems.at[0])
    early_small = small_stages(esbuf, core_es, cell_es, up_es, head_es, esmall_ref, rsems.at[1])
    late = reduce_stages(lbuf, core_l, cell_l, up_l, head_l, late_ref, rsems.at[2])
    late_small = small_stages(lsbuf, core_ls, cell_ls, up_ls, head_ls, lsmall_ref, rsems.at[3])
    early[0]()
    lax.fori_loop(0, span(4) // 2, feed_out, 0)
    early[1]()
    lax.fori_loop(span(4) // 2, clips // 2, feed_out, 0)
    branch_grads()
    esbuf[0:1, :] = jnp.sum(gb_ref[...], axis=0, keepdims=True)
    for r in range(4):
        line = jnp.sum(rows_ref[2 + r], axis=0, keepdims=True)
        for g in range(GROUPS):
            esbuf[1 + r : 2 + r, g * D : g * D + D] = line
    early_small[0]()
    lax.fori_loop(0, span(2), attend_back, 0)
    early_small[1]()
    lax.fori_loop(span(2), span(4), attend_back, 0)
    early[2]()
    early_small[2]()
    lax.fori_loop(span(4), span(8), attend_back, 0)
    for j in range(3):
        cols = slice(j * 512, j * 512 + 512)
        lbuf[0:D, cols] = nn(n1t_ref[...], dj_ref[:, cols]).astype(BF16)
    early[3]()
    late[0]()
    early_small[3]()
    for g in range(GROUPS):
        cols = slice(g * D, g * D + LANES)
        lsbuf[0:1, cols] = jnp.sum(gqv_ref[:, cols], axis=0, keepdims=True)
        cols = slice(g * D + 2 * LANES, g * D + D)
        lsbuf[0:1, cols] = jnp.sum(gqv_ref[:, cols], axis=0, keepdims=True)
    fold_table(tacc_ref, lsbuf)
    late[1]()
    lax.fori_loop(0, span(4) // 2, entry_back, 0)
    early[4]()
    lax.fori_loop(span(4) // 2, clips // 2, entry_back, 0)
    for r in range(2):
        line = jnp.sum(rows_ref[r], axis=0, keepdims=True)
        for g in range(GROUPS):
            lsbuf[4 + r : 5 + r, g * D : g * D + D] = line
    late_small[0]()
    early[5]()
    late[2]()
    late_small[1]()
    late[3]()
    late_small[2]()
    late[4]()
    late_small[3]()
    late[5]()
    square = jnp.zeros((8, D), F32)
    for ref in (early_ref, late_ref):
        value = ref[...].astype(F32)
        square = square + fold(value * value)
    es, ls = esmall_ref[...], lsmall_ref[...]
    row = iota((8, D), 0)
    square = square + jnp.where(row < 1, es * es, 0.0) + jnp.where(row < 4, ls * ls, 0.0)
    common = jnp.where((row >= 1) & (row < 5), es * es, 0.0)
    common = common + jnp.where((row >= 4) & (row < 6), ls * ls, 0.0)
    nslots[head] = jnp.broadcast_to(jnp.sum(square, keepdims=True), (8, LANES))
    sends = [
        remote(
            nslots.at[head], nslots.at[head], nsems.at[0, d], nsems.at[1, d], win, (head + d + 1) % 4
        )
        for d in range(3)
    ]
    for copy in sends:
        copy.start()
    for copy in sends:
        copy.wait()
    total = (nslots[0] + nslots[1]) + (nslots[2] + nslots[3])
    norm_ref[...] = jnp.sqrt(total + jnp.sum(common, keepdims=True))

    def finish(c, carry):
        rows = clip_rows(c, PAIR)
        pltpu.make_async_copy(dmid_ref.at[rows, :], din_hbm.at[rows, :], osems.at[1, c]).wait()
        return carry

    lax.fori_loop(0, clips // 2, finish, 0)
    for c in range(max(clips // 2 - 2, 0), clips // 2):
        send_out(c).wait()


def fold_table(tacc_ref, lsbuf):
    row = iota((256, 256), 0)
    lane = iota((256, 256), 1)
    spot = row % SPOT
    base = 112 - (spot // WIN * (2 * WIN - 1) + spot % WIN)
    for h in range(PER):
        own = jnp.where((lane == base) & (row // SPOT == h), 1.0, 0.0).astype(F32).astype(BF16)
        for g in range(GROUPS):
            spread = None
            for part in split_three(tacc_ref[g]):
                term = nn(part, own)
                spread = term if spread is None else spread + term
            total = None
            for a in range(WIN):
                piece = pltpu.roll(
                    spread[a * 8 : a * 8 + 8], 15 * a, axis=1, stride=1, stride_axis=0
                )
                total = piece if total is None else total + piece
            line = jnp.sum(total, axis=0, keepdims=True)
            for half in range(2):
                at = h * 256 + half * LANES
                lsbuf[1 + at // D : 2 + at // D, g * D + at % D : g * D + at % D + LANES] = line[
                    :, half * LANES : half * LANES + LANES
                ]


def block(frames, tok, og, qraw, praw, araw, braw, qvb, table, fc1b, rowp):
    rows = tok.shape[0]
    clips = rows // CLIP
    upper = max(lax.axis_size("win") // 8, 1).bit_length() - 1
    shape = jax.ShapeDtypeStruct
    sems = pltpu.SemaphoreType.DMA
    vmem = pltpu.VMEM
    spec = pl.BlockSpec
    inside = lambda: spec(memory_space=vmem)
    outside = lambda: spec(memory_space=pl.ANY)
    early, late = 2 * D, D + LANES
    return pl.pallas_call(
        partial(block_kernel, clips),
        in_specs=[spec(memory_space=pltpu.SMEM), outside(), outside()] + [inside()] * 8,
        out_specs=[outside(), outside()] + [inside()] * 5,
        out_shape=[
            shape((rows, D), F32),
            shape((rows, D), F32),
            shape((early, D), BF16),
            shape((late, D), BF16),
            shape((8, D), F32),
            shape((8, D), F32),
            shape((8, LANES), F32),
        ],
        scratch_shapes=[
            vmem((8, D), F32),
            vmem((256, LANES), F32),
            vmem((rows, D), BF16),
            vmem((rows, D), BF16),
            vmem((2 * PAIR, D), F32),
            vmem((rows, D), F32),
            vmem((D, rows), BF16),
            vmem((D, rows), BF16),
            vmem((D, rows), BF16),
            vmem((rows, 1536), BF16),
            vmem((rows, 1536), BF16),
            vmem((rows, FF), BF16),
            vmem((clips, 4, GROUPS, SPOT, PER * SPOT), BF16),
            vmem((rows, 512), BF16),
            vmem((D, 1536), BF16),
            vmem((512, D), BF16),
            vmem((D, FF), BF16),
            vmem((FF, D), BF16),
            vmem((GROUPS, 8, D), F32),
            vmem((8, 1536), F32),
            vmem((8, FF), F32),
            vmem((GROUPS, SPOT, PER * SPOT), F32),
            vmem((4, SPOT, PER * SPOT), jnp.int32),
            vmem((6, 8, D), F32),
            vmem((8, FF), F32),
            vmem((8, 1536), F32),
            vmem((GROUPS, SPOT, PER * SPOT), F32),
            vmem((early, 1536), BF16),
            vmem((late, 1536), BF16),
            vmem((8, 1536), F32),
            vmem((8, 1536), F32),
            vmem((early // 2, 1536), BF16),
            vmem((late // 2, 1536), BF16),
            vmem((8, 1536), F32),
            vmem((8, 1536), F32),
            vmem((3, early // 8, 1536), BF16),
            vmem((3, late // 8, 1536), BF16),
            vmem((4, 8, 1536), F32),
            vmem((4, 8, 1536), F32),
            vmem((upper + 1, early // 8, 1536), BF16),
            vmem((upper + 1, late // 8, 1536), BF16),
            vmem((upper + 1, 8, 1536), F32),
            vmem((upper + 1, 8, 1536), F32),
            vmem((3, early // 8, D), BF16),
            vmem((3, late // 8, D), BF16),
            vmem((4, 8, D), F32),
            vmem((4, 8, D), F32),
            vmem((4, 8, LANES), F32),
            sems((4, 11, 3)),
            sems((3, 3)),
            sems((4, 2, 14 + upper)),
            sems((2, 3)),
            sems((3, max(clips, 2))),
        ],
        compiler_params=pltpu.CompilerParams(
            vmem_limit_bytes=VMEM_LIMIT, collective_id=0, has_side_effects=True
        ),
    )(frames, tok, og, qraw, praw, araw, braw, qvb, table, fc1b, rowp)


def adam_step(weight, gradient, moment, second, factor, rate):
    clipped = gradient * factor
    moment_new = BETA_ONE * moment + (1.0 - BETA_ONE) * clipped
    second_new = BETA_TWO * second + (1.0 - BETA_TWO) * clipped * clipped
    moment_hat = moment_new * (1.0 / (1.0 - BETA_ONE**STEP))
    second_hat = second_new * (1.0 / (1.0 - BETA_TWO**STEP))
    master = weight - rate * (
        moment_hat / (jnp.sqrt(second_hat) + ADAM_EPS) + WEIGHT_DECAY * weight
    )
    return (gradient, moment_new, second_new, master)


def step_kernel(*refs):
    norm_ref, e1_ref, e2_ref, ep_ref, late_ref, es_ref, ls_ref = refs[:7]
    weights, firsts, seconds = refs[7:15], refs[15:23], refs[23:31]
    gn_ref, outs = refs[31], refs[32:]
    norm = norm_ref[0:1, 0:1]
    factor = jnp.minimum(1.0, CLIP_LIMIT / (norm + 1e-06))

    def put(i, gradient, rate, at=(slice(None), slice(None))):
        values = adam_step(weights[i][at], gradient, firsts[i][at], seconds[i][at], factor, rate)
        for k in range(4):
            outs[4 * i + k][at] = values[k]

    late = late_ref[...].astype(F32)
    width = weights[0].shape[2]
    for p in range(3):
        at = (slice(None), p, slice(None))
        put(0, late[:, p * LANES : p * LANES + width], LEARN_RATE, at)
    put(3, ep_ref[...].astype(F32), LEARN_RATE)
    put(4, e1_ref[...].astype(F32), LEARN_RATE)
    put(6, e2_ref[...].astype(F32).T, LEARN_RATE)

    @pl.when(pl.program_id(0) == 0)
    def _():
        gn_ref[...] = norm
        both = jnp.concatenate([ls_ref[0:1, :width], ls_ref[0:1, 2 * LANES : 2 * LANES + width]])
        put(1, both, LEARN_RATE)
        lines = []
        for h in range(PER):
            pieces = []
            for half in range(2):
                at = h * 256 + half * LANES
                pieces.append(ls_ref[1 + at // D : 2 + at // D, at % D : at % D + LANES])
            lines.append(jnp.concatenate(pieces, axis=1))
        lines = jnp.concatenate(lines + [jnp.zeros((8 - PER, 256), F32)])
        offsets = weights[2].shape[0]
        flip = iota((256, 256), 0) + iota((256, 256), 1) == offsets - 1
        flip = jnp.where(flip, 1.0, 0.0).astype(F32).astype(BF16)
        table = None
        for part in split_three(lines):
            term = nt(flip, part)
            table = term if table is None else table + term
        put(2, table[:offsets, :PER], ROW_RATE)
        put(5, es_ref[0:1, :], LEARN_RATE)
        put(7, jnp.concatenate([ls_ref[4:6, :], es_ref[1:5, :]]), ROW_RATE)


def take_step(norm, early, late, esmall, lsmall, weights, firsts, seconds):
    cuts = 3
    spec = pl.BlockSpec
    full = lambda a: spec(a.shape, lambda i: (0,) * a.ndim)
    third = lambda a: spec(
        (a.shape[0] // cuts,) + a.shape[1:], lambda i: (i,) + (0,) * (a.ndim - 1)
    )
    each = [
        third(a) if k in (0, 3, 4, 6) else full(a) for k, a in enumerate(weights)
    ]
    rows = D // cuts
    tall = weights[3].shape[0] // cuts
    shape = jax.ShapeDtypeStruct
    outs = pl.pallas_call(
        step_kernel,
        grid=(cuts,),
        in_specs=[
            full(norm),
            spec((rows, D), lambda i: (i, 0)),
            spec((D, rows), lambda i: (1, i)),
            spec((tall, D), lambda i: (D // tall + i, 0)),
            spec((rows, D), lambda i: (i, 0)),
            full(esmall),
            full(lsmall),
        ]
        + each * 3,
        out_specs=[spec((1, 1), lambda i: (0, 0))] + [e for e in each for _ in range(4)],
        out_shape=[shape((1, 1), F32)] + [shape(a.shape, F32) for a in weights for _ in range(4)],
        compiler_params=pltpu.CompilerParams(vmem_limit_bytes=VMEM_LIMIT),
    )(norm, early, early, late, late, esmall, lsmall, *weights, *firsts, *seconds)
    return outs[0], outs[1:]


def shards(
    tokens,
    out_grad,
    clip_frames,
    qkv_weight,
    qv_bias,
    rel_table,
    proj_weight,
    fc1_weight,
    fc1_bias,
    fc2_weight,
    row_params,
    qkv_first,
    qkv_second,
    qvb_first,
    qvb_second,
    table_first,
    table_second,
    proj_first,
    proj_second,
    fc1_first,
    fc1_second,
    fc1b_first,
    fc1b_second,
    fc2_first,
    fc2_second,
    rows_first,
    rows_second,
):
    line = lambda v: v.reshape(1, -1)
    output, input_grad, early, late, esmall, lsmall, norm = block(
        clip_frames,
        tokens,
        out_grad,
        qkv_weight,
        proj_weight,
        fc1_weight,
        fc2_weight,
        qv_bias,
        rel_table,
        line(fc1_bias),
        row_params,
    )
    weights = (
        qkv_weight,
        qv_bias,
        rel_table,
        proj_weight,
        fc1_weight,
        line(fc1_bias),
        fc2_weight,
        row_params,
    )
    firsts = (
        qkv_first,
        qvb_first,
        table_first,
        proj_first,
        fc1_first,
        line(fc1b_first),
        fc2_first,
        rows_first,
    )
    seconds = (
        qkv_second,
        qvb_second,
        table_second,
        proj_second,
        fc1_second,
        line(fc1b_second),
        fc2_second,
        rows_second,
    )
    grad_norm, updated = take_step(norm, early, late, esmall, lsmall, weights, firsts, seconds)
    updated = [v.reshape(-1) if 20 <= k < 24 else v for k, v in enumerate(updated)]
    return (output, input_grad, grad_norm.reshape(()), *updated)


def solution(mesh):
    rows = P(("win", "head"), None)
    last3, last2, first2, first1 = P(None, None, "head"), P(None, "head"), P("head", None), P("head")
    each = (last3, last2, last2, first2, last2, first1, first2, P())
    return jax.shard_map(
        shards,
        mesh=mesh,
        in_specs=(rows, rows, P("win")) + each + tuple(s for s in each for _ in range(2)),
        out_specs=(rows, rows, P()) + tuple(s for s in each for _ in range(4)),
        check_vma=False,
    )
```

```python
from functools import partial

import jax
import jax.numpy as jnp
from jax import lax
from jax.experimental import pallas as pl
from jax.experimental.pallas import tpu as pltpu
from jax.sharding import PartitionSpec as P

D = 384
HDIM = 24
HEADS = 16
GROUPS = 4
PER = 4
LANES = 128
FF = 1536
GRID = 16
WIN = 8
CLIP = GRID * GRID
SPOT = WIN * WIN
SHIFT = 4
STEP = 10
CHUNK = 768
PAIR = 2 * CLIP

NORM_EPS = 1e-05
MASKED = -1000000000.0
CLIP_LIMIT = 1.0
LEARN_RATE = 0.1
ROW_RATE = 0.5
BETA_ONE = 0.9
BETA_TWO = 0.999
ADAM_EPS = 1e-08
WEIGHT_DECAY = 0.01
SCALE = HDIM ** (-0.5)
F32 = jnp.float32
BF16 = jnp.bfloat16
VMEM_LIMIT = 60 * 1024 * 1024


def nn(a, b):
    return lax.dot_general(a, b, (((1,), (0,)), ((), ())), preferred_element_type=F32)


def nt(a, b):
    return lax.dot_general(a, b, (((1,), (1,)), ((), ())), preferred_element_type=F32)


def tn(a, b):
    return lax.dot_general(a, b, (((0,), (0,)), ((), ())), preferred_element_type=F32)


def iota(shape, axis):
    return lax.broadcasted_iota(jnp.int32, shape, axis)


def fold(x):
    return jnp.sum(x.reshape(x.shape[0] // 8, 8, x.shape[1]), axis=0)


def normalize(x):
    center = x - jnp.mean(x, axis=-1, keepdims=True)
    spread = jnp.mean(center * center, axis=-1, keepdims=True)
    inverse = lax.rsqrt(spread + NORM_EPS)
    return center * inverse, inverse


def norm_back(e, n, inverse, gain):
    q = e * gain
    return inverse * (
        q - jnp.mean(q, axis=-1, keepdims=True) - n * jnp.mean(q * n, axis=-1, keepdims=True)
    )


def to_windows(x):
    low = iota((8, x.shape[1]), 0) < 4
    first, second = [], []
    for t in range(GRID):
        a = x[16 * t : 16 * t + 8]
        b = x[16 * t + 8 : 16 * t + 16]
        first.append(pltpu.roll(jnp.where(low, b, a), 4, axis=0))
        second.append(pltpu.roll(jnp.where(low, a, b), 4, axis=0))
    pieces = []
    for wt in range(2):
        for side in (first, second):
            for a in range(WIN):
                pieces.append(side[(wt * WIN + a + SHIFT) % GRID])
    return jnp.concatenate(pieces, axis=0)


def from_windows(y):
    low = iota((8, y.shape[1]), 0) < 4
    pieces = []
    for t in range(GRID):
        rolled = (t - SHIFT) % GRID
        base = (rolled // WIN) * 128 + (rolled % WIN) * 8
        u = pltpu.roll(y[base : base + 8], 4, axis=0)
        v = pltpu.roll(y[base + 64 : base + 72], 4, axis=0)
        pieces.append(jnp.where(low, v, u))
        pieces.append(jnp.where(low, u, v))
    return jnp.concatenate(pieces, axis=0)


def head_masks(dtype):
    lane = iota((16, LANES), 1) // HDIM
    return [jnp.where(lane == h, 1.0, 0.0).astype(F32).astype(dtype) for h in range(PER)]


def stack_heads(x, masks):
    tiles = x.reshape(SPOT // 16, 16, LANES)
    return jnp.concatenate([(tiles * m[None]).reshape(SPOT, LANES) for m in masks], axis=0)


def pick_heads(r):
    lane = iota((SPOT, LANES), 1)
    out = r[3 * SPOT :]
    for h in (2, 1, 0):
        out = jnp.where(lane < (h + 1) * HDIM, r[h * SPOT : (h + 1) * SPOT], out)
    return out


def key_times(wt, wf):
    j = iota((SPOT, PER * SPOT), 0)
    i = iota((SPOT, PER * SPOT), 1) % SPOT
    time = (wt * WIN + j // WIN + SHIFT) % GRID
    same = j >= 0
    if wt:
        same = same & ((j // WIN < 4) == (i // WIN < 4))
    if wf:
        same = same & ((j % WIN < 4) == (i % WIN < 4))
    return jnp.where(same, time, 99)


def split_three(x):
    one = x.astype(BF16)
    rest = x - one.astype(F32)
    two = rest.astype(BF16)
    three = (rest - two.astype(F32)).astype(BF16)
    return one, two, three


def build_bias(table_ref, bias_ref):
    row = iota((256, 256), 0)
    lane = iota((256, 256), 1)
    spot = lane % SPOT
    base = spot // WIN * (2 * WIN - 1) + spot % WIN
    for g in range(GROUPS):
        total = None
        for h in range(PER):
            own = jnp.where((row == base) & (lane // SPOT == h), 1.0, 0.0).astype(F32).astype(BF16)
            line = jnp.broadcast_to(table_ref[g, 1 + h : 2 + h, :256], (8, 256))
            spread = jnp.concatenate(
                [
                    pltpu.roll(line, (15 * a + 144) % 256, axis=1, stride=1, stride_axis=0)
                    for a in range(WIN)
                ],
                axis=0,
            )
            for part in split_three(spread):
                term = nn(part, own)
                total = term if total is None else total + term
        bias_ref[g] = total


def gelu_parts(u):
    mag = jnp.abs(u) * (0.5**0.5)
    t = 1.0 / (1.0 + 0.3275911 * mag)
    bell = jnp.exp(-0.5 * (u * u))
    poly = t * (
        0.127414796
        + t * (-0.142248368 + t * (0.7107068705 + t * (-0.7265760135 + t * 0.5307027145)))
    )
    tail = poly * bell
    return jnp.where(u >= 0.0, 1.0 - tail, tail), bell * 0.3989422804014327


def place(win, head):
    return {"win": win, "head": head}


def remote(src, dst, send, recv, win, head):
    return pltpu.make_async_remote_copy(
        src_ref=src,
        dst_ref=dst,
        send_sem=send,
        recv_sem=recv,
        device_id=place(win, head),
        device_id_type=pl.DeviceIdType.MESH,
    )


def position():
    win, head = lax.axis_index("win"), lax.axis_index("head")
    core, cell = win % 2, (win // 2) % 4
    return win, head, core, cell, win - core - 2 * cell


def greet():
    win, head, core, cell, base = position()
    barrier = pltpu.get_barrier_semaphore()
    peers = [(win, (head + d) % 4) for d in (1, 2, 3)]
    peers += [(base + 2 * ((cell + d) % 4) + core, head) for d in (1, 2, 3)]
    peers += [(win + 1 - 2 * core, head)]
    for w, h in peers:
        pl.semaphore_signal(barrier, inc=1, device_id=place(w, h), device_id_type=pl.DeviceIdType.MESH)
    pl.semaphore_wait(barrier, len(peers))


def shard_view(ref, wide, head, start, count):
    if wide:
        return ref.at[pl.ds(start, count), pl.ds(pl.multiple_of(head * D, LANES), D)]
    rows = ref.shape[0] // 4
    return ref.at[pl.ds(pl.multiple_of(head * rows + start, 16), count), :]


def gather_stages(rows, full, wide, sems):
    win, head, core, cell, base = position()
    half, part = rows // 2, rows // 8
    mine = pl.multiple_of(core * half + cell * part, 16)
    near = pl.multiple_of(core * half, 16)

    def over_head(d):
        view = shard_view(full, wide, head, mine, part)
        return remote(view, view, sems.at[0, d], sems.at[1, d], win, (head + d + 1) % 4)

    def over_cell(d, c):
        view = shard_view(full, wide, (head + 3 - d) % 4, mine, part)
        peer = base + 2 * ((cell + c + 1) % 4) + core
        return remote(view, view, sems.at[2 + c, d], sems.at[5 + c, d], peer, head)

    def over_core(d):
        view = shard_view(full, wide, (head + 3 - d) % 4, near, half)
        return remote(view, view, sems.at[8, d], sems.at[9, d], win + 1 - 2 * core, head)

    def first():
        for d in range(3):
            over_head(d).start()

    def second():
        for d in range(3):
            over_head(d).wait_recv()
            for c in range(3):
                over_cell(d, c).start()

    def third():
        for d in range(3):
            for c in range(3):
                over_cell(d, c).wait_recv()
            over_core(d).start()

    def last():
        for d in range(3):
            over_core(d).wait_recv()
        for d in range(3):
            over_head(d).wait_send()
            for c in range(3):
                over_cell(d, c).wait_send()
            over_core(d).wait_send()

    return first, second, third, last


def reduce_stages(buf, from_core, from_cell, from_upper, from_head, final, sems):
    win, head, core, cell, base = position()
    rows = buf.shape[0]
    half, part = rows // 2, rows // 8
    near = pl.multiple_of(core * half, 16)
    far = pl.multiple_of((1 - core) * half, 16)
    mine = pl.multiple_of(core * half + cell * part, 16)
    other = win + 1 - 2 * core
    own = pl.ds(mine, part)

    def lanes(h):
        return pl.ds(pl.multiple_of(h * D, LANES), D)

    def to_core():
        return remote(
            buf.at[pl.ds(far, half), :], from_core, sems.at[0, 0], sems.at[1, 0], other, head
        )

    def to_cell(c):
        peer = (cell + c + 1) % 4
        start = pl.multiple_of(core * half + peer * part, 16)
        return remote(
            buf.at[pl.ds(start, part), :],
            from_cell.at[c],
            sems.at[0, 1 + c],
            sems.at[1, 1 + c],
            base + 2 * peer + core,
            head,
        )

    def to_upper(b):
        peer = win + (8 << b) - 2 * (8 << b) * (win // (8 << b) % 2)
        return remote(
            buf.at[own, :], from_upper.at[b], sems.at[0, 14 + b], sems.at[1, 14 + b], peer, head
        )

    def to_head(d):
        peer = (head + d + 1) % 4
        return remote(
            buf.at[own, lanes(peer)],
            from_head.at[d],
            sems.at[0, 4 + d],
            sems.at[1, 4 + d],
            win,
            peer,
        )

    def back_cell(c):
        peer = (cell + c + 1) % 4
        return remote(
            final.at[own, :],
            final.at[own, :],
            sems.at[0, 7 + c],
            sems.at[1, 7 + c],
            base + 2 * peer + core,
            head,
        )

    def back_core():
        view = final.at[pl.ds(near, half), :]
        return remote(view, view, sems.at[0, 10], sems.at[1, 10], other, head)

    def first():
        to_core().start()

    def second():
        to_core().wait_recv()
        for k in range(4):
            start = pl.multiple_of(core * half + k * part, 16)
            block = pl.ds(start, part)
            total = buf[block, :].astype(F32) + from_core[k * part : k * part + part].astype(F32)
            buf[block, :] = total.astype(BF16)
        for c in range(3):
            to_cell(c).start()

    def third():
        for c in range(3):
            to_cell(c).wait_recv()
        total = buf[own, :].astype(F32)
        for c in range(3):
            total = total + from_cell[c].astype(F32)
        buf[own, :] = total.astype(BF16)
        for b in range(from_upper.shape[0] - 1):
            to_upper(b).start()
            to_upper(b).wait()
            buf[own, :] = (buf[own, :].astype(F32) + from_upper[b].astype(F32)).astype(BF16)
        for d in range(3):
            to_head(d).start()

    def fourth():
        for d in range(3):
            to_head(d).wait_recv()
        total = buf[own, lanes(head)].astype(F32)
        for d in range(3):
            total = total + from_head[d].astype(F32)
        final[own, :] = total.astype(BF16)
        for c in range(3):
            back_cell(c).start()

    def fifth():
        for c in range(3):
            back_cell(c).wait_recv()
        back_core().start()

    def last():
        back_core().wait_recv()
        to_core().wait_send()
        for c in range(3):
            to_cell(c).wait_send()
            to_head(c).wait_send()
            back_cell(c).wait_send()
        back_core().wait_send()

    return first, second, third, fourth, fifth, last


def small_stages(buf, from_core, cells, from_upper, heads, final, sems):
    win, head, core, cell, base = position()
    other = win + 1 - 2 * core

    def lanes(h):
        return pl.ds(pl.multiple_of(h * D, LANES), D)

    def to_core():
        return remote(buf, from_core, sems.at[0, 0], sems.at[1, 0], other, head)

    def to_cell(c):
        view = cells.at[cell]
        peer = base + 2 * ((cell + c + 1) % 4) + core
        return remote(view, view, sems.at[0, 1 + c], sems.at[1, 1 + c], peer, head)

    def to_upper(b):
        peer = win + (8 << b) - 2 * (8 << b) * (win // (8 << b) % 2)
        return remote(buf, from_upper.at[b], sems.at[0, 14 + b], sems.at[1, 14 + b], peer, head)

    def to_head(d):
        peer = (head + d + 1) % 4
        return remote(
            buf.at[:, lanes(peer)], heads.at[head], sems.at[0, 4 + d], sems.at[1, 4 + d], win, peer
        )

    def first():
        to_core().start()

    def second():
        to_core().wait()
        cells[cell] = buf[...] + from_core[...]
        for c in range(3):
            to_cell(c).start()

    def third():
        for c in range(3):
            to_cell(c).wait()
        buf[...] = (cells[0] + cells[1]) + (cells[2] + cells[3])
        for b in range(from_upper.shape[0] - 1):
            to_upper(b).start()
            to_upper(b).wait()
            buf[...] = buf[...] + from_upper[b]
        heads[head] = buf[:, lanes(head)]
        for d in range(3):
            to_head(d).start()

    def last():
        for d in range(3):
            to_head(d).wait()
        final[...] = (heads[0] + heads[1]) + (heads[2] + heads[3])

    return first, second, third, last


def clip_rows(c, count=CLIP):
    return pl.ds(pl.multiple_of(c * count, count), count)


def block_kernel(
    clips,
    frames_ref,
    tok_hbm,
    og_hbm,
    qraw_ref,
    praw_ref,
    araw_ref,
    braw_ref,
    qvb_ref,
    table_ref,
    fc1b_ref,
    rowp_ref,
    out_hbm,
    din_hbm,
    one_ref,
    two_ref,
    late_ref,
    esmall_ref,
    lsmall_ref,
    norm_ref,
    sown_ref,
    tok_ref,
    og_ref,
    mid_ref,
    dmid_ref,
    n1t_ref,
    n2_ref,
    qkv_ref,
    dj_ref,
    hid_ref,
    probs_ref,
    att_ref,
    wqkv_ref,
    wproj_ref,
    w1_ref,
    w2_ref,
    small_ref,
    bqkv_ref,
    b1_ref,
    bias_ref,
    time_ref,
    rows_ref,
    gb_ref,
    gqv_ref,
    tacc_ref,
    buf_1,
    buf_2,
    lbuf,
    esbuf,
    lsbuf,
    core_1,
    core_2,
    core_l,
    core_es,
    core_ls,
    cell_1,
    cell_2,
    cell_l,
    cell_es,
    cell_ls,
    up_1,
    up_2,
    up_l,
    up_es,
    up_ls,
    head_1,
    head_2,
    head_l,
    head_es,
    head_ls,
    nslots,
    wsems,
    ssems,
    rsems,
    nsems,
    osems,
):
    win, head, core, cell, base = position()
    first_clip = head * clips

    def enter(c, carry):
        for part in range(2):
            rows = clip_rows(2 * c + part)
            n1, _ = normalize(to_windows(tok_ref[rows, :].astype(F32)))
            n1 = (n1 * rowp_ref[0:1] + rowp_ref[1:2]).astype(BF16)
            att_ref[rows, :D] = n1
            n1t_ref[:, rows] = n1.T
        return carry

    def project(c, carry):
        rows = clip_rows(c, PAIR)
        for part in range(3):
            cols = slice(part * 512, part * 512 + 512)
            y = nt(att_ref[rows, :D], wqkv_ref[cols, :]) + bqkv_ref[0:1, cols]
            qkv_ref[rows, cols] = y.astype(BF16)
        return carry

    def attend(c, carry):
        frames = frames_ref[first_clip + c]
        masks = head_masks(BF16)
        for w in range(4):
            spots = pl.ds(pl.multiple_of(c * CLIP + w * SPOT, SPOT), SPOT)
            for g in range(GROUPS):
                q = qkv_ref[spots, g * D : g * D + LANES]
                k = qkv_ref[spots, g * D + LANES : g * D + 2 * LANES]
                s = nt(k, stack_heads(q, masks)) * SCALE + bias_ref[g]
                s = jnp.where(time_ref[w] < frames, s, MASKED)
                e = jnp.exp(s - jnp.max(s, axis=0, keepdims=True))
                p = (e * (1.0 / jnp.sum(e, axis=0, keepdims=True))).astype(BF16)
                probs_ref[c, w, g] = p
        for w in range(4):
            spots = pl.ds(pl.multiple_of(c * CLIP + w * SPOT, SPOT), SPOT)
            for g in range(GROUPS):
                v = qkv_ref[spots, g * D + 2 * LANES : g * D + D]
                o = pick_heads(tn(probs_ref[c, w, g], v))
                att_ref[spots, g * LANES : g * LANES + LANES] = o.astype(BF16)
        return carry

    def send_out(c):
        rows = clip_rows(c, PAIR)
        return pltpu.make_async_copy(mid_ref.at[rows, :], out_hbm.at[rows, :], osems.at[0, c])

    def widen(c, carry):
        rows = clip_rows(c, PAIR)
        clip = [clip_rows(2 * c + part) for part in range(2)]
        x = jnp.concatenate([to_windows(tok_ref[r, :].astype(F32)) for r in clip], axis=0)
        og = jnp.concatenate([to_windows(og_ref[r, :].astype(F32)) for r in clip], axis=0)
        og_ref[rows, :] = og.astype(BF16)
        rows_ref[5] += fold(og)
        middle = x + nn(att_ref[rows, :], wproj_ref[...]) + rowp_ref[4:5]
        mid_ref[rows, :] = middle
        nrm, _ = normalize(middle)
        n2 = (nrm * rowp_ref[2:3] + rowp_ref[3:4]).astype(BF16)
        n2_ref[rows, :] = n2
        for j in range(FF // CHUNK):
            cols = slice(j * CHUNK, j * CHUNK + CHUNK)
            u = nn(n2, w1_ref[:, cols]) + b1_ref[0:1, cols]
            phi, dens = gelu_parts(u)
            hid_ref[rows, cols] = (u * phi).astype(BF16)
            dj_ref[rows, cols] = (phi + u * dens).astype(BF16)
        return carry

    def narrow_back(c, carry):
        rows = clip_rows(c, PAIR)
        for j in range(FF // CHUNK):
            cols = slice(j * CHUNK, j * CHUNK + CHUNK)
            dh = nt(og_ref[rows, :], w2_ref[cols, :])
            du = (dj_ref[rows, cols].astype(F32) * dh).astype(BF16)
            dj_ref[rows, cols] = du
            gb_ref[:, cols] += fold(du.astype(F32))
        return carry

    def widen_back(c, carry):
        rows = clip_rows(c, PAIR)
        dn2 = nt(dj_ref[rows, :], w1_ref[...])
        nrm, inv = normalize(mid_ref[rows, :])
        dmid = og_ref[rows, :].astype(F32) + norm_back(dn2, nrm, inv, rowp_ref[2:3])
        dmid_ref[rows, :] = dmid
        dbr = dmid.astype(BF16)
        rows_ref[2] += fold(dn2 * nrm)
        rows_ref[3] += fold(dn2)
        rows_ref[4] += fold(dbr.astype(F32))
        og_ref[rows, :] = dbr
        return carry

    def narrow(c, carry):
        rows = clip_rows(c, PAIR)
        result = mid_ref[rows, :] + nn(hid_ref[rows, :], w2_ref[...]) + rowp_ref[5:6]
        for part in range(2):
            result_part = from_windows(result[part * CLIP : part * CLIP + CLIP])
            mid_ref[clip_rows(2 * c + part), :] = result_part
        send_out(c).start()
        return carry

    def wide_grads(buf, given, back):
        for j in range(FF // 512):
            cols = slice(j * 512, j * 512 + 512)
            buf[:, cols] = tn(given[...], back[:, cols]).astype(BF16)

    def branch_grads():
        width = praw_ref.shape[0]
        for g in range(GROUPS):
            part = tn(att_ref[:, g * LANES : g * LANES + LANES], og_ref[...])
            lbuf[3 * width :, g * D : g * D + D] = part[:width].astype(BF16)
        for j in range(clips // 2):
            r = slice(j * PAIR, j * PAIR + PAIR)
            att_ref[r, :] = nt(og_ref[r, :], wproj_ref[...]).astype(BF16)

    def qkv_grads():
        width = praw_ref.shape[0]
        for j in range(3):
            value = nn(n1t_ref[...], dj_ref[:, j * 512 : j * 512 + 512])
            for k in range(4):
                g, p = (4 * j + k) // 3, (4 * j + k) % 3
                turned = value[:, k * LANES : k * LANES + LANES].T
                lbuf[p * width : p * width + width, g * D : g * D + D] = turned[:width].astype(BF16)

    def attend_back(c, carry):
        rows = clip_rows(c)
        frames = frames_ref[first_clip + c]
        masks = head_masks(BF16)
        for g in range(GROUPS):
            tacc = None
            for w in range(4):
                spots = pl.ds(pl.multiple_of(c * CLIP + w * SPOT, SPOT), SPOT)
                v = qkv_ref[spots, g * D + 2 * LANES : g * D + D]
                do = stack_heads(att_ref[spots, g * LANES : g * LANES + LANES], masks)
                p = probs_ref[c, w, g]
                pf = p.astype(F32)
                dp = nt(v, do)
                inner = jnp.sum(pf * dp, axis=0, keepdims=True)
                ds = jnp.where(time_ref[w] < frames, pf * (dp - inner), 0.0)
                tacc = ds if tacc is None else tacc + ds
                probs_ref[c, w, g] = ds.astype(BF16)
                dj_ref[spots, g * D + 2 * LANES : g * D + D] = nn(p, do).astype(BF16)
            tacc_ref[g] += tacc
        for g in range(GROUPS):
            for w in range(4):
                spots = pl.ds(pl.multiple_of(c * CLIP + w * SPOT, SPOT), SPOT)
                cq = slice(g * D, g * D + LANES)
                ck = slice(g * D + LANES, g * D + 2 * LANES)
                q = qkv_ref[spots, cq]
                k = qkv_ref[spots, ck]
                ds = probs_ref[c, w, g]
                dj_ref[spots, cq] = (pick_heads(tn(ds, k)) * SCALE).astype(BF16)
                dj_ref[spots, ck] = (nn(ds, stack_heads(q, masks)) * SCALE).astype(BF16)
        gqv_ref[...] += fold(dj_ref[rows, :].astype(F32))
        return carry

    def entry_back(c, carry):
        rows = clip_rows(c, PAIR)
        clip = [clip_rows(2 * c + part) for part in range(2)]
        x = jnp.concatenate([to_windows(tok_ref[r, :].astype(F32)) for r in clip], axis=0)
        n, inv = normalize(x)
        dn1 = nn(dj_ref[rows, :], wqkv_ref[...])
        rows_ref[0] += fold(dn1 * n)
        rows_ref[1] += fold(dn1)
        din = dmid_ref[rows, :] + norm_back(dn1, n, inv, rowp_ref[0:1])
        for part in range(2):
            r = clip[part]
            dmid_ref[r, :] = from_windows(din[part * CLIP : part * CLIP + CLIP])
        pltpu.make_async_copy(dmid_ref.at[rows, :], din_hbm.at[rows, :], osems.at[1, c]).start()
        return carry

    load_tok = pltpu.make_async_copy(tok_hbm, tok_ref, osems.at[2, 0])
    load_og = pltpu.make_async_copy(og_hbm, og_ref, osems.at[2, 1])
    load_tok.start()
    load_og.start()
    small = [
        remote(sown_ref, small_ref.at[head], ssems.at[0, d], ssems.at[1, d], win, (head + d + 1) % 4)
        for d in range(3)
    ]
    own_small = pltpu.make_async_copy(sown_ref, small_ref.at[head], ssems.at[2, 0])
    gq_w = gather_stages(D, wqkv_ref, False, wsems.at[0])
    others = [
        gather_stages(rows, full, wide, wsems.at[1 + i])
        for i, (rows, full, wide) in enumerate(
            ((LANES, wproj_ref, False), (D, w1_ref, True), (D, w2_ref, False))
        )
    ]
    for p in range(3):
        part = qraw_ref[p]
        part = jnp.concatenate([part, jnp.zeros((LANES - part.shape[0], D), F32)], axis=0)
        start = pl.multiple_of(head * D + p * LANES, LANES)
        wqkv_ref[pl.ds(start, LANES), :] = part.astype(BF16)
    greet()
    gq_w[0]()
    width = qvb_ref.shape[1]
    sown_ref[...] = jnp.zeros_like(sown_ref)
    sown_ref[0:1, :width] = qvb_ref[0:1, :]
    sown_ref[0:1, LANES : LANES + width] = qvb_ref[1:2, :]
    sown_ref[1 : 1 + PER, : table_ref.shape[1]] = table_ref[...]
    sown_ref[5:6, :] = fc1b_ref[...].reshape(1, D)
    own_small.start()
    for copy in small:
        copy.start()
    width = praw_ref.shape[0]
    tall = jnp.concatenate([praw_ref[...], jnp.zeros((LANES - width, D), F32)])
    wproj_ref[pl.ds(pl.multiple_of(head * LANES, LANES), LANES), :] = tall.astype(BF16)
    shard = pl.ds(pl.multiple_of(head * D, LANES), D)
    w1_ref[:, shard] = araw_ref[...].astype(BF16)
    w2_ref[shard, :] = braw_ref[...].astype(BF16)
    for k in others:
        k[0]()
    for wt in range(2):
        for wf in range(2):
            time_ref[wt * 2 + wf] = key_times(wt, wf)
    for ref in (rows_ref, gb_ref, gqv_ref, tacc_ref, esbuf, lsbuf):
        ref[...] = jnp.zeros_like(ref)
    load_tok.wait()
    lax.fori_loop(0, clips // 2, enter, 0)
    gq_w[1]()
    own_small.wait()
    for copy in small:
        copy.wait()
    for g in range(4):
        bqkv_ref[0:1, g * D : g * D + LANES] = small_ref[g, 0:1, :LANES]
        bqkv_ref[0:1, g * D + LANES : g * D + 2 * LANES] = jnp.zeros((1, LANES), F32)
        bqkv_ref[0:1, g * D + 2 * LANES : g * D + D] = small_ref[g, 0:1, LANES : 2 * LANES]
        b1_ref[0:1, g * D : g * D + D] = small_ref[g, 5:6, :]
    build_bias(small_ref, bias_ref)
    gq_w[2]()
    gq_w[3]()
    for k in others:
        k[1]()

    def span(share):
        return clips * share // 8

    lax.fori_loop(0, clips // 2, project, 0)
    lax.fori_loop(0, span(4), attend, 0)
    others[0][2]()
    others[1][2]()
    lax.fori_loop(span(4), span(8), attend, 0)
    others[0][3]()
    others[1][3]()
    load_og.wait()
    lax.fori_loop(0, span(4) // 2, widen, 0)
    others[2][2]()
    lax.fori_loop(span(4) // 2, clips // 2, widen, 0)
    others[2][3]()
    one = reduce_stages(buf_1, core_1, cell_1, up_1, head_1, one_ref, rsems.at[0])
    two = reduce_stages(buf_2, core_2, cell_2, up_2, head_2, two_ref, rsems.at[1])
    late = reduce_stages(lbuf, core_l, cell_l, up_l, head_l, late_ref, rsems.at[2])
    early_small = small_stages(esbuf, core_es, cell_es, up_es, head_es, esmall_ref, rsems.at[3])
    late_small = small_stages(lsbuf, core_ls, cell_ls, up_ls, head_ls, lsmall_ref, rsems.at[4])
    wide_grads(buf_2, og_ref, hid_ref)
    two[0]()
    lax.fori_loop(0, span(4) // 2, narrow_back, 0)
    two[1]()
    lax.fori_loop(span(4) // 2, clips // 2, narrow_back, 0)
    wide_grads(buf_1, n2_ref, dj_ref)
    one[0]()
    lax.fori_loop(0, span(4) // 2, widen_back, 0)
    one[1]()
    two[2]()
    lax.fori_loop(span(4) // 2, clips // 2, widen_back, 0)
    branch_grads()
    two[3]()
    esbuf[0:1, :] = jnp.sum(gb_ref[...], axis=0, keepdims=True)
    for r in range(4):
        line = jnp.sum(rows_ref[2 + r], axis=0, keepdims=True)
        for g in range(GROUPS):
            esbuf[1 + r : 2 + r, g * D : g * D + D] = line
    early_small[0]()
    lax.fori_loop(0, span(2), attend_back, 0)
    two[4]()
    one[2]()
    early_small[1]()
    lax.fori_loop(span(2), span(5), attend_back, 0)
    one[3]()
    two[5]()
    early_small[2]()
    lax.fori_loop(span(5), span(7), attend_back, 0)
    one[4]()
    lax.fori_loop(span(7), span(8), attend_back, 0)
    qkv_grads()
    late[0]()
    one[5]()
    early_small[3]()
    for g in range(GROUPS):
        cols = slice(g * D, g * D + LANES)
        lsbuf[0:1, cols] = jnp.sum(gqv_ref[:, cols], axis=0, keepdims=True)
        cols = slice(g * D + 2 * LANES, g * D + D)
        lsbuf[0:1, cols] = jnp.sum(gqv_ref[:, cols], axis=0, keepdims=True)
    late[1]()
    fold_table(tacc_ref, lsbuf)
    lax.fori_loop(0, clips // 2, entry_back, 0)
    for r in range(2):
        line = jnp.sum(rows_ref[r], axis=0, keepdims=True)
        for g in range(GROUPS):
            lsbuf[4 + r : 5 + r, g * D : g * D + D] = line
    late_small[0]()
    lax.fori_loop(0, span(4) // 2, narrow, 0)
    late[2]()
    late_small[1]()
    lax.fori_loop(span(4) // 2, clips // 2, narrow, 0)
    late_small[2]()
    late[3]()
    late_small[3]()
    late[4]()
    late[5]()
    square = jnp.zeros((8, D), F32)
    for ref in (one_ref, two_ref, late_ref):
        value = ref[...].astype(F32)
        square = square + fold(value * value)
    es, ls = esmall_ref[...], lsmall_ref[...]
    row = iota((8, D), 0)
    square = square + jnp.where(row < 1, es * es, 0.0) + jnp.where(row < 4, ls * ls, 0.0)
    common = jnp.where((row >= 1) & (row < 5), es * es, 0.0)
    common = common + jnp.where((row >= 4) & (row < 6), ls * ls, 0.0)
    nslots[head] = jnp.broadcast_to(jnp.sum(square, keepdims=True), (8, LANES))
    sends = [
        remote(
            nslots.at[head], nslots.at[head], nsems.at[0, d], nsems.at[1, d], win, (head + d + 1) % 4
        )
        for d in range(3)
    ]
    for copy in sends:
        copy.start()
    for copy in sends:
        copy.wait()
    total = (nslots[0] + nslots[1]) + (nslots[2] + nslots[3])
    norm_ref[...] = jnp.sqrt(total + jnp.sum(common, keepdims=True))

    def finish(c, carry):
        rows = clip_rows(c, PAIR)
        send_out(c).wait()
        pltpu.make_async_copy(dmid_ref.at[rows, :], din_hbm.at[rows, :], osems.at[1, c]).wait()
        return carry

    lax.fori_loop(0, clips // 2, finish, 0)


def fold_table(tacc_ref, lsbuf):
    row = iota((256, 256), 0)
    lane = iota((256, 256), 1)
    spot = row % SPOT
    base = 112 - (spot // WIN * (2 * WIN - 1) + spot % WIN)
    for h in range(PER):
        own = jnp.where((lane == base) & (row // SPOT == h), 1.0, 0.0).astype(F32).astype(BF16)
        for g in range(GROUPS):
            spread = None
            for part in split_three(tacc_ref[g]):
                term = nn(part, own)
                spread = term if spread is None else spread + term
            total = None
            for a in range(WIN):
                piece = pltpu.roll(
                    spread[a * 8 : a * 8 + 8], 15 * a, axis=1, stride=1, stride_axis=0
                )
                total = piece if total is None else total + piece
            line = jnp.sum(total, axis=0, keepdims=True)
            for half in range(2):
                at = h * 256 + half * LANES
                lsbuf[1 + at // D : 2 + at // D, g * D + at % D : g * D + at % D + LANES] = line[
                    :, half * LANES : half * LANES + LANES
                ]


def block(frames, tok, og, qraw, praw, araw, braw, qvb, table, fc1b, rowp):
    rows = tok.shape[0]
    clips = rows // CLIP
    upper = max(lax.axis_size("win") // 8, 1).bit_length() - 1
    shape = jax.ShapeDtypeStruct
    sems = pltpu.SemaphoreType.DMA
    vmem = pltpu.VMEM
    spec = pl.BlockSpec
    inside = lambda: spec(memory_space=vmem)
    outside = lambda: spec(memory_space=pl.ANY)
    half, part = D // 2, D // 8
    return pl.pallas_call(
        partial(block_kernel, clips),
        in_specs=[spec(memory_space=pltpu.SMEM), outside(), outside()] + [inside()] * 8,
        out_specs=[outside(), outside()] + [inside()] * 6,
        out_shape=[
            shape((rows, D), F32),
            shape((rows, D), F32),
            shape((D, D), BF16),
            shape((D, D), BF16),
            shape((D, D), BF16),
            shape((8, D), F32),
            shape((8, D), F32),
            shape((8, LANES), F32),
        ],
        scratch_shapes=[
            vmem((8, D), F32),
            vmem((rows, D), BF16),
            vmem((rows, D), BF16),
            vmem((rows, D), F32),
            vmem((rows, D), F32),
            vmem((D, rows), BF16),
            vmem((rows, D), BF16),
            vmem((rows, 1536), BF16),
            vmem((rows, 1536), BF16),
            vmem((rows, FF), BF16),
            vmem((clips, 4, GROUPS, SPOT, PER * SPOT), BF16),
            vmem((rows, 512), BF16),
            vmem((1536, D), BF16),
            vmem((512, D), BF16),
            vmem((D, FF), BF16),
            vmem((FF, D), BF16),
            vmem((GROUPS, 8, D), F32),
            vmem((8, 1536), F32),
            vmem((8, FF), F32),
            vmem((GROUPS, SPOT, PER * SPOT), F32),
            vmem((4, SPOT, PER * SPOT), jnp.int32),
            vmem((6, 8, D), F32),
            vmem((8, FF), F32),
            vmem((8, 1536), F32),
            vmem((GROUPS, SPOT, PER * SPOT), F32),
            vmem((D, 1536), BF16),
            vmem((D, 1536), BF16),
            vmem((D, 1536), BF16),
            vmem((8, 1536), F32),
            vmem((8, 1536), F32),
            vmem((half, 1536), BF16),
            vmem((half, 1536), BF16),
            vmem((half, 1536), BF16),
            vmem((8, 1536), F32),
            vmem((8, 1536), F32),
            vmem((3, part, 1536), BF16),
            vmem((3, part, 1536), BF16),
            vmem((3, part, 1536), BF16),
            vmem((4, 8, 1536), F32),
            vmem((4, 8, 1536), F32),
            vmem((upper + 1, part, 1536), BF16),
            vmem((upper + 1, part, 1536), BF16),
            vmem((upper + 1, part, 1536), BF16),
            vmem((upper + 1, 8, 1536), F32),
            vmem((upper + 1, 8, 1536), F32),
            vmem((3, part, D), BF16),
            vmem((3, part, D), BF16),
            vmem((3, part, D), BF16),
            vmem((4, 8, D), F32),
            vmem((4, 8, D), F32),
            vmem((4, 8, LANES), F32),
            sems((4, 11, 3)),
            sems((3, 3)),
            sems((5, 2, 14 + upper)),
            sems((2, 3)),
            sems((3, max(clips, 2))),
        ],
        compiler_params=pltpu.CompilerParams(
            vmem_limit_bytes=VMEM_LIMIT, collective_id=0, has_side_effects=True
        ),
    )(frames, tok, og, qraw, praw, araw, braw, qvb, table, fc1b, rowp)


def adam_step(weight, gradient, moment, second, factor, rate):
    clipped = gradient * factor
    moment_new = BETA_ONE * moment + (1.0 - BETA_ONE) * clipped
    second_new = BETA_TWO * second + (1.0 - BETA_TWO) * clipped * clipped
    moment_hat = moment_new * (1.0 / (1.0 - BETA_ONE**STEP))
    second_hat = second_new * (1.0 / (1.0 - BETA_TWO**STEP))
    master = weight - rate * (
        moment_hat / (jnp.sqrt(second_hat) + ADAM_EPS) + WEIGHT_DECAY * weight
    )
    return (gradient, moment_new, second_new, master)


def step_kernel(cuts, *refs):
    norm_ref, e1_ref, e2_ref, ep_ref, late_ref, es_ref, ls_ref, one_hbm, two_hbm = refs[:9]
    weights, firsts, seconds = refs[9:17], refs[17:25], refs[25:33]
    gn_ref, one_out, two_out, outs, sems = refs[33], refs[34], refs[35], refs[36:68], refs[68]
    bounce = refs[69:71]
    pulls = [
        pltpu.make_async_copy(one_hbm, bounce[0], sems.at[0]),
        pltpu.make_async_copy(two_hbm, bounce[1], sems.at[1]),
    ]
    pushes = [
        pltpu.make_async_copy(bounce[0], one_out, sems.at[2]),
        pltpu.make_async_copy(bounce[1], two_out, sems.at[3]),
    ]

    @pl.when(pl.program_id(0) == 0)
    def _():
        for pull in pulls:
            pull.start()

    @pl.when(pl.program_id(0) == 1)
    def _():
        for pull, push in zip(pulls, pushes):
            pull.wait()
            push.start()

    norm = norm_ref[0:1, 0:1]
    factor = jnp.minimum(1.0, CLIP_LIMIT / (norm + 1e-06))

    def put(i, gradient, rate, at=(slice(None), slice(None))):
        given = [ref[i][at].reshape(gradient.shape) for ref in (weights, firsts, seconds)]
        values = adam_step(given[0], gradient, given[1], given[2], factor, rate)
        for k in range(4):
            outs[4 * i + k][at] = values[k].reshape(outs[4 * i + k][at].shape)

    width = weights[0].shape[1]
    put(0, late_ref[...].astype(F32), LEARN_RATE, (0, slice(None), slice(None)))
    put(3, ep_ref[...].astype(F32), LEARN_RATE)
    put(4, e1_ref[...].astype(F32), LEARN_RATE)
    put(6, e2_ref[...].astype(F32).T, LEARN_RATE)

    @pl.when(pl.program_id(0) == 0)
    def _():
        gn_ref[...] = norm
        both = jnp.concatenate([ls_ref[0:1, :width], ls_ref[0:1, 2 * LANES : 2 * LANES + width]])
        put(1, both, LEARN_RATE)
        lines = []
        for h in range(PER):
            pieces = []
            for half in range(2):
                at = h * 256 + half * LANES
                pieces.append(ls_ref[1 + at // D : 2 + at // D, at % D : at % D + LANES])
            lines.append(jnp.concatenate(pieces, axis=1))
        lines = jnp.concatenate(lines + [jnp.zeros((8 - PER, 256), F32)])
        offsets = weights[2].shape[1]
        flip = iota((256, 256), 0) + iota((256, 256), 1) == offsets - 1
        flip = jnp.where(flip, 1.0, 0.0).astype(F32).astype(BF16)
        table = None
        for part in split_three(lines):
            term = nn(part, flip)
            table = term if table is None else table + term
        put(2, table[:PER, :offsets], ROW_RATE)
        put(5, es_ref[0:1, :], LEARN_RATE, (slice(None),))
        put(7, jnp.concatenate([ls_ref[4:6, :], es_ref[1:5, :]]), ROW_RATE)

    @pl.when(pl.program_id(0) == cuts - 1)
    def _():
        for push in pushes:
            push.wait()


def take_step(norm, g1, g2, late, esmall, lsmall, one, two, weights, firsts, seconds):
    cuts = 3
    spec = pl.BlockSpec
    full = lambda a: spec(a.shape, lambda i: (0,) * a.ndim)
    third = lambda a: spec(
        (a.shape[0] // cuts,) + a.shape[1:], lambda i: (i,) + (0,) * (a.ndim - 1)
    )
    each = [
        third(a) if k in (0, 3, 4, 6) else full(a) for k, a in enumerate(weights)
    ]
    rows = D // cuts
    tall = weights[3].shape[0] // cuts
    shape = jax.ShapeDtypeStruct
    outs = pl.pallas_call(
        partial(step_kernel, cuts),
        grid=(cuts,),
        in_specs=[
            full(norm),
            spec((rows, D), lambda i: (i, 0)),
            spec((D, rows), lambda i: (0, i)),
            spec((tall, D), lambda i: (cuts * (cuts * tall) // tall + i, 0)),
            spec((cuts * tall, D), lambda i: (i, 0)),
            full(esmall),
            full(lsmall),
            spec(memory_space=pl.ANY),
            spec(memory_space=pl.ANY),
        ]
        + each * 3,
        out_specs=[spec((1, 1), lambda i: (0, 0))]
        + [spec(memory_space=pl.ANY)] * 2
        + [e for e in each for _ in range(4)],
        out_shape=[shape((1, 1), F32), shape(one.shape, F32), shape(two.shape, F32)]
        + [shape(a.shape, F32) for a in weights for _ in range(4)],
        scratch_shapes=[
            pltpu.SemaphoreType.DMA((4,)),
            pltpu.VMEM(one.shape, F32),
            pltpu.VMEM(two.shape, F32),
        ],
        compiler_params=pltpu.CompilerParams(vmem_limit_bytes=VMEM_LIMIT),
    )(norm, g1, g2, late, late, esmall, lsmall, one, two, *weights, *firsts, *seconds)
    return outs[0], outs[1], outs[2], outs[3:]


def shards(
    tokens,
    out_grad,
    clip_frames,
    qkv_weight,
    qv_bias,
    rel_table,
    proj_weight,
    fc1_weight,
    fc1_bias,
    fc2_weight,
    row_params,
    qkv_first,
    qkv_second,
    qvb_first,
    qvb_second,
    table_first,
    table_second,
    proj_first,
    proj_second,
    fc1_first,
    fc1_second,
    fc1b_first,
    fc1b_second,
    fc2_first,
    fc2_second,
    rows_first,
    rows_second,
):
    parts = lambda v: v.transpose(1, 2, 0)
    weights = (
        parts(qkv_weight),
        qv_bias,
        rel_table.T,
        proj_weight,
        fc1_weight,
        fc1_bias,
        fc2_weight,
        row_params,
    )
    firsts = (
        parts(qkv_first),
        qvb_first,
        table_first.T,
        proj_first,
        fc1_first,
        fc1b_first,
        fc2_first,
        rows_first,
    )
    seconds = (
        parts(qkv_second),
        qvb_second,
        table_second.T,
        proj_second,
        fc1_second,
        fc1b_second,
        fc2_second,
        rows_second,
    )
    output, input_grad, g1, g2, late, esmall, lsmall, norm = block(
        clip_frames,
        tokens,
        out_grad,
        weights[0],
        proj_weight,
        fc1_weight,
        fc2_weight,
        qv_bias,
        weights[2],
        fc1_bias,
        row_params,
    )
    grad_norm, output, input_grad, updated = take_step(
        norm, g1, g2, late, esmall, lsmall, output, input_grad, weights, firsts, seconds
    )
    updated = [
        v.transpose(2, 0, 1) if k < 4 else v.T if 8 <= k < 12 else v for k, v in enumerate(updated)
    ]
    return (output, input_grad, grad_norm.reshape(()), *updated)


def solution(mesh):
    rows = P(("win", "head"), None)
    last3, last2, first2, first1 = P(None, None, "head"), P(None, "head"), P("head", None), P("head")
    each = (last3, last2, last2, first2, last2, first1, first2, P())
    return jax.shard_map(
        shards,
        mesh=mesh,
        in_specs=(rows, rows, P("win")) + each + tuple(s for s in each for _ in range(2)),
        out_specs=(rows, rows, P()) + tuple(s for s in each for _ in range(4)),
        check_vma=False,
    )
```

```python
from functools import partial

import jax
import jax.numpy as jnp
from jax import lax
from jax.experimental import pallas as pl
from jax.experimental.pallas import tpu as pltpu
from jax.sharding import PartitionSpec as P

D = 384
HDIM = 24
HEADS = 16
GROUPS = 4
PER = 4
LANES = 128
FF = 1536
GRID = 16
WIN = 8
CLIP = GRID * GRID
SPOT = WIN * WIN
SHIFT = 4
STEP = 10
CHUNK = 768
PAIR = 2 * CLIP

NORM_EPS = 1e-05
MASKED = -1000000000.0
CLIP_LIMIT = 1.0
LEARN_RATE = 0.1
ROW_RATE = 0.5
BETA_ONE = 0.9
BETA_TWO = 0.999
ADAM_EPS = 1e-08
WEIGHT_DECAY = 0.01
SCALE = HDIM ** (-0.5)
F32 = jnp.float32
BF16 = jnp.bfloat16
VMEM_LIMIT = 60 * 1024 * 1024


def nn(a, b):
    return lax.dot_general(a, b, (((1,), (0,)), ((), ())), preferred_element_type=F32)


def nt(a, b):
    return lax.dot_general(a, b, (((1,), (1,)), ((), ())), preferred_element_type=F32)


def tn(a, b):
    return lax.dot_general(a, b, (((0,), (0,)), ((), ())), preferred_element_type=F32)


def iota(shape, axis):
    return lax.broadcasted_iota(jnp.int32, shape, axis)


def fold(x):
    return jnp.sum(x.reshape(x.shape[0] // 8, 8, x.shape[1]), axis=0)


def normalize(x):
    center = x - jnp.mean(x, axis=-1, keepdims=True)
    spread = jnp.mean(center * center, axis=-1, keepdims=True)
    inverse = lax.rsqrt(spread + NORM_EPS)
    return center * inverse, inverse


def norm_back(e, n, inverse, gain):
    q = e * gain
    return inverse * (
        q - jnp.mean(q, axis=-1, keepdims=True) - n * jnp.mean(q * n, axis=-1, keepdims=True)
    )


def to_windows(x):
    low = iota((8, x.shape[1]), 0) < 4
    first, second = [], []
    for t in range(GRID):
        a = x[16 * t : 16 * t + 8]
        b = x[16 * t + 8 : 16 * t + 16]
        first.append(pltpu.roll(jnp.where(low, b, a), 4, axis=0))
        second.append(pltpu.roll(jnp.where(low, a, b), 4, axis=0))
    pieces = []
    for wt in range(2):
        for side in (first, second):
            for a in range(WIN):
                pieces.append(side[(wt * WIN + a + SHIFT) % GRID])
    return jnp.concatenate(pieces, axis=0)


def from_windows(y):
    low = iota((8, y.shape[1]), 0) < 4
    pieces = []
    for t in range(GRID):
        rolled = (t - SHIFT) % GRID
        base = (rolled // WIN) * 128 + (rolled % WIN) * 8
        u = pltpu.roll(y[base : base + 8], 4, axis=0)
        v = pltpu.roll(y[base + 64 : base + 72], 4, axis=0)
        pieces.append(jnp.where(low, v, u))
        pieces.append(jnp.where(low, u, v))
    return jnp.concatenate(pieces, axis=0)


def head_masks(dtype):
    lane = iota((16, LANES), 1) // HDIM
    return [jnp.where(lane == h, 1.0, 0.0).astype(F32).astype(dtype) for h in range(PER)]


def stack_heads(x, masks):
    tiles = x.reshape(SPOT // 16, 16, LANES)
    return jnp.concatenate([(tiles * m[None]).reshape(SPOT, LANES) for m in masks], axis=0)


def pick_heads(r):
    lane = iota((SPOT, LANES), 1)
    out = r[3 * SPOT :]
    for h in (2, 1, 0):
        out = jnp.where(lane < (h + 1) * HDIM, r[h * SPOT : (h + 1) * SPOT], out)
    return out


def key_times(wt, wf):
    j = iota((SPOT, PER * SPOT), 0)
    i = iota((SPOT, PER * SPOT), 1) % SPOT
    time = (wt * WIN + j // WIN + SHIFT) % GRID
    same = j >= 0
    if wt:
        same = same & ((j // WIN < 4) == (i // WIN < 4))
    if wf:
        same = same & ((j % WIN < 4) == (i % WIN < 4))
    return jnp.where(same, time, 99)


def split_three(x):
    one = x.astype(BF16)
    rest = x - one.astype(F32)
    two = rest.astype(BF16)
    three = (rest - two.astype(F32)).astype(BF16)
    return one, two, three


def build_bias(table_ref, bias_ref):
    row = iota((256, 256), 0)
    lane = iota((256, 256), 1)
    spot = lane % SPOT
    base = spot // WIN * (2 * WIN - 1) + spot % WIN
    for g in range(GROUPS):
        total = None
        for h in range(PER):
            own = jnp.where((row == base) & (lane // SPOT == h), 1.0, 0.0).astype(F32).astype(BF16)
            line = jnp.broadcast_to(table_ref[g, 1 + h : 2 + h, :256], (8, 256))
            spread = jnp.concatenate(
                [
                    pltpu.roll(line, (15 * a + 144) % 256, axis=1, stride=1, stride_axis=0)
                    for a in range(WIN)
                ],
                axis=0,
            )
            for part in split_three(spread):
                term = nn(part, own)
                total = term if total is None else total + term
        bias_ref[g] = total


def gelu_parts(u):
    bell = jnp.exp(-0.5 * (u * u))
    return 0.5 + 0.5 * lax.erf(u * (0.5**0.5)), bell * 0.3989422804014327


def place(win, head):
    return {"win": win, "head": head}


def remote(src, dst, send, recv, win, head):
    return pltpu.make_async_remote_copy(
        src_ref=src,
        dst_ref=dst,
        send_sem=send,
        recv_sem=recv,
        device_id=place(win, head),
        device_id_type=pl.DeviceIdType.MESH,
    )


def position():
    win, head = lax.axis_index("win"), lax.axis_index("head")
    core, cell = win % 2, (win // 2) % 4
    return win, head, core, cell, win - core - 2 * cell


def greet():
    win, head, core, cell, base = position()
    barrier = pltpu.get_barrier_semaphore()
    peers = [(win, (head + d) % 4) for d in (1, 2, 3)]
    peers += [(base + 2 * ((cell + k % 4) % 4) + (core + k // 4) % 2, head) for k in range(1, 8)]
    for w, h in peers:
        pl.semaphore_signal(barrier, inc=1, device_id=place(w, h), device_id_type=pl.DeviceIdType.MESH)
    pl.semaphore_wait(barrier, len(peers))


def shard_view(ref, wide, head, start, count):
    if wide:
        return ref.at[pl.ds(start, count), pl.ds(pl.multiple_of(head * D, LANES), D)]
    rows = ref.shape[0] // 4
    return ref.at[pl.ds(pl.multiple_of(head * rows + start, 16), count), :]


def gather_stages(rows, full, wide, sems):
    win, head, core, cell, base = position()
    half, part = rows // 2, rows // 8
    mine = pl.multiple_of(core * half + cell * part, 16)
    near = pl.multiple_of(core * half, 16)

    def over_head(d):
        view = shard_view(full, wide, head, mine, part)
        return remote(view, view, sems.at[0, d], sems.at[1, d], win, (head + d + 1) % 4)

    def over_cell(d, c):
        view = shard_view(full, wide, (head + 3 - d) % 4, mine, part)
        peer = base + 2 * ((cell + c + 1) % 4) + core
        return remote(view, view, sems.at[2 + c, d], sems.at[5 + c, d], peer, head)

    def over_core(d):
        view = shard_view(full, wide, (head + 3 - d) % 4, near, half)
        return remote(view, view, sems.at[8, d], sems.at[9, d], win + 1 - 2 * core, head)

    def first():
        for d in range(3):
            over_head(d).start()

    def second():
        for d in range(3):
            over_head(d).wait_recv()
            for c in range(3):
                over_cell(d, c).start()

    def third():
        for d in range(3):
            for c in range(3):
                over_cell(d, c).wait_recv()
            over_core(d).start()

    def last():
        for d in range(3):
            over_core(d).wait_recv()
        for d in range(3):
            over_head(d).wait_send()
            for c in range(3):
                over_cell(d, c).wait_send()
            over_core(d).wait_send()

    return first, second, third, last


def reduce_stages(buf, from_core, from_cell, from_upper, from_head, final, sems):
    win, head, core, cell, base = position()
    rows = buf.shape[0]
    half, part = rows // 2, rows // 8
    near = pl.multiple_of(core * half, 16)
    far = pl.multiple_of((1 - core) * half, 16)
    mine = pl.multiple_of(core * half + cell * part, 16)
    other = win + 1 - 2 * core
    own = pl.ds(mine, part)

    def lanes(h):
        return pl.ds(pl.multiple_of(h * D, LANES), D)

    def to_core():
        return remote(
            buf.at[pl.ds(far, half), :], from_core, sems.at[0, 0], sems.at[1, 0], other, head
        )

    def to_cell(c):
        peer = (cell + c + 1) % 4
        start = pl.multiple_of(core * half + peer * part, 16)
        return remote(
            buf.at[pl.ds(start, part), :],
            from_cell.at[c],
            sems.at[0, 1 + c],
            sems.at[1, 1 + c],
            base + 2 * peer + core,
            head,
        )

    def to_upper(b):
        peer = win + (8 << b) - 2 * (8 << b) * (win // (8 << b) % 2)
        return remote(
            buf.at[own, :], from_upper.at[b], sems.at[0, 14 + b], sems.at[1, 14 + b], peer, head
        )

    def to_head(d):
        peer = (head + d + 1) % 4
        return remote(
            buf.at[own, lanes(peer)],
            from_head.at[d],
            sems.at[0, 4 + d],
            sems.at[1, 4 + d],
            win,
            peer,
        )

    def back(k):
        peer = base + 2 * ((cell + k % 4) % 4) + (core + k // 4) % 2
        view = final.at[own, :]
        return remote(view, view, sems.at[0, 6 + k], sems.at[1, 6 + k], peer, head)

    def first():
        to_core().start()

    def second():
        to_core().wait_recv()
        for k in range(4):
            start = pl.multiple_of(core * half + k * part, 16)
            block = pl.ds(start, part)
            total = buf[block, :].astype(F32) + from_core[k * part : k * part + part].astype(F32)
            buf[block, :] = total.astype(BF16)
        for c in range(3):
            to_cell(c).start()

    def third():
        for c in range(3):
            to_cell(c).wait_recv()
        total = buf[own, :].astype(F32)
        for c in range(3):
            total = total + from_cell[c].astype(F32)
        buf[own, :] = total.astype(BF16)
        for b in range(from_upper.shape[0] - 1):
            to_upper(b).start()
            to_upper(b).wait()
            buf[own, :] = (buf[own, :].astype(F32) + from_upper[b].astype(F32)).astype(BF16)
        for d in range(3):
            to_head(d).start()

    def fourth():
        for d in range(3):
            to_head(d).wait_recv()
        total = buf[own, lanes(head)].astype(F32)
        for d in range(3):
            total = total + from_head[d].astype(F32)
        final[own, :] = total.astype(BF16)
        for k in range(1, 8):
            back(k).start()

    def last():
        for k in range(1, 8):
            back(k).wait_recv()
        to_core().wait_send()
        for c in range(3):
            to_cell(c).wait_send()
            to_head(c).wait_send()
        for k in range(1, 8):
            back(k).wait_send()

    return first, second, third, fourth, last


def small_stages(buf, from_core, cells, from_upper, heads, final, sems):
    win, head, core, cell, base = position()
    other = win + 1 - 2 * core

    def lanes(h):
        return pl.ds(pl.multiple_of(h * D, LANES), D)

    def to_core():
        return remote(buf, from_core, sems.at[0, 0], sems.at[1, 0], other, head)

    def to_cell(c):
        view = cells.at[cell]
        peer = base + 2 * ((cell + c + 1) % 4) + core
        return remote(view, view, sems.at[0, 1 + c], sems.at[1, 1 + c], peer, head)

    def to_upper(b):
        peer = win + (8 << b) - 2 * (8 << b) * (win // (8 << b) % 2)
        return remote(buf, from_upper.at[b], sems.at[0, 14 + b], sems.at[1, 14 + b], peer, head)

    def to_head(d):
        peer = (head + d + 1) % 4
        return remote(
            buf.at[:, lanes(peer)], heads.at[head], sems.at[0, 4 + d], sems.at[1, 4 + d], win, peer
        )

    def first():
        to_core().start()

    def second():
        to_core().wait()
        cells[cell] = buf[...] + from_core[...]
        for c in range(3):
            to_cell(c).start()

    def third():
        for c in range(3):
            to_cell(c).wait()
        buf[...] = (cells[0] + cells[1]) + (cells[2] + cells[3])
        for b in range(from_upper.shape[0] - 1):
            to_upper(b).start()
            to_upper(b).wait()
            buf[...] = buf[...] + from_upper[b]
        heads[head] = buf[:, lanes(head)]
        for d in range(3):
            to_head(d).start()

    def last():
        for d in range(3):
            to_head(d).wait()
        final[...] = (heads[0] + heads[1]) + (heads[2] + heads[3])

    return first, second, third, last


def clip_rows(c, count=CLIP):
    return pl.ds(pl.multiple_of(c * count, count), count)


def block_kernel(
    clips,
    frames_ref,
    tok_hbm,
    og_hbm,
    qraw_ref,
    praw_ref,
    araw_ref,
    braw_ref,
    qvb_ref,
    table_ref,
    fc1b_ref,
    rowp_ref,
    out_hbm,
    din_hbm,
    one_ref,
    two_ref,
    late_ref,
    esmall_ref,
    lsmall_ref,
    norm_ref,
    sown_ref,
    tok_ref,
    og_ref,
    mid_ref,
    dmid_ref,
    n1t_ref,
    n2_ref,
    qkv_ref,
    dj_ref,
    hid_ref,
    probs_ref,
    att_ref,
    wqkv_ref,
    wproj_ref,
    w1_ref,
    w2_ref,
    small_ref,
    bqkv_ref,
    b1_ref,
    bias_ref,
    time_ref,
    rows_ref,
    gb_ref,
    tacc_ref,
    buf_1,
    buf_2,
    lbuf,
    esbuf,
    lsbuf,
    core_1,
    core_2,
    core_l,
    core_es,
    core_ls,
    cell_1,
    cell_2,
    cell_l,
    cell_es,
    cell_ls,
    up_1,
    up_2,
    up_l,
    up_es,
    up_ls,
    head_1,
    head_2,
    head_l,
    head_es,
    head_ls,
    nslots,
    wsems,
    ssems,
    rsems,
    nsems,
    osems,
):
    win, head, core, cell, base = position()
    first_clip = head * clips

    def enter(c, carry):
        for part in range(2):
            rows = clip_rows(2 * c + part)
            n1, _ = normalize(to_windows(tok_ref[rows, :].astype(F32)))
            n1 = (n1 * rowp_ref[0:1] + rowp_ref[1:2]).astype(BF16)
            att_ref[rows, :D] = n1
            n1t_ref[:D, rows] = n1.T
        return carry

    def project(c, carry):
        rows = clip_rows(c, PAIR)
        for part in range(3):
            cols = slice(part * 512, part * 512 + 512)
            y = nt(att_ref[rows, :D], wqkv_ref[cols, :]) + bqkv_ref[0:1, cols]
            qkv_ref[rows, cols] = y.astype(BF16)
        return carry

    def attend(c, carry):
        frames = frames_ref[first_clip + c]
        masks = head_masks(BF16)
        for w in range(4):
            spots = pl.ds(pl.multiple_of(c * CLIP + w * SPOT, SPOT), SPOT)
            for g in range(GROUPS):
                q = qkv_ref[spots, g * D : g * D + LANES]
                k = qkv_ref[spots, g * D + LANES : g * D + 2 * LANES]
                s = nt(k, stack_heads(q, masks)) * SCALE + bias_ref[g]
                s = jnp.where(time_ref[w] < frames, s, MASKED)
                e = jnp.exp(s - jnp.max(s, axis=0, keepdims=True))
                p = (e * (1.0 / jnp.sum(e, axis=0, keepdims=True))).astype(BF16)
                probs_ref[c, w, g] = p
        for w in range(4):
            spots = pl.ds(pl.multiple_of(c * CLIP + w * SPOT, SPOT), SPOT)
            for g in range(GROUPS):
                v = qkv_ref[spots, g * D + 2 * LANES : g * D + D]
                o = pick_heads(tn(probs_ref[c, w, g], v))
                att_ref[spots, g * LANES : g * LANES + LANES] = o.astype(BF16)
        return carry

    def send_out(c):
        rows = clip_rows(c, PAIR)
        return pltpu.make_async_copy(mid_ref.at[rows, :], out_hbm.at[rows, :], osems.at[0, c])

    def widen(c, carry):
        rows = clip_rows(c, PAIR)
        clip = [clip_rows(2 * c + part) for part in range(2)]
        x = jnp.concatenate([to_windows(tok_ref[r, :].astype(F32)) for r in clip], axis=0)
        og = jnp.concatenate([to_windows(og_ref[r, :].astype(F32)) for r in clip], axis=0)
        og_ref[rows, :] = og.astype(BF16)
        rows_ref[5] += fold(og)
        middle = x + nn(att_ref[rows, :], wproj_ref[...]) + rowp_ref[4:5]
        mid_ref[rows, :] = middle
        nrm, _ = normalize(middle)
        n2 = (nrm * rowp_ref[2:3] + rowp_ref[3:4]).astype(BF16)
        n2_ref[rows, :] = n2
        for j in range(FF // CHUNK):
            cols = slice(j * CHUNK, j * CHUNK + CHUNK)
            u = nn(n2, w1_ref[:, cols]) + b1_ref[0:1, cols]
            phi, dens = gelu_parts(u)
            hid_ref[rows, cols] = (u * phi).astype(BF16)
            dj_ref[rows, cols] = (phi + u * dens).astype(BF16)
        return carry

    def narrow_back(c, carry):
        rows = clip_rows(c, PAIR)
        for j in range(FF // CHUNK):
            cols = slice(j * CHUNK, j * CHUNK + CHUNK)
            dh = nt(og_ref[rows, :], w2_ref[cols, :])
            du = (dj_ref[rows, cols].astype(F32) * dh).astype(BF16)
            dj_ref[rows, cols] = du
            gb_ref[:, cols] += fold(du.astype(F32))
        return carry

    def widen_back(c, carry):
        rows = clip_rows(c, PAIR)
        dn2 = nt(dj_ref[rows, :], w1_ref[...])
        nrm, inv = normalize(mid_ref[rows, :])
        dmid = og_ref[rows, :].astype(F32) + norm_back(dn2, nrm, inv, rowp_ref[2:3])
        dmid_ref[rows, :] = dmid
        dbr = dmid.astype(BF16)
        rows_ref[2] += fold(dn2 * nrm)
        rows_ref[3] += fold(dn2)
        rows_ref[4] += fold(dbr.astype(F32))
        og_ref[rows, :] = dbr
        return carry

    def narrow(c, carry):
        rows = clip_rows(c, PAIR)
        result = mid_ref[rows, :] + nn(hid_ref[rows, :], w2_ref[...]) + rowp_ref[5:6]
        for part in range(2):
            result_part = from_windows(result[part * CLIP : part * CLIP + CLIP])
            mid_ref[clip_rows(2 * c + part), :] = result_part
        send_out(c).start()
        return carry

    def wide_grads(buf, given, back):
        for j in range(FF // 512):
            cols = slice(j * 512, j * 512 + 512)
            buf[:, cols] = tn(given[...], back[:, cols]).astype(BF16)

    def branch_grads():
        width = praw_ref.shape[0]
        for g in range(GROUPS):
            part = tn(att_ref[:, g * LANES : g * LANES + LANES], og_ref[...])
            lbuf[3 * width :, g * D : g * D + D] = part[:width].astype(BF16)
        for j in range(clips // 2):
            r = slice(j * PAIR, j * PAIR + PAIR)
            att_ref[r, :] = nt(og_ref[r, :], wproj_ref[...]).astype(BF16)

    def qkv_grads():
        width = praw_ref.shape[0]
        for j in range(3):
            value = nn(n1t_ref[...], dj_ref[:, j * 512 : j * 512 + 512])
            for k in range(4):
                g, p = (4 * j + k) // 3, (4 * j + k) % 3
                turned = value[:D, k * LANES : k * LANES + LANES].T
                if p != 1:
                    cols = slice(g * D + p * LANES, g * D + p * LANES + LANES)
                    lsbuf[0:1, cols] = value[D : D + 1, k * LANES : k * LANES + LANES]
                lbuf[p * width : p * width + width, g * D : g * D + D] = turned[:width].astype(BF16)

    def attend_back(c, carry):
        rows = clip_rows(c)
        frames = frames_ref[first_clip + c]
        masks = head_masks(BF16)
        for g in range(GROUPS):
            tacc = None
            for w in range(4):
                spots = pl.ds(pl.multiple_of(c * CLIP + w * SPOT, SPOT), SPOT)
                v = qkv_ref[spots, g * D + 2 * LANES : g * D + D]
                do = stack_heads(att_ref[spots, g * LANES : g * LANES + LANES], masks)
                p = probs_ref[c, w, g]
                pf = p.astype(F32)
                dp = nt(v, do)
                inner = jnp.sum(pf * dp, axis=0, keepdims=True)
                ds = jnp.where(time_ref[w] < frames, pf * (dp - inner), 0.0)
                tacc = ds if tacc is None else tacc + ds
                probs_ref[c, w, g] = ds.astype(BF16)
                dj_ref[spots, g * D + 2 * LANES : g * D + D] = nn(p, do).astype(BF16)
            tacc_ref[g] += tacc
        for g in range(GROUPS):
            for w in range(4):
                spots = pl.ds(pl.multiple_of(c * CLIP + w * SPOT, SPOT), SPOT)
                cq = slice(g * D, g * D + LANES)
                ck = slice(g * D + LANES, g * D + 2 * LANES)
                q = qkv_ref[spots, cq]
                k = qkv_ref[spots, ck]
                ds = probs_ref[c, w, g]
                dj_ref[spots, cq] = (pick_heads(tn(ds, k)) * SCALE).astype(BF16)
                dj_ref[spots, ck] = (nn(ds, stack_heads(q, masks)) * SCALE).astype(BF16)
        return carry

    def entry_back(c, carry):
        rows = clip_rows(c, PAIR)
        clip = [clip_rows(2 * c + part) for part in range(2)]
        x = jnp.concatenate([to_windows(tok_ref[r, :].astype(F32)) for r in clip], axis=0)
        n, inv = normalize(x)
        dn1 = nn(dj_ref[rows, :], wqkv_ref[...])
        rows_ref[0] += fold(dn1 * n)
        rows_ref[1] += fold(dn1)
        din = dmid_ref[rows, :] + norm_back(dn1, n, inv, rowp_ref[0:1])
        for part in range(2):
            r = clip[part]
            dmid_ref[r, :] = from_windows(din[part * CLIP : part * CLIP + CLIP])
        pltpu.make_async_copy(dmid_ref.at[rows, :], din_hbm.at[rows, :], osems.at[1, c]).start()
        return carry

    load_tok = pltpu.make_async_copy(tok_hbm, tok_ref, osems.at[2, 0])
    load_og = pltpu.make_async_copy(og_hbm, og_ref, osems.at[2, 1])
    load_tok.start()
    load_og.start()
    small = [
        remote(sown_ref, small_ref.at[head], ssems.at[0, d], ssems.at[1, d], win, (head + d + 1) % 4)
        for d in range(3)
    ]
    own_small = pltpu.make_async_copy(sown_ref, small_ref.at[head], ssems.at[2, 0])
    gq_w = gather_stages(D, wqkv_ref, False, wsems.at[0])
    others = [
        gather_stages(rows, full, wide, wsems.at[1 + i])
        for i, (rows, full, wide) in enumerate(
            ((LANES, wproj_ref, False), (D, w1_ref, True), (D, w2_ref, False))
        )
    ]
    for p in range(3):
        part = qraw_ref[p]
        part = jnp.concatenate([part, jnp.zeros((LANES - part.shape[0], D), F32)], axis=0)
        start = pl.multiple_of(head * D + p * LANES, LANES)
        wqkv_ref[pl.ds(start, LANES), :] = part.astype(BF16)
    greet()
    gq_w[0]()
    width = qvb_ref.shape[1]
    sown_ref[...] = jnp.zeros_like(sown_ref)
    sown_ref[0:1, :width] = qvb_ref[0:1, :]
    sown_ref[0:1, LANES : LANES + width] = qvb_ref[1:2, :]
    sown_ref[1 : 1 + PER, : table_ref.shape[1]] = table_ref[...]
    sown_ref[5:6, :] = fc1b_ref[...].reshape(1, D)
    own_small.start()
    for copy in small:
        copy.start()
    width = praw_ref.shape[0]
    tall = jnp.concatenate([praw_ref[...], jnp.zeros((LANES - width, D), F32)])
    wproj_ref[pl.ds(pl.multiple_of(head * LANES, LANES), LANES), :] = tall.astype(BF16)
    shard = pl.ds(pl.multiple_of(head * D, LANES), D)
    w1_ref[:, shard] = araw_ref[...].astype(BF16)
    w2_ref[shard, :] = braw_ref[...].astype(BF16)
    for k in others:
        k[0]()
    for wt in range(2):
        for wf in range(2):
            time_ref[wt * 2 + wf] = key_times(wt, wf)
    for ref in (rows_ref, gb_ref, tacc_ref, esbuf, lsbuf):
        ref[...] = jnp.zeros_like(ref)
    n1t_ref[D:, :] = jnp.ones((16, n1t_ref.shape[1]), F32).astype(BF16)
    load_tok.wait()
    lax.fori_loop(0, clips // 2, enter, 0)
    gq_w[1]()
    own_small.wait()
    for copy in small:
        copy.wait()
    for g in range(4):
        bqkv_ref[0:1, g * D : g * D + LANES] = small_ref[g, 0:1, :LANES]
        bqkv_ref[0:1, g * D + LANES : g * D + 2 * LANES] = jnp.zeros((1, LANES), F32)
        bqkv_ref[0:1, g * D + 2 * LANES : g * D + D] = small_ref[g, 0:1, LANES : 2 * LANES]
        b1_ref[0:1, g * D : g * D + D] = small_ref[g, 5:6, :]
    build_bias(small_ref, bias_ref)
    gq_w[2]()
    gq_w[3]()
    others[0][1]()
    others[1][1]()

    def span(share):
        return clips * share // 8

    lax.fori_loop(0, clips // 2, project, 0)
    others[2][1]()
    lax.fori_loop(0, span(4), attend, 0)
    others[0][2]()
    others[1][2]()
    lax.fori_loop(span(4), span(8), attend, 0)
    others[0][3]()
    others[1][3]()
    load_og.wait()
    lax.fori_loop(0, span(4) // 2, widen, 0)
    others[2][2]()
    lax.fori_loop(span(4) // 2, clips // 2, widen, 0)
    others[2][3]()
    one = reduce_stages(buf_1, core_1, cell_1, up_1, head_1, one_ref, rsems.at[0])
    two = reduce_stages(buf_2, core_2, cell_2, up_2, head_2, two_ref, rsems.at[1])
    late = reduce_stages(lbuf, core_l, cell_l, up_l, head_l, late_ref, rsems.at[2])
    early_small = small_stages(esbuf, core_es, cell_es, up_es, head_es, esmall_ref, rsems.at[3])
    late_small = small_stages(lsbuf, core_ls, cell_ls, up_ls, head_ls, lsmall_ref, rsems.at[4])
    wide_grads(buf_2, og_ref, hid_ref)
    two[0]()
    lax.fori_loop(0, span(4) // 2, narrow_back, 0)
    two[1]()
    lax.fori_loop(span(4) // 2, clips // 2, narrow_back, 0)
    wide_grads(buf_1, n2_ref, dj_ref)
    one[0]()
    lax.fori_loop(0, span(4) // 2, widen_back, 0)
    one[1]()
    two[2]()
    lax.fori_loop(span(4) // 2, clips // 2, widen_back, 0)
    branch_grads()
    two[3]()
    esbuf[0:1, :] = jnp.sum(gb_ref[...], axis=0, keepdims=True)
    for r in range(4):
        line = jnp.sum(rows_ref[2 + r], axis=0, keepdims=True)
        for g in range(GROUPS):
            esbuf[1 + r : 2 + r, g * D : g * D + D] = line
    early_small[0]()
    lax.fori_loop(0, span(2), attend_back, 0)
    one[2]()
    early_small[1]()
    lax.fori_loop(span(2), span(5), attend_back, 0)
    two[4]()
    one[3]()
    early_small[2]()
    lax.fori_loop(span(5), span(8), attend_back, 0)
    qkv_grads()
    late[0]()
    one[4]()
    early_small[3]()
    fold_table(tacc_ref, lsbuf)
    late[1]()
    lax.fori_loop(0, clips // 2, entry_back, 0)
    for r in range(2):
        line = jnp.sum(rows_ref[r], axis=0, keepdims=True)
        for g in range(GROUPS):
            lsbuf[4 + r : 5 + r, g * D : g * D + D] = line
    late_small[0]()
    late[2]()
    lax.fori_loop(0, span(4) // 2, narrow, 0)
    late_small[1]()
    lax.fori_loop(span(4) // 2, clips // 2, narrow, 0)
    late[3]()
    late_small[2]()
    square = jnp.zeros((8, D), F32)
    for ref in (one_ref, two_ref):
        value = ref[...].astype(F32)
        square = square + fold(value * value)
    late_small[3]()
    late[4]()
    value = late_ref[...].astype(F32)
    square = square + fold(value * value)
    es, ls = esmall_ref[...], lsmall_ref[...]
    row = iota((8, D), 0)
    square = square + jnp.where(row < 1, es * es, 0.0) + jnp.where(row < 4, ls * ls, 0.0)
    common = jnp.where((row >= 1) & (row < 5), es * es, 0.0)
    common = common + jnp.where((row >= 4) & (row < 6), ls * ls, 0.0)
    nslots[head] = jnp.broadcast_to(jnp.sum(square, keepdims=True), (8, LANES))
    sends = [
        remote(
            nslots.at[head], nslots.at[head], nsems.at[0, d], nsems.at[1, d], win, (head + d + 1) % 4
        )
        for d in range(3)
    ]
    for copy in sends:
        copy.start()
    for copy in sends:
        copy.wait()
    total = (nslots[0] + nslots[1]) + (nslots[2] + nslots[3])
    norm_ref[...] = jnp.sqrt(total + jnp.sum(common, keepdims=True))

    def finish(c, carry):
        rows = clip_rows(c, PAIR)
        send_out(c).wait()
        pltpu.make_async_copy(dmid_ref.at[rows, :], din_hbm.at[rows, :], osems.at[1, c]).wait()
        return carry

    lax.fori_loop(0, clips // 2, finish, 0)


def fold_table(tacc_ref, lsbuf):
    row = iota((256, 256), 0)
    lane = iota((256, 256), 1)
    spot = row % SPOT
    base = 112 - (spot // WIN * (2 * WIN - 1) + spot % WIN)
    for h in range(PER):
        own = jnp.where((lane == base) & (row // SPOT == h), 1.0, 0.0).astype(F32).astype(BF16)
        for g in range(GROUPS):
            spread = None
            for part in split_three(tacc_ref[g]):
                term = nn(part, own)
                spread = term if spread is None else spread + term
            total = None
            for a in range(WIN):
                piece = pltpu.roll(
                    spread[a * 8 : a * 8 + 8], 15 * a, axis=1, stride=1, stride_axis=0
                )
                total = piece if total is None else total + piece
            line = jnp.sum(total, axis=0, keepdims=True)
            for half in range(2):
                at = h * 256 + half * LANES
                lsbuf[1 + at // D : 2 + at // D, g * D + at % D : g * D + at % D + LANES] = line[
                    :, half * LANES : half * LANES + LANES
                ]


def block(frames, tok, og, qraw, praw, araw, braw, qvb, table, fc1b, rowp):
    rows = tok.shape[0]
    clips = rows // CLIP
    upper = max(lax.axis_size("win") // 8, 1).bit_length() - 1
    shape = jax.ShapeDtypeStruct
    sems = pltpu.SemaphoreType.DMA
    vmem = pltpu.VMEM
    spec = pl.BlockSpec
    inside = lambda: spec(memory_space=vmem)
    outside = lambda: spec(memory_space=pl.ANY)
    half, part = D // 2, D // 8
    return pl.pallas_call(
        partial(block_kernel, clips),
        in_specs=[spec(memory_space=pltpu.SMEM), outside(), outside()] + [inside()] * 8,
        out_specs=[outside(), outside()] + [inside()] * 6,
        out_shape=[
            shape((rows, D), F32),
            shape((rows, D), F32),
            shape((D, D), BF16),
            shape((D, D), BF16),
            shape((D, D), BF16),
            shape((8, D), F32),
            shape((8, D), F32),
            shape((8, LANES), F32),
        ],
        scratch_shapes=[
            vmem((8, D), F32),
            vmem((rows, D), BF16),
            vmem((rows, D), BF16),
            vmem((rows, D), F32),
            vmem((rows, D), F32),
            vmem((D + 16, rows), BF16),
            vmem((rows, D), BF16),
            vmem((rows, 1536), BF16),
            vmem((rows, 1536), BF16),
            vmem((rows, FF), BF16),
            vmem((clips, 4, GROUPS, SPOT, PER * SPOT), BF16),
            vmem((rows, 512), BF16),
            vmem((1536, D), BF16),
            vmem((512, D), BF16),
            vmem((D, FF), BF16),
            vmem((FF, D), BF16),
            vmem((GROUPS, 8, D), F32),
            vmem((8, 1536), F32),
            vmem((8, FF), F32),
            vmem((GROUPS, SPOT, PER * SPOT), F32),
            vmem((4, SPOT, PER * SPOT), jnp.int32),
            vmem((6, 8, D), F32),
            vmem((8, FF), F32),
            vmem((GROUPS, SPOT, PER * SPOT), F32),
            vmem((D, 1536), BF16),
            vmem((D, 1536), BF16),
            vmem((D, 1536), BF16),
            vmem((8, 1536), F32),
            vmem((8, 1536), F32),
            vmem((half, 1536), BF16),
            vmem((half, 1536), BF16),
            vmem((half, 1536), BF16),
            vmem((8, 1536), F32),
            vmem((8, 1536), F32),
            vmem((3, part, 1536), BF16),
            vmem((3, part, 1536), BF16),
            vmem((3, part, 1536), BF16),
            vmem((4, 8, 1536), F32),
            vmem((4, 8, 1536), F32),
            vmem((upper + 1, part, 1536), BF16),
            vmem((upper + 1, part, 1536), BF16),
            vmem((upper + 1, part, 1536), BF16),
            vmem((upper + 1, 8, 1536), F32),
            vmem((upper + 1, 8, 1536), F32),
            vmem((3, part, D), BF16),
            vmem((3, part, D), BF16),
            vmem((3, part, D), BF16),
            vmem((4, 8, D), F32),
            vmem((4, 8, D), F32),
            vmem((4, 8, LANES), F32),
            sems((4, 11, 3)),
            sems((3, 3)),
            sems((5, 2, 14 + upper)),
            sems((2, 3)),
            sems((3, max(clips, 2))),
        ],
        compiler_params=pltpu.CompilerParams(
            vmem_limit_bytes=VMEM_LIMIT, collective_id=0, has_side_effects=True
        ),
    )(frames, tok, og, qraw, praw, araw, braw, qvb, table, fc1b, rowp)


def adam_step(weight, gradient, moment, second, factor, rate):
    clipped = gradient * factor
    moment_new = BETA_ONE * moment + (1.0 - BETA_ONE) * clipped
    second_new = BETA_TWO * second + (1.0 - BETA_TWO) * clipped * clipped
    moment_hat = moment_new * (1.0 / (1.0 - BETA_ONE**STEP))
    second_hat = second_new * (1.0 / (1.0 - BETA_TWO**STEP))
    master = weight - rate * (
        moment_hat / (jnp.sqrt(second_hat) + ADAM_EPS) + WEIGHT_DECAY * weight
    )
    return (gradient, moment_new, second_new, master)


def step_kernel(cuts, *refs):
    norm_ref, e1_ref, e2_ref, ep_ref, late_ref, es_ref, ls_ref, one_hbm, two_hbm = refs[:9]
    weights, firsts, seconds = refs[9:17], refs[17:25], refs[25:33]
    gn_ref, one_out, two_out, outs, sems = refs[33], refs[34], refs[35], refs[36:68], refs[68]
    bounce = refs[69:71]
    pulls = [
        pltpu.make_async_copy(one_hbm, bounce[0], sems.at[0]),
        pltpu.make_async_copy(two_hbm, bounce[1], sems.at[1]),
    ]
    pushes = [
        pltpu.make_async_copy(bounce[0], one_out, sems.at[2]),
        pltpu.make_async_copy(bounce[1], two_out, sems.at[3]),
    ]

    @pl.when(pl.program_id(0) == 0)
    def _():
        for pull in pulls:
            pull.start()

    @pl.when(pl.program_id(0) == 1)
    def _():
        for pull, push in zip(pulls, pushes):
            pull.wait()
            push.start()

    norm = norm_ref[0:1, 0:1]
    factor = jnp.minimum(1.0, CLIP_LIMIT / (norm + 1e-06))

    def put(i, gradient, rate, at=(slice(None), slice(None))):
        given = [ref[i][at].reshape(gradient.shape) for ref in (weights, firsts, seconds)]
        values = adam_step(given[0], gradient, given[1], given[2], factor, rate)
        for k in range(4):
            outs[4 * i + k][at] = values[k].reshape(outs[4 * i + k][at].shape)

    width = weights[0].shape[1]
    put(0, late_ref[...].astype(F32), LEARN_RATE, (0, slice(None), slice(None)))
    put(3, ep_ref[...].astype(F32), LEARN_RATE)
    put(4, e1_ref[...].astype(F32), LEARN_RATE)
    put(6, e2_ref[...].astype(F32).T, LEARN_RATE)

    @pl.when(pl.program_id(0) == 0)
    def _():
        gn_ref[...] = norm
        both = jnp.concatenate([ls_ref[0:1, :width], ls_ref[0:1, 2 * LANES : 2 * LANES + width]])
        put(1, both, LEARN_RATE)
        lines = []
        for h in range(PER):
            pieces = []
            for half in range(2):
                at = h * 256 + half * LANES
                pieces.append(ls_ref[1 + at // D : 2 + at // D, at % D : at % D + LANES])
            lines.append(jnp.concatenate(pieces, axis=1))
        lines = jnp.concatenate(lines + [jnp.zeros((8 - PER, 256), F32)])
        offsets = weights[2].shape[1]
        flip = iota((256, 256), 0) + iota((256, 256), 1) == offsets - 1
        flip = jnp.where(flip, 1.0, 0.0).astype(F32).astype(BF16)
        table = None
        for part in split_three(lines):
            term = nn(part, flip)
            table = term if table is None else table + term
        put(2, table[:PER, :offsets], ROW_RATE)
        put(5, es_ref[0:1, :], LEARN_RATE, (slice(None),))
        put(7, jnp.concatenate([ls_ref[4:6, :], es_ref[1:5, :]]), ROW_RATE)

    @pl.when(pl.program_id(0) == cuts - 1)
    def _():
        for push in pushes:
            push.wait()


def take_step(norm, g1, g2, late, esmall, lsmall, one, two, weights, firsts, seconds):
    cuts = 3
    spec = pl.BlockSpec
    full = lambda a: spec(a.shape, lambda i: (0,) * a.ndim)
    third = lambda a: spec(
        (a.shape[0] // cuts,) + a.shape[1:], lambda i: (i,) + (0,) * (a.ndim - 1)
    )
    each = [
        third(a) if k in (0, 3, 4, 6) else full(a) for k, a in enumerate(weights)
    ]
    rows = D // cuts
    tall = weights[3].shape[0] // cuts
    shape = jax.ShapeDtypeStruct
    outs = pl.pallas_call(
        partial(step_kernel, cuts),
        grid=(cuts,),
        in_specs=[
            full(norm),
            spec((rows, D), lambda i: (i, 0)),
            spec((D, rows), lambda i: (0, i)),
            spec((tall, D), lambda i: (cuts * (cuts * tall) // tall + i, 0)),
            spec((cuts * tall, D), lambda i: (i, 0)),
            full(esmall),
            full(lsmall),
            spec(memory_space=pl.ANY),
            spec(memory_space=pl.ANY),
        ]
        + each * 3,
        out_specs=[spec((1, 1), lambda i: (0, 0))]
        + [spec(memory_space=pl.ANY)] * 2
        + [e for e in each for _ in range(4)],
        out_shape=[shape((1, 1), F32), shape(one.shape, F32), shape(two.shape, F32)]
        + [shape(a.shape, F32) for a in weights for _ in range(4)],
        scratch_shapes=[
            pltpu.SemaphoreType.DMA((4,)),
            pltpu.VMEM(one.shape, F32),
            pltpu.VMEM(two.shape, F32),
        ],
        compiler_params=pltpu.CompilerParams(vmem_limit_bytes=VMEM_LIMIT),
    )(norm, g1, g2, late, late, esmall, lsmall, one, two, *weights, *firsts, *seconds)
    return outs[0], outs[1], outs[2], outs[3:]


def shards(
    tokens,
    out_grad,
    clip_frames,
    qkv_weight,
    qv_bias,
    rel_table,
    proj_weight,
    fc1_weight,
    fc1_bias,
    fc2_weight,
    row_params,
    qkv_first,
    qkv_second,
    qvb_first,
    qvb_second,
    table_first,
    table_second,
    proj_first,
    proj_second,
    fc1_first,
    fc1_second,
    fc1b_first,
    fc1b_second,
    fc2_first,
    fc2_second,
    rows_first,
    rows_second,
):
    parts = lambda v: v.transpose(1, 2, 0)
    weights = (
        parts(qkv_weight),
        qv_bias,
        rel_table.T,
        proj_weight,
        fc1_weight,
        fc1_bias,
        fc2_weight,
        row_params,
    )
    firsts = (
        parts(qkv_first),
        qvb_first,
        table_first.T,
        proj_first,
        fc1_first,
        fc1b_first,
        fc2_first,
        rows_first,
    )
    seconds = (
        parts(qkv_second),
        qvb_second,
        table_second.T,
        proj_second,
        fc1_second,
        fc1b_second,
        fc2_second,
        rows_second,
    )
    output, input_grad, g1, g2, late, esmall, lsmall, norm = block(
        clip_frames,
        tokens,
        out_grad,
        weights[0],
        proj_weight,
        fc1_weight,
        fc2_weight,
        qv_bias,
        weights[2],
        fc1_bias,
        row_params,
    )
    grad_norm, output, input_grad, updated = take_step(
        norm, g1, g2, late, esmall, lsmall, output, input_grad, weights, firsts, seconds
    )
    updated = [
        v.transpose(2, 0, 1) if k < 4 else v.T if 8 <= k < 12 else v for k, v in enumerate(updated)
    ]
    return (output, input_grad, grad_norm.reshape(()), *updated)


def solution(mesh):
    rows = P(("win", "head"), None)
    last3, last2, first2, first1 = P(None, None, "head"), P(None, "head"), P("head", None), P("head")
    each = (last3, last2, last2, first2, last2, first1, first2, P())
    return jax.shard_map(
        shards,
        mesh=mesh,
        in_specs=(rows, rows, P("win")) + each + tuple(s for s in each for _ in range(2)),
        out_specs=(rows, rows, P()) + tuple(s for s in each for _ in range(4)),
        check_vma=False,
    )
```

```python
from functools import partial

import jax
import jax.numpy as jnp
from jax import lax
from jax.experimental import pallas as pl
from jax.experimental.pallas import tpu as pltpu
from jax.sharding import PartitionSpec as P

D = 384
HDIM = 24
HEADS = 16
GROUPS = 4
PER = 4
LANES = 128
FF = 1536
GRID = 16
WIN = 8
CLIP = GRID * GRID
SPOT = WIN * WIN
SHIFT = 4
STEP = 10
CHUNK = 768
PAIR = 2 * CLIP

NORM_EPS = 1e-05
MASKED = -1000000000.0
CLIP_LIMIT = 1.0
LEARN_RATE = 0.1
ROW_RATE = 0.5
BETA_ONE = 0.9
BETA_TWO = 0.999
ADAM_EPS = 1e-08
WEIGHT_DECAY = 0.01
SCALE = HDIM ** (-0.5)
F32 = jnp.float32
BF16 = jnp.bfloat16
VMEM_LIMIT = 50 * 1024 * 1024
TAIL_LIMIT = 30 * 1024 * 1024


def nn(a, b):
    return lax.dot_general(a, b, (((1,), (0,)), ((), ())), preferred_element_type=F32)


def nt(a, b):
    return lax.dot_general(a, b, (((1,), (1,)), ((), ())), preferred_element_type=F32)


def tn(a, b):
    return lax.dot_general(a, b, (((0,), (0,)), ((), ())), preferred_element_type=F32)


def iota(shape, axis):
    return lax.broadcasted_iota(jnp.int32, shape, axis)


def fold(x):
    return jnp.sum(x.reshape(x.shape[0] // 8, 8, x.shape[1]), axis=0)


def normalize(x):
    center = x - jnp.mean(x, axis=-1, keepdims=True)
    spread = jnp.mean(center * center, axis=-1, keepdims=True)
    inverse = lax.rsqrt(spread + NORM_EPS)
    return center * inverse, inverse


def norm_back(e, n, inverse, gain):
    q = e * gain
    return inverse * (
        q - jnp.mean(q, axis=-1, keepdims=True) - n * jnp.mean(q * n, axis=-1, keepdims=True)
    )


def to_windows(x):
    low = iota((8, x.shape[1]), 0) < 4
    first, second = [], []
    for t in range(GRID):
        a = x[16 * t : 16 * t + 8]
        b = x[16 * t + 8 : 16 * t + 16]
        first.append(pltpu.roll(jnp.where(low, b, a), 4, axis=0))
        second.append(pltpu.roll(jnp.where(low, a, b), 4, axis=0))
    pieces = []
    for wt in range(2):
        for side in (first, second):
            for a in range(WIN):
                pieces.append(side[(wt * WIN + a + SHIFT) % GRID])
    return jnp.concatenate(pieces, axis=0)


def from_windows(y):
    low = iota((8, y.shape[1]), 0) < 4
    pieces = []
    for t in range(GRID):
        rolled = (t - SHIFT) % GRID
        base = (rolled // WIN) * 128 + (rolled % WIN) * 8
        u = pltpu.roll(y[base : base + 8], 4, axis=0)
        v = pltpu.roll(y[base + 64 : base + 72], 4, axis=0)
        pieces.append(jnp.where(low, v, u))
        pieces.append(jnp.where(low, u, v))
    return jnp.concatenate(pieces, axis=0)


def head_masks(dtype):
    lane = iota((16, LANES), 1) // HDIM
    return [jnp.where(lane == h, 1.0, 0.0).astype(F32).astype(dtype) for h in range(PER)]


def stack_heads(x, masks):
    tiles = x.reshape(SPOT // 16, 16, LANES)
    return jnp.concatenate([(tiles * m[None]).reshape(SPOT, LANES) for m in masks], axis=0)


def pick_heads(r):
    lane = iota((SPOT, LANES), 1)
    out = r[3 * SPOT :]
    for h in (2, 1, 0):
        out = jnp.where(lane < (h + 1) * HDIM, r[h * SPOT : (h + 1) * SPOT], out)
    return out


def key_times(wt, wf):
    j = iota((SPOT, PER * SPOT), 0)
    i = iota((SPOT, PER * SPOT), 1) % SPOT
    time = (wt * WIN + j // WIN + SHIFT) % GRID
    same = j >= 0
    if wt:
        same = same & ((j // WIN < 4) == (i // WIN < 4))
    if wf:
        same = same & ((j % WIN < 4) == (i % WIN < 4))
    return jnp.where(same, time, 99)


def split_three(x):
    one = x.astype(BF16)
    rest = x - one.astype(F32)
    two = rest.astype(BF16)
    three = (rest - two.astype(F32)).astype(BF16)
    return one, two, three


def build_bias(table_ref, bias_ref):
    row = iota((256, 256), 0)
    lane = iota((256, 256), 1)
    spot = lane % SPOT
    base = spot // WIN * (2 * WIN - 1) + spot % WIN
    for g in range(GROUPS):
        total = None
        for h in range(PER):
            own = jnp.where((row == base) & (lane // SPOT == h), 1.0, 0.0).astype(F32).astype(BF16)
            line = jnp.broadcast_to(table_ref[g, 1 + h : 2 + h, :256], (8, 256))
            spread = jnp.concatenate(
                [
                    pltpu.roll(line, (15 * a + 144) % 256, axis=1, stride=1, stride_axis=0)
                    for a in range(WIN)
                ],
                axis=0,
            )
            for part in split_three(spread):
                term = nn(part, own)
                total = term if total is None else total + term
        bias_ref[g] = total


def gelu_parts(u):
    bell = jnp.exp(-0.5 * (u * u))
    return 0.5 + 0.5 * lax.erf(u * (0.5**0.5)), bell * 0.3989422804014327


def place(win, head):
    return {"win": win, "head": head}


def remote(src, dst, send, recv, win, head):
    return pltpu.make_async_remote_copy(
        src_ref=src,
        dst_ref=dst,
        send_sem=send,
        recv_sem=recv,
        device_id=place(win, head),
        device_id_type=pl.DeviceIdType.MESH,
    )


def position():
    win, head = lax.axis_index("win"), lax.axis_index("head")
    core, cell = win % 2, (win // 2) % 4
    return win, head, core, cell, win - core - 2 * cell


def greet():
    win, head, core, cell, base = position()
    barrier = pltpu.get_barrier_semaphore()
    peers = [(win, (head + d) % 4) for d in (1, 2, 3)]
    peers += [(base + 2 * ((cell + k % 4) % 4) + (core + k // 4) % 2, head) for k in range(1, 8)]
    for w, h in peers:
        pl.semaphore_signal(barrier, inc=1, device_id=place(w, h), device_id_type=pl.DeviceIdType.MESH)
    return lambda: pl.semaphore_wait(barrier, len(peers))


def shard_view(ref, wide, head, start, count):
    if wide:
        return ref.at[pl.ds(start, count), pl.ds(pl.multiple_of(head * D, LANES), D)]
    rows = ref.shape[0] // 4
    return ref.at[pl.ds(pl.multiple_of(head * rows + start, 16), count), :]


def gather_stages(rows, full, wide, sems):
    win, head, core, cell, base = position()
    half, part = rows // 2, rows // 8
    mine = pl.multiple_of(core * half + cell * part, 16)
    near = pl.multiple_of(core * half, 16)

    def over_head(d):
        view = shard_view(full, wide, head, mine, part)
        return remote(view, view, sems.at[0, d], sems.at[1, d], win, (head + d + 1) % 4)

    def over_cell(d, c):
        view = shard_view(full, wide, (head + 3 - d) % 4, mine, part)
        peer = base + 2 * ((cell + c + 1) % 4) + core
        return remote(view, view, sems.at[2 + c, d], sems.at[5 + c, d], peer, head)

    def over_core(d):
        view = shard_view(full, wide, (head + 3 - d) % 4, near, half)
        return remote(view, view, sems.at[8, d], sems.at[9, d], win + 1 - 2 * core, head)

    def first():
        for d in range(3):
            over_head(d).start()

    def second():
        for d in range(3):
            over_head(d).wait_recv()
            for c in range(3):
                over_cell(d, c).start()

    def third():
        for d in range(3):
            for c in range(3):
                over_cell(d, c).wait_recv()
            over_core(d).start()

    def last():
        for d in range(3):
            over_core(d).wait_recv()
        for d in range(3):
            over_head(d).wait_send()
            for c in range(3):
                over_cell(d, c).wait_send()
            over_core(d).wait_send()

    return first, second, third, last


def reduce_stages(buf, from_core, from_cell, from_upper, from_head, final, sems):
    win, head, core, cell, base = position()
    rows = buf.shape[0]
    half, part = rows // 2, rows // 8
    near = pl.multiple_of(core * half, 16)
    far = pl.multiple_of((1 - core) * half, 16)
    mine = pl.multiple_of(core * half + cell * part, 16)
    other = win + 1 - 2 * core
    own = pl.ds(mine, part)

    def lanes(h):
        return pl.ds(pl.multiple_of(h * D, LANES), D)

    def to_core():
        return remote(
            buf.at[pl.ds(far, half), :], from_core, sems.at[0, 0], sems.at[1, 0], other, head
        )

    def to_cell(c):
        peer = (cell + c + 1) % 4
        start = pl.multiple_of(core * half + peer * part, 16)
        return remote(
            buf.at[pl.ds(start, part), :],
            from_cell.at[c],
            sems.at[0, 1 + c],
            sems.at[1, 1 + c],
            base + 2 * peer + core,
            head,
        )

    def to_upper(b):
        peer = win + (8 << b) - 2 * (8 << b) * (win // (8 << b) % 2)
        return remote(
            buf.at[own, :], from_upper.at[b], sems.at[0, 14 + b], sems.at[1, 14 + b], peer, head
        )

    def to_head(d):
        peer = (head + d + 1) % 4
        return remote(
            buf.at[own, lanes(peer)],
            from_head.at[d],
            sems.at[0, 4 + d],
            sems.at[1, 4 + d],
            win,
            peer,
        )

    def back(k):
        peer = base + 2 * ((cell + k % 4) % 4) + (core + k // 4) % 2
        view = final.at[own, :]
        return remote(view, view, sems.at[0, 6 + k], sems.at[1, 6 + k], peer, head)

    def first():
        to_core().start()

    def second():
        to_core().wait_recv()
        for k in range(4):
            start = pl.multiple_of(core * half + k * part, 16)
            block = pl.ds(start, part)
            total = buf[block, :].astype(F32) + from_core[k * part : k * part + part].astype(F32)
            buf[block, :] = total.astype(BF16)
        for c in range(3):
            to_cell(c).start()

    def third():
        for c in range(3):
            to_cell(c).wait_recv()
        total = buf[own, :].astype(F32)
        for c in range(3):
            total = total + from_cell[c].astype(F32)
        buf[own, :] = total.astype(BF16)
        for b in range(from_upper.shape[0] - 1):
            to_upper(b).start()
            to_upper(b).wait()
            buf[own, :] = (buf[own, :].astype(F32) + from_upper[b].astype(F32)).astype(BF16)
        for d in range(3):
            to_head(d).start()

    def fourth():
        for d in range(3):
            to_head(d).wait_recv()
        total = buf[own, lanes(head)].astype(F32)
        for d in range(3):
            total = total + from_head[d].astype(F32)
        final[own, :] = total.astype(BF16)
        for k in range(1, 8):
            back(k).start()

    def last():
        for k in range(1, 8):
            back(k).wait_recv()
        to_core().wait_send()
        for c in range(3):
            to_cell(c).wait_send()
            to_head(c).wait_send()
        for k in range(1, 8):
            back(k).wait_send()

    return first, second, third, fourth, last


def small_stages(buf, from_core, cells, from_upper, heads, final, sems):
    win, head, core, cell, base = position()
    other = win + 1 - 2 * core

    def lanes(h):
        return pl.ds(pl.multiple_of(h * D, LANES), D)

    def to_core():
        return remote(buf, from_core, sems.at[0, 0], sems.at[1, 0], other, head)

    def to_cell(c):
        view = cells.at[cell]
        peer = base + 2 * ((cell + c + 1) % 4) + core
        return remote(view, view, sems.at[0, 1 + c], sems.at[1, 1 + c], peer, head)

    def to_upper(b):
        peer = win + (8 << b) - 2 * (8 << b) * (win // (8 << b) % 2)
        return remote(buf, from_upper.at[b], sems.at[0, 14 + b], sems.at[1, 14 + b], peer, head)

    def to_head(d):
        peer = (head + d + 1) % 4
        return remote(
            buf.at[:, lanes(peer)], heads.at[head], sems.at[0, 4 + d], sems.at[1, 4 + d], win, peer
        )

    def first():
        to_core().start()

    def second():
        to_core().wait()
        cells[cell] = buf[...] + from_core[...]
        for c in range(3):
            to_cell(c).start()

    def third():
        for c in range(3):
            to_cell(c).wait()
        buf[...] = (cells[0] + cells[1]) + (cells[2] + cells[3])
        for b in range(from_upper.shape[0] - 1):
            to_upper(b).start()
            to_upper(b).wait()
            buf[...] = buf[...] + from_upper[b]
        heads[head] = buf[:, lanes(head)]
        for d in range(3):
            to_head(d).start()

    def last():
        for d in range(3):
            to_head(d).wait()
        final[...] = (heads[0] + heads[1]) + (heads[2] + heads[3])

    return first, second, third, last


def clip_rows(c, count=CLIP):
    return pl.ds(pl.multiple_of(c * count, count), count)


def block_kernel(clips, *refs):
    block_body(clips, refs[3:27], refs[39:63], *refs[:3], *refs[27:39], *refs[63:])


def block_body(
    clips,
    held,
    kept,
    frames_ref,
    tok_hbm,
    og_hbm,
    qvb_ref,
    table_ref,
    fc1b_ref,
    rowp_ref,
    mid_ref,
    dmid_ref,
    one_ref,
    two_ref,
    late_ref,
    esmall_ref,
    lsmall_ref,
    norm_ref,
    sown_ref,
    tok_ref,
    og_ref,
    n1t_ref,
    n2_ref,
    qkv_ref,
    dj_ref,
    hid_ref,
    probs_ref,
    att_ref,
    wqkv_ref,
    wproj_ref,
    w1_ref,
    w2_ref,
    small_ref,
    bqkv_ref,
    b1_ref,
    bias_ref,
    time_ref,
    rows_ref,
    gb_ref,
    tacc_ref,
    buf_1,
    buf_2,
    gp_ref,
    esbuf,
    lsbuf,
    core_1,
    core_2,
    core_es,
    core_ls,
    cell_1,
    cell_2,
    cell_es,
    cell_ls,
    up_1,
    up_2,
    up_es,
    up_ls,
    head_1,
    head_2,
    head_l,
    head_es,
    head_ls,
    nslots,
    wsems,
    ssems,
    rsems,
    nsems,
    osems,
):
    win, head, core, cell, base = position()
    first_clip = head * clips
    lbuf = buf_2

    def enter(c, carry):
        for part in range(2):
            rows = clip_rows(2 * c + part)
            n1, _ = normalize(to_windows(tok_ref[rows, :].astype(F32)))
            n1 = (n1 * rowp_ref[0:1] + rowp_ref[1:2]).astype(BF16)
            att_ref[rows, :D] = n1
            n1t_ref[:D, rows] = n1.T
        return carry

    def project(c, carry):
        rows = clip_rows(c, PAIR)
        for part in range(3):
            cols = slice(part * 512, part * 512 + 512)
            y = nt(att_ref[rows, :D], wqkv_ref[cols, :]) + bqkv_ref[0:1, cols]
            qkv_ref[rows, cols] = y.astype(BF16)
        return carry

    def attend(c, carry):
        frames = frames_ref[first_clip + c]
        masks = head_masks(BF16)
        for w in range(4):
            spots = pl.ds(pl.multiple_of(c * CLIP + w * SPOT, SPOT), SPOT)
            for g in range(GROUPS):
                q = qkv_ref[spots, g * D : g * D + LANES]
                k = qkv_ref[spots, g * D + LANES : g * D + 2 * LANES]
                s = nt(k, stack_heads(q, masks)) * SCALE + bias_ref[g]
                s = jnp.where(time_ref[w] < frames, s, MASKED)
                e = jnp.exp(s - jnp.max(s, axis=0, keepdims=True))
                p = (e * (1.0 / jnp.sum(e, axis=0, keepdims=True))).astype(BF16)
                probs_ref[c, w, g] = p
        for w in range(4):
            spots = pl.ds(pl.multiple_of(c * CLIP + w * SPOT, SPOT), SPOT)
            for g in range(GROUPS):
                v = qkv_ref[spots, g * D + 2 * LANES : g * D + D]
                o = pick_heads(tn(probs_ref[c, w, g], v))
                att_ref[spots, g * LANES : g * LANES + LANES] = o.astype(BF16)
        return carry

    def widen(c, carry):
        rows = clip_rows(c, PAIR)
        clip = [clip_rows(2 * c + part) for part in range(2)]
        x = jnp.concatenate([to_windows(tok_ref[r, :].astype(F32)) for r in clip], axis=0)
        og = jnp.concatenate([to_windows(og_ref[r, :].astype(F32)) for r in clip], axis=0)
        og_ref[rows, :] = og.astype(BF16)
        rows_ref[5] += fold(og)
        middle = x + nn(att_ref[rows, :], wproj_ref[...]) + rowp_ref[4:5]
        mid_ref[rows, :] = middle
        nrm, _ = normalize(middle)
        n2 = (nrm * rowp_ref[2:3] + rowp_ref[3:4]).astype(BF16)
        n2_ref[rows, :] = n2
        for j in range(FF // CHUNK):
            cols = slice(j * CHUNK, j * CHUNK + CHUNK)
            u = nn(n2, w1_ref[:, cols]) + b1_ref[0:1, cols]
            phi, dens = gelu_parts(u)
            hid_ref[rows, cols] = (u * phi).astype(BF16)
            dj_ref[rows, cols] = (phi + u * dens).astype(BF16)
        return carry

    def narrow_back(c, carry):
        rows = clip_rows(c, PAIR)
        for j in range(FF // CHUNK):
            cols = slice(j * CHUNK, j * CHUNK + CHUNK)
            dh = nt(og_ref[rows, :], w2_ref[cols, :])
            du = (dj_ref[rows, cols].astype(F32) * dh).astype(BF16)
            dj_ref[rows, cols] = du
            gb_ref[:, cols] += fold(du.astype(F32))
        return carry

    def widen_back(c, carry):
        rows = clip_rows(c, PAIR)
        dn2 = nt(dj_ref[rows, :], w1_ref[...])
        nrm, inv = normalize(mid_ref[rows, :])
        dmid = og_ref[rows, :].astype(F32) + norm_back(dn2, nrm, inv, rowp_ref[2:3])
        dmid_ref[rows, :] = dmid
        dbr = dmid.astype(BF16)
        rows_ref[2] += fold(dn2 * nrm)
        rows_ref[3] += fold(dn2)
        rows_ref[4] += fold(dbr.astype(F32))
        og_ref[rows, :] = dbr
        return carry

    def narrow(c, carry):
        rows = clip_rows(c, PAIR)
        result = mid_ref[rows, :] + nn(hid_ref[rows, :], w2_ref[...]) + rowp_ref[5:6]
        for part in range(2):
            result_part = from_windows(result[part * CLIP : part * CLIP + CLIP])
            mid_ref[clip_rows(2 * c + part), :] = result_part
        return carry

    def wide_grads(buf, given, back):
        for j in range(FF // 512):
            cols = slice(j * 512, j * 512 + 512)
            buf[:, cols] = tn(given[...], back[:, cols]).astype(BF16)

    def branch_grads():
        width = praw_ref.shape[0]
        for g in range(GROUPS):
            part = tn(att_ref[:, g * LANES : g * LANES + LANES], og_ref[...])
            gp_ref[:, g * D : g * D + D] = part[:width].astype(BF16)
        for j in range(clips // 2):
            r = slice(j * PAIR, j * PAIR + PAIR)
            att_ref[r, :] = nt(og_ref[r, :], wproj_ref[...]).astype(BF16)

    def qkv_grads():
        width = praw_ref.shape[0]
        lbuf[3 * width :, :] = gp_ref[...]
        for j in range(3):
            value = nn(n1t_ref[...], dj_ref[:, j * 512 : j * 512 + 512])
            for k in range(4):
                g, p = (4 * j + k) // 3, (4 * j + k) % 3
                turned = value[:D, k * LANES : k * LANES + LANES].T
                if p != 1:
                    cols = slice(g * D + p * LANES, g * D + p * LANES + LANES)
                    lsbuf[0:1, cols] = value[D : D + 1, k * LANES : k * LANES + LANES]
                lbuf[p * width : p * width + width, g * D : g * D + D] = turned[:width].astype(BF16)

    def attend_back(c, carry):
        rows = clip_rows(c)
        frames = frames_ref[first_clip + c]
        masks = head_masks(BF16)
        for g in range(GROUPS):
            tacc = None
            for w in range(4):
                spots = pl.ds(pl.multiple_of(c * CLIP + w * SPOT, SPOT), SPOT)
                v = qkv_ref[spots, g * D + 2 * LANES : g * D + D]
                do = stack_heads(att_ref[spots, g * LANES : g * LANES + LANES], masks)
                p = probs_ref[c, w, g]
                pf = p.astype(F32)
                dp = nt(v, do)
                inner = jnp.sum(pf * dp, axis=0, keepdims=True)
                ds = jnp.where(time_ref[w] < frames, pf * (dp - inner), 0.0)
                tacc = ds if tacc is None else tacc + ds
                probs_ref[c, w, g] = ds.astype(BF16)
                dj_ref[spots, g * D + 2 * LANES : g * D + D] = nn(p, do).astype(BF16)
            tacc_ref[g] += tacc
        for g in range(GROUPS):
            for w in range(4):
                spots = pl.ds(pl.multiple_of(c * CLIP + w * SPOT, SPOT), SPOT)
                cq = slice(g * D, g * D + LANES)
                ck = slice(g * D + LANES, g * D + 2 * LANES)
                q = qkv_ref[spots, cq]
                k = qkv_ref[spots, ck]
                ds = probs_ref[c, w, g]
                dj_ref[spots, cq] = (pick_heads(tn(ds, k)) * SCALE).astype(BF16)
                dj_ref[spots, ck] = (nn(ds, stack_heads(q, masks)) * SCALE).astype(BF16)
        return carry

    def entry_back(c, carry):
        rows = clip_rows(c, PAIR)
        clip = [clip_rows(2 * c + part) for part in range(2)]
        x = jnp.concatenate([to_windows(tok_ref[r, :].astype(F32)) for r in clip], axis=0)
        n, inv = normalize(x)
        dn1 = nn(dj_ref[rows, :], wqkv_ref[...])
        rows_ref[0] += fold(dn1 * n)
        rows_ref[1] += fold(dn1)
        din = dmid_ref[rows, :] + norm_back(dn1, n, inv, rowp_ref[0:1])
        for part in range(2):
            r = clip[part]
            dmid_ref[r, :] = from_windows(din[part * CLIP : part * CLIP + CLIP])
        return carry

    qraw_ref, praw_ref, araw_ref, braw_ref = kept[0], kept[3], kept[6], kept[9]
    keeps = [pltpu.make_async_copy(a, b, osems.at[0, 2 + i]) for i, (a, b) in enumerate(zip(held, kept))]
    for i in (0, 3, 6, 9):
        keeps[i].start()
    load_tok = pltpu.make_async_copy(tok_hbm, tok_ref, osems.at[0, 0])
    load_og = pltpu.make_async_copy(og_hbm, og_ref, osems.at[0, 1])
    load_tok.start()
    greeting = greet()
    small = [
        remote(sown_ref, small_ref.at[head], ssems.at[0, d], ssems.at[1, d], win, (head + d + 1) % 4)
        for d in range(3)
    ]
    own_small = pltpu.make_async_copy(sown_ref, small_ref.at[head], ssems.at[2, 0])
    gq_w = gather_stages(D, wqkv_ref, False, wsems.at[0])
    others = [
        gather_stages(rows, full, wide, wsems.at[1 + i])
        for i, (rows, full, wide) in enumerate(
            ((LANES, wproj_ref, False), (D, w1_ref, True), (D, w2_ref, False))
        )
    ]
    keeps[0].wait()
    for p in range(3):
        part = qraw_ref[p]
        part = jnp.concatenate([part, jnp.zeros((LANES - part.shape[0], D), F32)], axis=0)
        start = pl.multiple_of(head * D + p * LANES, LANES)
        wqkv_ref[pl.ds(start, LANES), :] = part.astype(BF16)
    greeting()
    gq_w[0]()
    load_og.start()
    width = qvb_ref.shape[1]
    sown_ref[...] = jnp.zeros_like(sown_ref)
    sown_ref[0:1, :width] = qvb_ref[0:1, :]
    sown_ref[0:1, LANES : LANES + width] = qvb_ref[1:2, :]
    sown_ref[1 : 1 + PER, : table_ref.shape[1]] = table_ref[...]
    sown_ref[5:6, :] = fc1b_ref[...].reshape(1, D)
    own_small.start()
    for copy in small:
        copy.start()
    width = praw_ref.shape[0]
    for i in (3, 6, 9):
        keeps[i].wait()
    tall = jnp.concatenate([praw_ref[...], jnp.zeros((LANES - width, D), F32)])
    wproj_ref[pl.ds(pl.multiple_of(head * LANES, LANES), LANES), :] = tall.astype(BF16)
    shard = pl.ds(pl.multiple_of(head * D, LANES), D)
    w1_ref[:, shard] = araw_ref[...].astype(BF16)
    w2_ref[shard, :] = braw_ref[...].astype(BF16)
    for k in others:
        k[0]()
    for wt in range(2):
        for wf in range(2):
            time_ref[wt * 2 + wf] = key_times(wt, wf)
    for ref in (rows_ref, gb_ref, tacc_ref, esbuf, lsbuf):
        ref[...] = jnp.zeros_like(ref)
    n1t_ref[D:, :] = jnp.ones((16, n1t_ref.shape[1]), F32).astype(BF16)
    load_tok.wait()
    lax.fori_loop(0, clips // 2, enter, 0)
    gq_w[1]()
    own_small.wait()
    for copy in small:
        copy.wait()
    for g in range(4):
        bqkv_ref[0:1, g * D : g * D + LANES] = small_ref[g, 0:1, :LANES]
        bqkv_ref[0:1, g * D + LANES : g * D + 2 * LANES] = jnp.zeros((1, LANES), F32)
        bqkv_ref[0:1, g * D + 2 * LANES : g * D + D] = small_ref[g, 0:1, LANES : 2 * LANES]
        b1_ref[0:1, g * D : g * D + D] = small_ref[g, 5:6, :]
    build_bias(small_ref, bias_ref)
    gq_w[2]()
    gq_w[3]()
    others[0][1]()
    others[1][1]()

    def span(share):
        return clips * share // 8

    lax.fori_loop(0, clips // 2, project, 0)
    others[2][1]()
    lax.fori_loop(0, span(4), attend, 0)
    others[0][2]()
    others[1][2]()
    lax.fori_loop(span(4), span(8), attend, 0)
    others[0][3]()
    others[1][3]()
    load_og.wait()
    for i in range(24):
        if i % 3 or i >= 12:
            keeps[i].start()
    lax.fori_loop(0, span(4) // 2, widen, 0)
    others[2][2]()
    lax.fori_loop(span(4) // 2, clips // 2, widen, 0)
    others[2][3]()
    one = reduce_stages(buf_1, core_1, cell_1, up_1, head_1, one_ref, rsems.at[0])
    two = reduce_stages(buf_2, core_2, cell_2, up_2, head_2, two_ref, rsems.at[1])
    late = reduce_stages(lbuf, core_2, cell_2, up_2, head_l, late_ref, rsems.at[2])
    early_small = small_stages(esbuf, core_es, cell_es, up_es, head_es, esmall_ref, rsems.at[3])
    late_small = small_stages(lsbuf, core_ls, cell_ls, up_ls, head_ls, lsmall_ref, rsems.at[4])
    wide_grads(buf_2, og_ref, hid_ref)
    two[0]()
    lax.fori_loop(0, span(4) // 2, narrow_back, 0)
    two[1]()
    lax.fori_loop(span(4) // 2, clips // 2, narrow_back, 0)
    wide_grads(buf_1, n2_ref, dj_ref)
    one[0]()
    lax.fori_loop(0, span(4) // 2, widen_back, 0)
    one[1]()
    two[2]()
    lax.fori_loop(span(4) // 2, clips // 2, widen_back, 0)
    branch_grads()
    two[3]()
    esbuf[0:1, :] = jnp.sum(gb_ref[...], axis=0, keepdims=True)
    for r in range(4):
        line = jnp.sum(rows_ref[2 + r], axis=0, keepdims=True)
        for g in range(GROUPS):
            esbuf[1 + r : 2 + r, g * D : g * D + D] = line
    early_small[0]()
    lax.fori_loop(0, span(2), attend_back, 0)
    one[2]()
    early_small[1]()
    lax.fori_loop(span(2), span(5), attend_back, 0)
    two[4]()
    one[3]()
    early_small[2]()
    lax.fori_loop(span(5), span(8), attend_back, 0)
    qkv_grads()
    late[0]()
    one[4]()
    early_small[3]()
    fold_table(tacc_ref, lsbuf)
    late[1]()
    lax.fori_loop(0, clips // 2, entry_back, 0)
    for r in range(2):
        line = jnp.sum(rows_ref[r], axis=0, keepdims=True)
        for g in range(GROUPS):
            lsbuf[4 + r : 5 + r, g * D : g * D + D] = line
    late_small[0]()
    late[2]()
    lax.fori_loop(0, span(4) // 2, narrow, 0)
    late_small[1]()
    lax.fori_loop(span(4) // 2, clips // 2, narrow, 0)
    late[3]()
    late_small[2]()
    square = jnp.zeros((8, D), F32)
    for ref in (one_ref, two_ref):
        value = ref[...].astype(F32)
        square = square + fold(value * value)
    late_small[3]()
    late[4]()
    value = late_ref[...].astype(F32)
    square = square + fold(value * value)
    es, ls = esmall_ref[...], lsmall_ref[...]
    row = iota((8, D), 0)
    square = square + jnp.where(row < 1, es * es, 0.0) + jnp.where(row < 4, ls * ls, 0.0)
    common = jnp.where((row >= 1) & (row < 5), es * es, 0.0)
    common = common + jnp.where((row >= 4) & (row < 6), ls * ls, 0.0)
    nslots[head] = jnp.broadcast_to(jnp.sum(square, keepdims=True), (8, LANES))
    sends = [
        remote(
            nslots.at[head], nslots.at[head], nsems.at[0, d], nsems.at[1, d], win, (head + d + 1) % 4
        )
        for d in range(3)
    ]
    for copy in sends:
        copy.start()
    for copy in sends:
        copy.wait()
    total = (nslots[0] + nslots[1]) + (nslots[2] + nslots[3])
    for i in range(24):
        if i % 3 or i >= 12:
            keeps[i].wait()
    norm_ref[...] = jnp.sqrt(total + jnp.sum(common, keepdims=True))


def fold_table(tacc_ref, lsbuf):
    row = iota((256, 256), 0)
    lane = iota((256, 256), 1)
    spot = row % SPOT
    base = 112 - (spot // WIN * (2 * WIN - 1) + spot % WIN)
    for h in range(PER):
        own = jnp.where((lane == base) & (row // SPOT == h), 1.0, 0.0).astype(F32).astype(BF16)
        for g in range(GROUPS):
            spread = None
            for part in split_three(tacc_ref[g]):
                term = nn(part, own)
                spread = term if spread is None else spread + term
            total = None
            for a in range(WIN):
                piece = pltpu.roll(
                    spread[a * 8 : a * 8 + 8], 15 * a, axis=1, stride=1, stride_axis=0
                )
                total = piece if total is None else total + piece
            line = jnp.sum(total, axis=0, keepdims=True)
            for half in range(2):
                at = h * 256 + half * LANES
                lsbuf[1 + at // D : 2 + at // D, g * D + at % D : g * D + at % D + LANES] = line[
                    :, half * LANES : half * LANES + LANES
                ]


def block(frames, tok, og, held, qvb, table, fc1b, rowp):
    rows = tok.shape[0]
    clips = rows // CLIP
    upper = max(lax.axis_size("win") // 8, 1).bit_length() - 1
    shape = jax.ShapeDtypeStruct
    sems = pltpu.SemaphoreType.DMA
    vmem = pltpu.VMEM
    spec = pl.BlockSpec
    inside = lambda: spec(memory_space=vmem)
    outside = lambda: spec(memory_space=pl.ANY)
    half, part = D // 2, D // 8
    praw = held[3]
    return pl.pallas_call(
        partial(block_kernel, clips),
        in_specs=[spec(memory_space=pltpu.SMEM)] + [outside()] * 26 + [inside()] * 4,
        out_specs=[inside()] * 32,
        out_shape=[
            vmem((rows, D), F32),
            vmem((rows, D), F32),
            vmem((D, D), BF16),
            vmem((D, D), BF16),
            vmem((D, D), BF16),
            vmem((8, D), F32),
            vmem((8, D), F32),
            vmem((8, LANES), F32),
        ]
        + [vmem(a.shape, F32) for a in held],
        scratch_shapes=[
            vmem((8, D), F32),
            vmem((rows, D), BF16),
            vmem((rows, D), BF16),
            vmem((D + 16, rows), BF16),
            vmem((rows, D), BF16),
            vmem((rows, 1536), BF16),
            vmem((rows, 1536), BF16),
            vmem((rows, FF), BF16),
            vmem((clips, 4, GROUPS, SPOT, PER * SPOT), BF16),
            vmem((rows, 512), BF16),
            vmem((1536, D), BF16),
            vmem((512, D), BF16),
            vmem((D, FF), BF16),
            vmem((FF, D), BF16),
            vmem((GROUPS, 8, D), F32),
            vmem((8, 1536), F32),
            vmem((8, FF), F32),
            vmem((GROUPS, SPOT, PER * SPOT), F32),
            vmem((4, SPOT, PER * SPOT), jnp.int32),
            vmem((6, 8, D), F32),
            vmem((8, FF), F32),
            vmem((GROUPS, SPOT, PER * SPOT), F32),
            vmem((D, 1536), BF16),
            vmem((D, 1536), BF16),
            vmem((praw.shape[0], 1536), BF16),
            vmem((8, 1536), F32),
            vmem((8, 1536), F32),
            vmem((half, 1536), BF16),
            vmem((half, 1536), BF16),
            vmem((8, 1536), F32),
            vmem((8, 1536), F32),
            vmem((3, part, 1536), BF16),
            vmem((3, part, 1536), BF16),
            vmem((4, 8, 1536), F32),
            vmem((4, 8, 1536), F32),
            vmem((upper + 1, part, 1536), BF16),
            vmem((upper + 1, part, 1536), BF16),
            vmem((upper + 1, 8, 1536), F32),
            vmem((upper + 1, 8, 1536), F32),
            vmem((3, part, D), BF16),
            vmem((3, part, D), BF16),
            vmem((3, part, D), BF16),
            vmem((4, 8, D), F32),
            vmem((4, 8, D), F32),
            vmem((4, 8, LANES), F32),
            sems((4, 11, 3)),
            sems((3, 3)),
            sems((5, 2, 14 + upper)),
            sems((2, 3)),
            sems((1, 26)),
        ],
        compiler_params=pltpu.CompilerParams(
            vmem_limit_bytes=VMEM_LIMIT, collective_id=0, has_side_effects=True
        ),
    )(frames, tok, og, *held, qvb, table, fc1b, rowp)


def adam_step(weight, gradient, moment, second, factor, rate):
    clipped = gradient * factor
    moment_new = BETA_ONE * moment + (1.0 - BETA_ONE) * clipped
    second_new = BETA_TWO * second + (1.0 - BETA_TWO) * clipped * clipped
    moment_hat = moment_new * (1.0 / (1.0 - BETA_ONE**STEP))
    second_hat = second_new * (1.0 / (1.0 - BETA_TWO**STEP))
    master = weight - rate * (
        moment_hat / (jnp.sqrt(second_hat) + ADAM_EPS) + WEIGHT_DECAY * weight
    )
    return (gradient, moment_new, second_new, master)


def step_kernel(cuts, *refs):
    norm_ref, g1_ref, g2_ref, late_ref, es_ref, ls_ref, one_ref, two_ref = refs[:8]
    large, little = refs[8:20], refs[20:32]
    gn_ref, one_out, two_out, outs, sems = refs[32], refs[33], refs[34], refs[35:67], refs[67]
    step = pl.program_id(0)
    pushes = [
        pltpu.make_async_copy(one_ref, one_out, sems.at[0]),
        pltpu.make_async_copy(two_ref, two_out, sems.at[1]),
    ]

    @pl.when(step == 0)
    def _():
        for push in pushes:
            push.start()

    norm = norm_ref[0:1, 0:1]
    factor = jnp.minimum(1.0, CLIP_LIMIT / (norm + 1e-06))

    def put(i, gradient, rate, given):
        given = [value.reshape(gradient.shape) for value in given]
        values = adam_step(given[0], gradient, given[1], given[2], factor, rate)
        for k in range(4):
            out = outs[4 * i + k]
            out[...] = values[k].reshape(out.shape)

    def some(k, count):
        rows = pl.ds(pl.multiple_of(step * count, count), count)
        return [large[3 * k + n][rows, :] for n in range(3)]

    width = large[0].shape[1]
    rows, tall = D // cuts, width // cuts
    late = late_ref[pl.ds(pl.multiple_of(step * width, width), width), :].astype(F32)
    put(0, late, LEARN_RATE, [large[n][step] for n in range(3)])
    late = late_ref[pl.ds(pl.multiple_of(cuts * width + step * tall, tall), tall), :].astype(F32)
    put(3, late, LEARN_RATE, some(1, tall))
    own = pl.ds(pl.multiple_of(step * rows, rows), rows)
    put(4, g1_ref[own, :].astype(F32), LEARN_RATE, some(2, rows))
    put(6, g2_ref[:, own].astype(F32).T, LEARN_RATE, some(3, rows))

    @pl.when(step == 0)
    def _():
        gn_ref[...] = norm
        whole = lambda k: [little[3 * k + n][...] for n in range(3)]
        both = jnp.concatenate([ls_ref[0:1, :width], ls_ref[0:1, 2 * LANES : 2 * LANES + width]])
        put(1, both, LEARN_RATE, whole(0))
        lines = []
        for h in range(PER):
            pieces = []
            for half in range(2):
                at = h * 256 + half * LANES
                pieces.append(ls_ref[1 + at // D : 2 + at // D, at % D : at % D + LANES])
            lines.append(jnp.concatenate(pieces, axis=1))
        lines = jnp.concatenate(lines + [jnp.zeros((8 - PER, 256), F32)])
        offsets = little[3].shape[1]
        flip = iota((256, 256), 0) + iota((256, 256), 1) == offsets - 1
        flip = jnp.where(flip, 1.0, 0.0).astype(F32).astype(BF16)
        table = None
        for part in split_three(lines):
            term = nn(part, flip)
            table = term if table is None else table + term
        put(2, table[:PER, :offsets], ROW_RATE, whole(1))
        put(5, es_ref[0:1, :], LEARN_RATE, whole(2))
        put(7, jnp.concatenate([ls_ref[4:6, :], es_ref[1:5, :]]), ROW_RATE, whole(3))

    @pl.when(step == cuts - 1)
    def _():
        for push in pushes:
            push.wait()


def take_step(held, results):
    little = held[12:]
    cuts = 3
    spec = pl.BlockSpec
    near = spec(memory_space=pltpu.VMEM)
    full = lambda a: spec(a.shape, lambda i: (0,) * a.ndim)
    third = lambda a: spec(
        (a.shape[0] // cuts,) + a.shape[1:], lambda i: (i,) + (0,) * (a.ndim - 1)
    )
    order = [(third, held[0]), (full, little[0]), (full, little[3]), (third, held[3])]
    order += [(third, held[6]), (full, little[6]), (third, held[9]), (full, little[9])]
    one, two = results[6:]
    shape = jax.ShapeDtypeStruct
    close = [pltpu.with_memory_space_constraint(v, pltpu.VMEM) for v in (*results, *held)]
    outs = pl.pallas_call(
        partial(step_kernel, cuts),
        grid=(cuts,),
        in_specs=[near] * 32,
        out_specs=[spec((1, 1), lambda i: (0, 0))]
        + [spec(memory_space=pl.ANY)] * 2
        + [kind(a) for kind, a in order for _ in range(4)],
        out_shape=[shape((1, 1), F32), shape(one.shape, F32), shape(two.shape, F32)]
        + [shape(a.shape, F32) for _, a in order for _ in range(4)],
        scratch_shapes=[pltpu.SemaphoreType.DMA((2,))],
        compiler_params=pltpu.CompilerParams(vmem_limit_bytes=TAIL_LIMIT),
    )(*close)
    return outs[0], outs[1], outs[2], outs[3:]


def shards(
    tokens,
    out_grad,
    clip_frames,
    qkv_weight,
    qv_bias,
    rel_table,
    proj_weight,
    fc1_weight,
    fc1_bias,
    fc2_weight,
    row_params,
    qkv_first,
    qkv_second,
    qvb_first,
    qvb_second,
    table_first,
    table_second,
    proj_first,
    proj_second,
    fc1_first,
    fc1_second,
    fc1b_first,
    fc1b_second,
    fc2_first,
    fc2_second,
    rows_first,
    rows_second,
):
    parts = lambda v: v.transpose(1, 2, 0)
    large = [parts(qkv_weight), parts(qkv_first), parts(qkv_second)]
    large += [proj_weight, proj_first, proj_second, fc1_weight, fc1_first, fc1_second]
    large += [fc2_weight, fc2_first, fc2_second]
    little = [qv_bias, qvb_first, qvb_second, rel_table.T, table_first.T, table_second.T]
    little += [fc1_bias, fc1b_first, fc1b_second, row_params, rows_first, rows_second]
    output, input_grad, g1, g2, late, esmall, lsmall, norm, *kept = block(
        clip_frames, tokens, out_grad, large + little, qv_bias, little[3], fc1_bias, row_params
    )
    results = (norm, g1, g2, late, esmall, lsmall, output, input_grad)
    grad_norm, output, input_grad, updated = take_step(kept, results)
    updated = [
        v.transpose(2, 0, 1) if k < 4 else v.T if 8 <= k < 12 else v for k, v in enumerate(updated)
    ]
    return (output, input_grad, grad_norm.reshape(()), *updated)


def solution(mesh):
    rows = P(("win", "head"), None)
    last3, last2, first2, first1 = P(None, None, "head"), P(None, "head"), P("head", None), P("head")
    each = (last3, last2, last2, first2, last2, first1, first2, P())
    return jax.shard_map(
        shards,
        mesh=mesh,
        in_specs=(rows, rows, P("win")) + each + tuple(s for s in each for _ in range(2)),
        out_specs=(rows, rows, P()) + tuple(s for s in each for _ in range(4)),
        check_vma=False,
    )
```

```python
from functools import partial

import jax
import jax.numpy as jnp
from jax import lax
from jax.experimental import pallas as pl
from jax.experimental.pallas import tpu as pltpu
from jax.sharding import PartitionSpec as P

D = 384
HDIM = 24
HEADS = 16
GROUPS = 4
PER = 4
LANES = 128
FF = 1536
GRID = 16
WIN = 8
CLIP = GRID * GRID
SPOT = WIN * WIN
SHIFT = 4
STEP = 10
CHUNK = 768
PAIR = 2 * CLIP
FOUR = 4 * CLIP

NORM_EPS = 1e-05
MASKED = -1000000000.0
CLIP_LIMIT = 1.0
LEARN_RATE = 0.1
ROW_RATE = 0.5
BETA_ONE = 0.9
BETA_TWO = 0.999
ADAM_EPS = 1e-08
WEIGHT_DECAY = 0.01
SCALE = HDIM ** (-0.5)
F32 = jnp.float32
BF16 = jnp.bfloat16
VMEM_LIMIT = 50 * 1024 * 1024
TAIL_LIMIT = 30 * 1024 * 1024


def nn(a, b):
    return lax.dot_general(a, b, (((1,), (0,)), ((), ())), preferred_element_type=F32)


def nt(a, b):
    return lax.dot_general(a, b, (((1,), (1,)), ((), ())), preferred_element_type=F32)


def tn(a, b):
    return lax.dot_general(a, b, (((0,), (0,)), ((), ())), preferred_element_type=F32)


def iota(shape, axis):
    return lax.broadcasted_iota(jnp.int32, shape, axis)


def fold(x):
    return jnp.sum(x.reshape(x.shape[0] // 8, 8, x.shape[1]), axis=0)


def normalize(x):
    center = x - jnp.mean(x, axis=-1, keepdims=True)
    spread = jnp.mean(center * center, axis=-1, keepdims=True)
    inverse = lax.rsqrt(spread + NORM_EPS)
    return center * inverse, inverse


def norm_back(e, n, inverse, gain):
    q = e * gain
    return inverse * (
        q - jnp.mean(q, axis=-1, keepdims=True) - n * jnp.mean(q * n, axis=-1, keepdims=True)
    )


def to_windows(x):
    low = iota((8, x.shape[1]), 0) < 4
    first, second = [], []
    for t in range(GRID):
        a = x[16 * t : 16 * t + 8]
        b = x[16 * t + 8 : 16 * t + 16]
        first.append(pltpu.roll(jnp.where(low, b, a), 4, axis=0))
        second.append(pltpu.roll(jnp.where(low, a, b), 4, axis=0))
    pieces = []
    for wt in range(2):
        for side in (first, second):
            for a in range(WIN):
                pieces.append(side[(wt * WIN + a + SHIFT) % GRID])
    return jnp.concatenate(pieces, axis=0)


def from_windows(y):
    low = iota((8, y.shape[1]), 0) < 4
    pieces = []
    for t in range(GRID):
        rolled = (t - SHIFT) % GRID
        base = (rolled // WIN) * 128 + (rolled % WIN) * 8
        u = pltpu.roll(y[base : base + 8], 4, axis=0)
        v = pltpu.roll(y[base + 64 : base + 72], 4, axis=0)
        pieces.append(jnp.where(low, v, u))
        pieces.append(jnp.where(low, u, v))
    return jnp.concatenate(pieces, axis=0)


def head_masks(dtype):
    lane = iota((16, LANES), 1) // HDIM
    return [jnp.where(lane == h, 1.0, 0.0).astype(F32).astype(dtype) for h in range(PER)]


def stack_heads(x, masks):
    tiles = x.reshape(SPOT // 16, 16, LANES)
    return jnp.concatenate([(tiles * m[None]).reshape(SPOT, LANES) for m in masks], axis=0)


def pick_heads(r):
    lane = iota((SPOT, LANES), 1)
    out = r[3 * SPOT :]
    for h in (2, 1, 0):
        out = jnp.where(lane < (h + 1) * HDIM, r[h * SPOT : (h + 1) * SPOT], out)
    return out


def key_times(wt, wf):
    j = iota((SPOT, PER * SPOT), 0)
    i = iota((SPOT, PER * SPOT), 1) % SPOT
    time = (wt * WIN + j // WIN + SHIFT) % GRID
    same = j >= 0
    if wt:
        same = same & ((j // WIN < 4) == (i // WIN < 4))
    if wf:
        same = same & ((j % WIN < 4) == (i % WIN < 4))
    return jnp.where(same, time, 99)


def split_three(x):
    one = x.astype(BF16)
    rest = x - one.astype(F32)
    two = rest.astype(BF16)
    three = (rest - two.astype(F32)).astype(BF16)
    return one, two, three


def build_bias(table_ref, bias_ref):
    row = iota((256, 256), 0)
    lane = iota((256, 256), 1)
    spot = lane % SPOT
    base = spot // WIN * (2 * WIN - 1) + spot % WIN
    for g in range(GROUPS):
        total = None
        for h in range(PER):
            own = jnp.where((row == base) & (lane // SPOT == h), 1.0, 0.0).astype(F32).astype(BF16)
            line = jnp.broadcast_to(table_ref[g, 1 + h : 2 + h, :256], (8, 256))
            spread = jnp.concatenate(
                [
                    pltpu.roll(line, (15 * a + 144) % 256, axis=1, stride=1, stride_axis=0)
                    for a in range(WIN)
                ],
                axis=0,
            )
            for part in split_three(spread):
                term = nn(part, own)
                total = term if total is None else total + term
        bias_ref[g] = total


def gelu_parts(u):
    bell = jnp.exp(-0.5 * (u * u))
    return 0.5 + 0.5 * lax.erf(u * (0.5**0.5)), bell * 0.3989422804014327


def place(win, head):
    return {"win": win, "head": head}


def remote(src, dst, send, recv, win, head):
    return pltpu.make_async_remote_copy(
        src_ref=src,
        dst_ref=dst,
        send_sem=send,
        recv_sem=recv,
        device_id=place(win, head),
        device_id_type=pl.DeviceIdType.MESH,
    )


def position():
    win, head = lax.axis_index("win"), lax.axis_index("head")
    core, cell = win % 2, (win // 2) % 4
    return win, head, core, cell, win - core - 2 * cell


def greet():
    win, head, core, cell, base = position()
    barrier = pltpu.get_barrier_semaphore()
    peers = [(win, (head + d) % 4) for d in (1, 2, 3)]
    peers += [(base + 2 * ((cell + k % 4) % 4) + (core + k // 4) % 2, head) for k in range(1, 8)]
    for w, h in peers:
        pl.semaphore_signal(barrier, inc=1, device_id=place(w, h), device_id_type=pl.DeviceIdType.MESH)
    return lambda: pl.semaphore_wait(barrier, len(peers))


def shard_view(ref, wide, head, start, count):
    if wide:
        return ref.at[pl.ds(start, count), pl.ds(pl.multiple_of(head * D, LANES), D)]
    rows = ref.shape[0] // 4
    return ref.at[pl.ds(pl.multiple_of(head * rows + start, 16), count), :]


def gather_stages(rows, full, wide, sems):
    win, head, core, cell, base = position()
    half, part = rows // 2, rows // 8
    mine = pl.multiple_of(core * half + cell * part, 16)
    near = pl.multiple_of(core * half, 16)

    def over_head(d):
        view = shard_view(full, wide, head, mine, part)
        return remote(view, view, sems.at[0, d], sems.at[1, d], win, (head + d + 1) % 4)

    def over_cell(d, c):
        view = shard_view(full, wide, (head + 3 - d) % 4, mine, part)
        peer = base + 2 * ((cell + c + 1) % 4) + core
        return remote(view, view, sems.at[2 + c, d], sems.at[5 + c, d], peer, head)

    def over_core(d):
        view = shard_view(full, wide, (head + 3 - d) % 4, near, half)
        return remote(view, view, sems.at[8, d], sems.at[9, d], win + 1 - 2 * core, head)

    def first():
        for d in range(3):
            over_head(d).start()

    def second():
        for d in range(3):
            over_head(d).wait_recv()
            for c in range(3):
                over_cell(d, c).start()

    def third():
        for d in range(3):
            for c in range(3):
                over_cell(d, c).wait_recv()
            over_core(d).start()

    def last():
        for d in range(3):
            over_core(d).wait_recv()
        for d in range(3):
            over_head(d).wait_send()
            for c in range(3):
                over_cell(d, c).wait_send()
            over_core(d).wait_send()

    return first, second, third, last


def reduce_stages(buf, from_core, from_cell, from_upper, from_head, final, sems):
    win, head, core, cell, base = position()
    rows = buf.shape[0]
    half, part = rows // 2, rows // 8
    near = pl.multiple_of(core * half, 16)
    far = pl.multiple_of((1 - core) * half, 16)
    mine = pl.multiple_of(core * half + cell * part, 16)
    other = win + 1 - 2 * core
    own = pl.ds(mine, part)

    def lanes(h):
        return pl.ds(pl.multiple_of(h * D, LANES), D)

    def to_core():
        return remote(
            buf.at[pl.ds(far, half), :], from_core, sems.at[0, 0], sems.at[1, 0], other, head
        )

    def to_cell(c):
        peer = (cell + c + 1) % 4
        start = pl.multiple_of(core * half + peer * part, 16)
        return remote(
            buf.at[pl.ds(start, part), :],
            from_cell.at[c],
            sems.at[0, 1 + c],
            sems.at[1, 1 + c],
            base + 2 * peer + core,
            head,
        )

    def to_upper(b):
        peer = win + (8 << b) - 2 * (8 << b) * (win // (8 << b) % 2)
        return remote(
            buf.at[own, :], from_upper.at[b], sems.at[0, 14 + b], sems.at[1, 14 + b], peer, head
        )

    def to_head(d):
        peer = (head + d + 1) % 4
        return remote(
            buf.at[own, lanes(peer)],
            from_head.at[d],
            sems.at[0, 4 + d],
            sems.at[1, 4 + d],
            win,
            peer,
        )

    def back(k):
        peer = base + 2 * ((cell + k % 4) % 4) + (core + k // 4) % 2
        view = final.at[own, :]
        return remote(view, view, sems.at[0, 6 + k], sems.at[1, 6 + k], peer, head)

    def first():
        to_core().start()

    def second():
        to_core().wait_recv()
        for k in range(4):
            start = pl.multiple_of(core * half + k * part, 16)
            block = pl.ds(start, part)
            total = buf[block, :].astype(F32) + from_core[k * part : k * part + part].astype(F32)
            buf[block, :] = total.astype(BF16)
        for c in range(3):
            to_cell(c).start()

    def third():
        for c in range(3):
            to_cell(c).wait_recv()
        total = buf[own, :].astype(F32)
        for c in range(3):
            total = total + from_cell[c].astype(F32)
        buf[own, :] = total.astype(BF16)
        for b in range(from_upper.shape[0] - 1):
            to_upper(b).start()
            to_upper(b).wait()
            buf[own, :] = (buf[own, :].astype(F32) + from_upper[b].astype(F32)).astype(BF16)
        for d in range(3):
            to_head(d).start()

    def fourth():
        for d in range(3):
            to_head(d).wait_recv()
        total = buf[own, lanes(head)].astype(F32)
        for d in range(3):
            total = total + from_head[d].astype(F32)
        final[own, :] = total.astype(BF16)
        for k in range(1, 8):
            back(k).start()

    def last():
        for k in range(1, 8):
            back(k).wait_recv()
        to_core().wait_send()
        for c in range(3):
            to_cell(c).wait_send()
            to_head(c).wait_send()
        for k in range(1, 8):
            back(k).wait_send()

    return first, second, third, fourth, last


def small_stages(buf, from_core, cells, from_upper, heads, final, sems):
    win, head, core, cell, base = position()
    other = win + 1 - 2 * core

    def lanes(h):
        return pl.ds(pl.multiple_of(h * D, LANES), D)

    def to_core():
        return remote(buf, from_core, sems.at[0, 0], sems.at[1, 0], other, head)

    def to_cell(c):
        view = cells.at[cell]
        peer = base + 2 * ((cell + c + 1) % 4) + core
        return remote(view, view, sems.at[0, 1 + c], sems.at[1, 1 + c], peer, head)

    def to_upper(b):
        peer = win + (8 << b) - 2 * (8 << b) * (win // (8 << b) % 2)
        return remote(buf, from_upper.at[b], sems.at[0, 14 + b], sems.at[1, 14 + b], peer, head)

    def to_head(d):
        peer = (head + d + 1) % 4
        return remote(
            buf.at[:, lanes(peer)], heads.at[head], sems.at[0, 4 + d], sems.at[1, 4 + d], win, peer
        )

    def first():
        to_core().start()

    def second():
        to_core().wait()
        cells[cell] = buf[...] + from_core[...]
        for c in range(3):
            to_cell(c).start()

    def third():
        for c in range(3):
            to_cell(c).wait()
        buf[...] = (cells[0] + cells[1]) + (cells[2] + cells[3])
        for b in range(from_upper.shape[0] - 1):
            to_upper(b).start()
            to_upper(b).wait()
            buf[...] = buf[...] + from_upper[b]
        heads[head] = buf[:, lanes(head)]
        for d in range(3):
            to_head(d).start()

    def last():
        for d in range(3):
            to_head(d).wait()
        final[...] = (heads[0] + heads[1]) + (heads[2] + heads[3])

    return first, second, third, last


def clip_rows(c, count=CLIP):
    return pl.ds(pl.multiple_of(c * count, count), count)


def block_kernel(clips, *refs):
    block_body(clips, refs[3:27], refs[39:63], *refs[:3], *refs[27:39], *refs[63:])


def block_body(
    clips,
    held,
    kept,
    frames_ref,
    tok_hbm,
    og_hbm,
    qvb_ref,
    table_ref,
    fc1b_ref,
    rowp_ref,
    mid_ref,
    dmid_ref,
    one_ref,
    two_ref,
    late_ref,
    esmall_ref,
    lsmall_ref,
    norm_ref,
    sown_ref,
    tok_ref,
    og_ref,
    n1t_ref,
    n2_ref,
    qkv_ref,
    dj_ref,
    hid_ref,
    probs_ref,
    att_ref,
    wqkv_ref,
    wproj_ref,
    w1_ref,
    w2_ref,
    small_ref,
    bqkv_ref,
    b1_ref,
    bias_ref,
    time_ref,
    rows_ref,
    gb_ref,
    tacc_ref,
    buf_1,
    buf_2,
    gp_ref,
    esbuf,
    lsbuf,
    core_1,
    core_2,
    core_es,
    core_ls,
    cell_1,
    cell_2,
    cell_es,
    cell_ls,
    up_1,
    up_2,
    up_es,
    up_ls,
    head_1,
    head_2,
    head_l,
    head_es,
    head_ls,
    nslots,
    wsems,
    ssems,
    rsems,
    nsems,
    osems,
):
    win, head, core, cell, base = position()
    first_clip = head * clips
    lbuf = buf_2

    def enter(c, carry):
        for part in range(2):
            rows = clip_rows(2 * c + part)
            n1, _ = normalize(to_windows(tok_ref[rows, :].astype(F32)))
            n1 = (n1 * rowp_ref[0:1] + rowp_ref[1:2]).astype(BF16)
            att_ref[rows, :D] = n1
            n1t_ref[:D, rows] = n1.T
        return carry

    def project(c, carry):
        rows = clip_rows(c, FOUR)
        for part in range(3):
            cols = slice(part * 512, part * 512 + 512)
            y = nt(att_ref[rows, :D], wqkv_ref[cols, :]) + bqkv_ref[0:1, cols]
            qkv_ref[rows, cols] = y.astype(BF16)
        return carry

    def attend(c, carry):
        frames = frames_ref[first_clip + c]
        masks = head_masks(BF16)
        for w in range(4):
            spots = pl.ds(pl.multiple_of(c * CLIP + w * SPOT, SPOT), SPOT)
            for g in range(GROUPS):
                q = qkv_ref[spots, g * D : g * D + LANES]
                k = qkv_ref[spots, g * D + LANES : g * D + 2 * LANES]
                s = nt(k, stack_heads(q, masks)) * SCALE + bias_ref[g]
                s = jnp.where(time_ref[w] < frames, s, MASKED)
                e = jnp.exp(s - jnp.max(s, axis=0, keepdims=True))
                p = (e * (1.0 / jnp.sum(e, axis=0, keepdims=True))).astype(BF16)
                probs_ref[c, w, g] = p
        for w in range(4):
            spots = pl.ds(pl.multiple_of(c * CLIP + w * SPOT, SPOT), SPOT)
            for g in range(GROUPS):
                v = qkv_ref[spots, g * D + 2 * LANES : g * D + D]
                o = pick_heads(tn(probs_ref[c, w, g], v))
                att_ref[spots, g * LANES : g * LANES + LANES] = o.astype(BF16)
        return carry

    def widen(c, carry):
        rows = clip_rows(c, FOUR)
        clip = [clip_rows(4 * c + part) for part in range(4)]
        x = jnp.concatenate([to_windows(tok_ref[r, :].astype(F32)) for r in clip], axis=0)
        og = jnp.concatenate([to_windows(og_ref[r, :].astype(F32)) for r in clip], axis=0)
        og_ref[rows, :] = og.astype(BF16)
        rows_ref[5] += fold(og)
        middle = x + nn(att_ref[rows, :], wproj_ref[...]) + rowp_ref[4:5]
        mid_ref[rows, :] = middle
        nrm, _ = normalize(middle)
        n2 = (nrm * rowp_ref[2:3] + rowp_ref[3:4]).astype(BF16)
        n2_ref[rows, :] = n2
        for j in range(FF // CHUNK):
            cols = slice(j * CHUNK, j * CHUNK + CHUNK)
            u = nn(n2, w1_ref[:, cols]) + b1_ref[0:1, cols]
            phi, dens = gelu_parts(u)
            hid_ref[rows, cols] = (u * phi).astype(BF16)
            dj_ref[rows, cols] = (phi + u * dens).astype(BF16)
        return carry

    def narrow_back(c, carry):
        rows = clip_rows(c, FOUR)
        for j in range(FF // CHUNK):
            cols = slice(j * CHUNK, j * CHUNK + CHUNK)
            dh = nt(og_ref[rows, :], w2_ref[cols, :])
            du = (dj_ref[rows, cols].astype(F32) * dh).astype(BF16)
            dj_ref[rows, cols] = du
            gb_ref[:, cols] += fold(du.astype(F32))
        return carry

    def widen_back(c, carry):
        rows = clip_rows(c, FOUR)
        dn2 = nt(dj_ref[rows, :], w1_ref[...])
        nrm, inv = normalize(mid_ref[rows, :])
        dmid = og_ref[rows, :].astype(F32) + norm_back(dn2, nrm, inv, rowp_ref[2:3])
        dmid_ref[rows, :] = dmid
        dbr = dmid.astype(BF16)
        rows_ref[2] += fold(dn2 * nrm)
        rows_ref[3] += fold(dn2)
        rows_ref[4] += fold(dbr.astype(F32))
        og_ref[rows, :] = dbr
        return carry

    def narrow(c, carry):
        rows = clip_rows(c, FOUR)
        result = mid_ref[rows, :] + nn(hid_ref[rows, :], w2_ref[...]) + rowp_ref[5:6]
        for part in range(4):
            result_part = from_windows(result[part * CLIP : part * CLIP + CLIP])
            mid_ref[clip_rows(4 * c + part), :] = result_part
        return carry

    def wide_grads(buf, given, back):
        for j in range(FF // 512):
            cols = slice(j * 512, j * 512 + 512)
            buf[:, cols] = tn(given[...], back[:, cols]).astype(BF16)

    def branch_grads():
        width = praw_ref.shape[0]
        for g in range(GROUPS):
            part = tn(att_ref[:, g * LANES : g * LANES + LANES], og_ref[...])
            gp_ref[:, g * D : g * D + D] = part[:width].astype(BF16)
        for j in range(clips // 2):
            r = slice(j * PAIR, j * PAIR + PAIR)
            att_ref[r, :] = nt(og_ref[r, :], wproj_ref[...]).astype(BF16)

    def qkv_grads():
        width = praw_ref.shape[0]
        lbuf[3 * width :, :] = gp_ref[...]
        for j in range(3):
            value = nn(n1t_ref[...], dj_ref[:, j * 512 : j * 512 + 512])
            for k in range(4):
                g, p = (4 * j + k) // 3, (4 * j + k) % 3
                turned = value[:D, k * LANES : k * LANES + LANES].T
                if p != 1:
                    cols = slice(g * D + p * LANES, g * D + p * LANES + LANES)
                    lsbuf[0:1, cols] = value[D : D + 1, k * LANES : k * LANES + LANES]
                lbuf[p * width : p * width + width, g * D : g * D + D] = turned[:width].astype(BF16)

    def attend_back(c, carry):
        rows = clip_rows(c)
        frames = frames_ref[first_clip + c]
        masks = head_masks(BF16)
        for g in range(GROUPS):
            tacc = None
            for w in range(4):
                spots = pl.ds(pl.multiple_of(c * CLIP + w * SPOT, SPOT), SPOT)
                v = qkv_ref[spots, g * D + 2 * LANES : g * D + D]
                do = stack_heads(att_ref[spots, g * LANES : g * LANES + LANES], masks)
                p = probs_ref[c, w, g]
                pf = p.astype(F32)
                dp = nt(v, do)
                inner = jnp.sum(pf * dp, axis=0, keepdims=True)
                ds = jnp.where(time_ref[w] < frames, pf * (dp - inner), 0.0)
                tacc = ds if tacc is None else tacc + ds
                probs_ref[c, w, g] = ds.astype(BF16)
                dj_ref[spots, g * D + 2 * LANES : g * D + D] = nn(p, do).astype(BF16)
            tacc_ref[g] += tacc
        for g in range(GROUPS):
            for w in range(4):
                spots = pl.ds(pl.multiple_of(c * CLIP + w * SPOT, SPOT), SPOT)
                cq = slice(g * D, g * D + LANES)
                ck = slice(g * D + LANES, g * D + 2 * LANES)
                q = qkv_ref[spots, cq]
                k = qkv_ref[spots, ck]
                ds = probs_ref[c, w, g]
                dj_ref[spots, cq] = (pick_heads(tn(ds, k)) * SCALE).astype(BF16)
                dj_ref[spots, ck] = (nn(ds, stack_heads(q, masks)) * SCALE).astype(BF16)
        return carry

    def entry_back(c, carry):
        rows = clip_rows(c, PAIR)
        clip = [clip_rows(2 * c + part) for part in range(2)]
        x = jnp.concatenate([to_windows(tok_ref[r, :].astype(F32)) for r in clip], axis=0)
        n, inv = normalize(x)
        dn1 = nn(dj_ref[rows, :], wqkv_ref[...])
        rows_ref[0] += fold(dn1 * n)
        rows_ref[1] += fold(dn1)
        din = dmid_ref[rows, :] + norm_back(dn1, n, inv, rowp_ref[0:1])
        for part in range(2):
            r = clip[part]
            dmid_ref[r, :] = from_windows(din[part * CLIP : part * CLIP + CLIP])
        return carry

    qraw_ref, praw_ref, araw_ref, braw_ref = kept[0], kept[3], kept[6], kept[9]
    keeps = [pltpu.make_async_copy(a, b, osems.at[0, 2 + i]) for i, (a, b) in enumerate(zip(held, kept))]
    for i in (0, 3, 6, 9):
        keeps[i].start()
    load_tok = pltpu.make_async_copy(tok_hbm, tok_ref, osems.at[0, 0])
    load_og = pltpu.make_async_copy(og_hbm, og_ref, osems.at[0, 1])
    load_tok.start()
    greeting = greet()
    small = [
        remote(sown_ref, small_ref.at[head], ssems.at[0, d], ssems.at[1, d], win, (head + d + 1) % 4)
        for d in range(3)
    ]
    own_small = pltpu.make_async_copy(sown_ref, small_ref.at[head], ssems.at[2, 0])
    gq_w = gather_stages(D, wqkv_ref, False, wsems.at[0])
    others = [
        gather_stages(rows, full, wide, wsems.at[1 + i])
        for i, (rows, full, wide) in enumerate(
            ((LANES, wproj_ref, False), (D, w1_ref, True), (D, w2_ref, False))
        )
    ]
    keeps[0].wait()
    for p in range(3):
        part = qraw_ref[p]
        part = jnp.concatenate([part, jnp.zeros((LANES - part.shape[0], D), F32)], axis=0)
        start = pl.multiple_of(head * D + p * LANES, LANES)
        wqkv_ref[pl.ds(start, LANES), :] = part.astype(BF16)
    greeting()
    gq_w[0]()
    load_og.start()
    width = qvb_ref.shape[1]
    sown_ref[...] = jnp.zeros_like(sown_ref)
    sown_ref[0:1, :width] = qvb_ref[0:1, :]
    sown_ref[0:1, LANES : LANES + width] = qvb_ref[1:2, :]
    sown_ref[1 : 1 + PER, : table_ref.shape[1]] = table_ref[...]
    sown_ref[5:6, :] = fc1b_ref[...].reshape(1, D)
    own_small.start()
    for copy in small:
        copy.start()
    width = praw_ref.shape[0]
    for i in (3, 6, 9):
        keeps[i].wait()
    tall = jnp.concatenate([praw_ref[...], jnp.zeros((LANES - width, D), F32)])
    wproj_ref[pl.ds(pl.multiple_of(head * LANES, LANES), LANES), :] = tall.astype(BF16)
    shard = pl.ds(pl.multiple_of(head * D, LANES), D)
    w1_ref[:, shard] = araw_ref[...].astype(BF16)
    w2_ref[shard, :] = braw_ref[...].astype(BF16)
    for k in others:
        k[0]()
    for wt in range(2):
        for wf in range(2):
            time_ref[wt * 2 + wf] = key_times(wt, wf)
    for ref in (rows_ref, gb_ref, tacc_ref, esbuf, lsbuf):
        ref[...] = jnp.zeros_like(ref)
    n1t_ref[D:, :] = jnp.ones((16, n1t_ref.shape[1]), F32).astype(BF16)
    load_tok.wait()
    lax.fori_loop(0, clips // 2, enter, 0)
    gq_w[1]()
    own_small.wait()
    for copy in small:
        copy.wait()
    for g in range(4):
        bqkv_ref[0:1, g * D : g * D + LANES] = small_ref[g, 0:1, :LANES]
        bqkv_ref[0:1, g * D + LANES : g * D + 2 * LANES] = jnp.zeros((1, LANES), F32)
        bqkv_ref[0:1, g * D + 2 * LANES : g * D + D] = small_ref[g, 0:1, LANES : 2 * LANES]
        b1_ref[0:1, g * D : g * D + D] = small_ref[g, 5:6, :]
    build_bias(small_ref, bias_ref)
    gq_w[2]()
    gq_w[3]()
    others[0][1]()
    others[1][1]()

    def span(share):
        return clips * share // 8

    lax.fori_loop(0, clips // 4, project, 0)
    others[2][1]()
    lax.fori_loop(0, span(4), attend, 0)
    others[0][2]()
    others[1][2]()
    lax.fori_loop(span(4), span(8), attend, 0)
    others[0][3]()
    others[1][3]()
    load_og.wait()
    for i in range(24):
        if i % 3 or i >= 12:
            keeps[i].start()
    lax.fori_loop(0, span(4) // 4, widen, 0)
    others[2][2]()
    lax.fori_loop(span(4) // 4, clips // 4, widen, 0)
    others[2][3]()
    one = reduce_stages(buf_1, core_1, cell_1, up_1, head_1, one_ref, rsems.at[0])
    two = reduce_stages(buf_2, core_2, cell_2, up_2, head_2, two_ref, rsems.at[1])
    late = reduce_stages(lbuf, core_2, cell_2, up_2, head_l, late_ref, rsems.at[2])
    early_small = small_stages(esbuf, core_es, cell_es, up_es, head_es, esmall_ref, rsems.at[3])
    late_small = small_stages(lsbuf, core_ls, cell_ls, up_ls, head_ls, lsmall_ref, rsems.at[4])
    wide_grads(buf_2, og_ref, hid_ref)
    two[0]()
    lax.fori_loop(0, span(4) // 4, narrow_back, 0)
    two[1]()
    lax.fori_loop(span(4) // 4, clips // 4, narrow_back, 0)
    wide_grads(buf_1, n2_ref, dj_ref)
    one[0]()
    lax.fori_loop(0, span(4) // 4, widen_back, 0)
    one[1]()
    two[2]()
    lax.fori_loop(span(4) // 4, clips // 4, widen_back, 0)
    branch_grads()
    two[3]()
    esbuf[0:1, :] = jnp.sum(gb_ref[...], axis=0, keepdims=True)
    for r in range(4):
        line = jnp.sum(rows_ref[2 + r], axis=0, keepdims=True)
        for g in range(GROUPS):
            esbuf[1 + r : 2 + r, g * D : g * D + D] = line
    early_small[0]()
    lax.fori_loop(0, span(2), attend_back, 0)
    one[2]()
    early_small[1]()
    lax.fori_loop(span(2), span(5), attend_back, 0)
    two[4]()
    one[3]()
    early_small[2]()
    lax.fori_loop(span(5), span(8), attend_back, 0)
    qkv_grads()
    late[0]()
    one[4]()
    early_small[3]()
    fold_table(tacc_ref, lsbuf)
    late[1]()
    lax.fori_loop(0, clips // 2, entry_back, 0)
    for r in range(2):
        line = jnp.sum(rows_ref[r], axis=0, keepdims=True)
        for g in range(GROUPS):
            lsbuf[4 + r : 5 + r, g * D : g * D + D] = line
    late_small[0]()
    late[2]()
    lax.fori_loop(0, span(4) // 4, narrow, 0)
    late_small[1]()
    lax.fori_loop(span(4) // 4, clips // 4, narrow, 0)
    late[3]()
    late_small[2]()
    square = jnp.zeros((8, D), F32)
    for ref in (one_ref, two_ref):
        value = ref[...].astype(F32)
        square = square + fold(value * value)
    late_small[3]()
    late[4]()
    value = late_ref[...].astype(F32)
    square = square + fold(value * value)
    es, ls = esmall_ref[...], lsmall_ref[...]
    row = iota((8, D), 0)
    square = square + jnp.where(row < 1, es * es, 0.0) + jnp.where(row < 4, ls * ls, 0.0)
    common = jnp.where((row >= 1) & (row < 5), es * es, 0.0)
    common = common + jnp.where((row >= 4) & (row < 6), ls * ls, 0.0)
    nslots[head] = jnp.broadcast_to(jnp.sum(square, keepdims=True), (8, LANES))
    sends = [
        remote(
            nslots.at[head], nslots.at[head], nsems.at[0, d], nsems.at[1, d], win, (head + d + 1) % 4
        )
        for d in range(3)
    ]
    for copy in sends:
        copy.start()
    for copy in sends:
        copy.wait()
    total = (nslots[0] + nslots[1]) + (nslots[2] + nslots[3])
    for i in range(24):
        if i % 3 or i >= 12:
            keeps[i].wait()
    norm_ref[...] = jnp.sqrt(total + jnp.sum(common, keepdims=True))


def fold_table(tacc_ref, lsbuf):
    row = iota((256, 256), 0)
    lane = iota((256, 256), 1)
    spot = row % SPOT
    base = 112 - (spot // WIN * (2 * WIN - 1) + spot % WIN)
    for h in range(PER):
        own = jnp.where((lane == base) & (row // SPOT == h), 1.0, 0.0).astype(F32).astype(BF16)
        for g in range(GROUPS):
            spread = None
            for part in split_three(tacc_ref[g]):
                term = nn(part, own)
                spread = term if spread is None else spread + term
            total = None
            for a in range(WIN):
                piece = pltpu.roll(
                    spread[a * 8 : a * 8 + 8], 15 * a, axis=1, stride=1, stride_axis=0
                )
                total = piece if total is None else total + piece
            line = jnp.sum(total, axis=0, keepdims=True)
            for half in range(2):
                at = h * 256 + half * LANES
                lsbuf[1 + at // D : 2 + at // D, g * D + at % D : g * D + at % D + LANES] = line[
                    :, half * LANES : half * LANES + LANES
                ]


def block(frames, tok, og, held, qvb, table, fc1b, rowp):
    rows = tok.shape[0]
    clips = rows // CLIP
    upper = max(lax.axis_size("win") // 8, 1).bit_length() - 1
    shape = jax.ShapeDtypeStruct
    sems = pltpu.SemaphoreType.DMA
    vmem = pltpu.VMEM
    spec = pl.BlockSpec
    inside = lambda: spec(memory_space=vmem)
    outside = lambda: spec(memory_space=pl.ANY)
    half, part = D // 2, D // 8
    praw = held[3]
    return pl.pallas_call(
        partial(block_kernel, clips),
        in_specs=[spec(memory_space=pltpu.SMEM)] + [outside()] * 26 + [inside()] * 4,
        out_specs=[inside()] * 32,
        out_shape=[
            vmem((rows, D), F32),
            vmem((rows, D), F32),
            vmem((D, D), BF16),
            vmem((D, D), BF16),
            vmem((D, D), BF16),
            vmem((8, D), F32),
            vmem((8, D), F32),
            vmem((8, LANES), F32),
        ]
        + [vmem(a.shape, F32) for a in held],
        scratch_shapes=[
            vmem((8, D), F32),
            vmem((rows, D), BF16),
            vmem((rows, D), BF16),
            vmem((D + 16, rows), BF16),
            vmem((rows, D), BF16),
            vmem((rows, 1536), BF16),
            vmem((rows, 1536), BF16),
            vmem((rows, FF), BF16),
            vmem((clips, 4, GROUPS, SPOT, PER * SPOT), BF16),
            vmem((rows, 512), BF16),
            vmem((1536, D), BF16),
            vmem((512, D), BF16),
            vmem((D, FF), BF16),
            vmem((FF, D), BF16),
            vmem((GROUPS, 8, D), F32),
            vmem((8, 1536), F32),
            vmem((8, FF), F32),
            vmem((GROUPS, SPOT, PER * SPOT), F32),
            vmem((4, SPOT, PER * SPOT), jnp.int32),
            vmem((6, 8, D), F32),
            vmem((8, FF), F32),
            vmem((GROUPS, SPOT, PER * SPOT), F32),
            vmem((D, 1536), BF16),
            vmem((D, 1536), BF16),
            vmem((praw.shape[0], 1536), BF16),
            vmem((8, 1536), F32),
            vmem((8, 1536), F32),
            vmem((half, 1536), BF16),
            vmem((half, 1536), BF16),
            vmem((8, 1536), F32),
            vmem((8, 1536), F32),
            vmem((3, part, 1536), BF16),
            vmem((3, part, 1536), BF16),
            vmem((4, 8, 1536), F32),
            vmem((4, 8, 1536), F32),
            vmem((upper + 1, part, 1536), BF16),
            vmem((upper + 1, part, 1536), BF16),
            vmem((upper + 1, 8, 1536), F32),
            vmem((upper + 1, 8, 1536), F32),
            vmem((3, part, D), BF16),
            vmem((3, part, D), BF16),
            vmem((3, part, D), BF16),
            vmem((4, 8, D), F32),
            vmem((4, 8, D), F32),
            vmem((4, 8, LANES), F32),
            sems((4, 11, 3)),
            sems((3, 3)),
            sems((5, 2, 14 + upper)),
            sems((2, 3)),
            sems((1, 26)),
        ],
        compiler_params=pltpu.CompilerParams(
            vmem_limit_bytes=VMEM_LIMIT, collective_id=0, has_side_effects=True
        ),
    )(frames, tok, og, *held, qvb, table, fc1b, rowp)


def adam_step(weight, gradient, moment, second, factor, rate):
    clipped = gradient * factor
    moment_new = BETA_ONE * moment + (1.0 - BETA_ONE) * clipped
    second_new = BETA_TWO * second + (1.0 - BETA_TWO) * clipped * clipped
    moment_hat = moment_new * (1.0 / (1.0 - BETA_ONE**STEP))
    second_hat = second_new * (1.0 / (1.0 - BETA_TWO**STEP))
    master = weight - rate * (
        moment_hat / (jnp.sqrt(second_hat) + ADAM_EPS) + WEIGHT_DECAY * weight
    )
    return (gradient, moment_new, second_new, master)


def step_kernel(cuts, *refs):
    norm_ref, g1_ref, g2_ref, late_ref, es_ref, ls_ref, one_ref, two_ref = refs[:8]
    large, little = refs[8:20], refs[20:32]
    gn_ref, one_out, two_out, outs, sems = refs[32], refs[33], refs[34], refs[35:67], refs[67]
    step = pl.program_id(0)
    pushes = [
        pltpu.make_async_copy(one_ref, one_out, sems.at[0]),
        pltpu.make_async_copy(two_ref, two_out, sems.at[1]),
    ]

    @pl.when(step == 0)
    def _():
        for push in pushes:
            push.start()

    norm = norm_ref[0:1, 0:1]
    factor = jnp.minimum(1.0, CLIP_LIMIT / (norm + 1e-06))

    def put(i, gradient, rate, given):
        given = [value.reshape(gradient.shape) for value in given]
        values = adam_step(given[0], gradient, given[1], given[2], factor, rate)
        for k in range(4):
            out = outs[4 * i + k]
            out[...] = values[k].reshape(out.shape)

    def some(k, count):
        rows = pl.ds(pl.multiple_of(step * count, count), count)
        return [large[3 * k + n][rows, :] for n in range(3)]

    width = large[0].shape[1]
    rows, tall = D // cuts, width // cuts
    late = late_ref[pl.ds(pl.multiple_of(step * width, width), width), :].astype(F32)
    put(0, late, LEARN_RATE, [large[n][step] for n in range(3)])
    late = late_ref[pl.ds(pl.multiple_of(cuts * width + step * tall, tall), tall), :].astype(F32)
    put(3, late, LEARN_RATE, some(1, tall))
    own = pl.ds(pl.multiple_of(step * rows, rows), rows)
    put(4, g1_ref[own, :].astype(F32), LEARN_RATE, some(2, rows))
    put(6, g2_ref[:, own].astype(F32).T, LEARN_RATE, some(3, rows))

    @pl.when(step == 0)
    def _():
        gn_ref[...] = norm
        whole = lambda k: [little[3 * k + n][...] for n in range(3)]
        both = jnp.concatenate([ls_ref[0:1, :width], ls_ref[0:1, 2 * LANES : 2 * LANES + width]])
        put(1, both, LEARN_RATE, whole(0))
        lines = []
        for h in range(PER):
            pieces = []
            for half in range(2):
                at = h * 256 + half * LANES
                pieces.append(ls_ref[1 + at // D : 2 + at // D, at % D : at % D + LANES])
            lines.append(jnp.concatenate(pieces, axis=1))
        lines = jnp.concatenate(lines + [jnp.zeros((8 - PER, 256), F32)])
        offsets = little[3].shape[1]
        flip = iota((256, 256), 0) + iota((256, 256), 1) == offsets - 1
        flip = jnp.where(flip, 1.0, 0.0).astype(F32).astype(BF16)
        table = None
        for part in split_three(lines):
            term = nn(part, flip)
            table = term if table is None else table + term
        put(2, table[:PER, :offsets], ROW_RATE, whole(1))
        put(5, es_ref[0:1, :], LEARN_RATE, whole(2))
        put(7, jnp.concatenate([ls_ref[4:6, :], es_ref[1:5, :]]), ROW_RATE, whole(3))

    @pl.when(step == cuts - 1)
    def _():
        for push in pushes:
            push.wait()


def take_step(held, results):
    little = held[12:]
    cuts = 3
    spec = pl.BlockSpec
    near = spec(memory_space=pltpu.VMEM)
    full = lambda a: spec(a.shape, lambda i: (0,) * a.ndim)
    third = lambda a: spec(
        (a.shape[0] // cuts,) + a.shape[1:], lambda i: (i,) + (0,) * (a.ndim - 1)
    )
    order = [(third, held[0]), (full, little[0]), (full, little[3]), (third, held[3])]
    order += [(third, held[6]), (full, little[6]), (third, held[9]), (full, little[9])]
    one, two = results[6:]
    shape = jax.ShapeDtypeStruct
    close = [pltpu.with_memory_space_constraint(v, pltpu.VMEM) for v in (*results, *held)]
    outs = pl.pallas_call(
        partial(step_kernel, cuts),
        grid=(cuts,),
        in_specs=[near] * 32,
        out_specs=[spec((1, 1), lambda i: (0, 0))]
        + [spec(memory_space=pl.ANY)] * 2
        + [kind(a) for kind, a in order for _ in range(4)],
        out_shape=[shape((1, 1), F32), shape(one.shape, F32), shape(two.shape, F32)]
        + [shape(a.shape, F32) for _, a in order for _ in range(4)],
        scratch_shapes=[pltpu.SemaphoreType.DMA((2,))],
        compiler_params=pltpu.CompilerParams(vmem_limit_bytes=TAIL_LIMIT),
    )(*close)
    return outs[0], outs[1], outs[2], outs[3:]


def shards(
    tokens,
    out_grad,
    clip_frames,
    qkv_weight,
    qv_bias,
    rel_table,
    proj_weight,
    fc1_weight,
    fc1_bias,
    fc2_weight,
    row_params,
    qkv_first,
    qkv_second,
    qvb_first,
    qvb_second,
    table_first,
    table_second,
    proj_first,
    proj_second,
    fc1_first,
    fc1_second,
    fc1b_first,
    fc1b_second,
    fc2_first,
    fc2_second,
    rows_first,
    rows_second,
):
    parts = lambda v: v.transpose(1, 2, 0)
    large = [parts(qkv_weight), parts(qkv_first), parts(qkv_second)]
    large += [proj_weight, proj_first, proj_second, fc1_weight, fc1_first, fc1_second]
    large += [fc2_weight, fc2_first, fc2_second]
    little = [qv_bias, qvb_first, qvb_second, rel_table.T, table_first.T, table_second.T]
    little += [fc1_bias, fc1b_first, fc1b_second, row_params, rows_first, rows_second]
    output, input_grad, g1, g2, late, esmall, lsmall, norm, *kept = block(
        clip_frames, tokens, out_grad, large + little, qv_bias, little[3], fc1_bias, row_params
    )
    results = (norm, g1, g2, late, esmall, lsmall, output, input_grad)
    grad_norm, output, input_grad, updated = take_step(kept, results)
    updated = [
        v.transpose(2, 0, 1) if k < 4 else v.T if 8 <= k < 12 else v for k, v in enumerate(updated)
    ]
    return (output, input_grad, grad_norm.reshape(()), *updated)


def solution(mesh):
    rows = P(("win", "head"), None)
    last3, last2, first2, first1 = P(None, None, "head"), P(None, "head"), P("head", None), P("head")
    each = (last3, last2, last2, first2, last2, first1, first2, P())
    return jax.shard_map(
        shards,
        mesh=mesh,
        in_specs=(rows, rows, P("win")) + each + tuple(s for s in each for _ in range(2)),
        out_specs=(rows, rows, P()) + tuple(s for s in each for _ in range(4)),
        check_vma=False,
    )
```
